256 devices in a mesh: sec: 64 (over z, x_hi, y), row: 4 (over x_lo, core).
Axes of the slice: x: 4 (x_hi: 2, x_lo: 2; x = x_hi * 2 + x_lo), y: 4, z: 8, core: 2. Of those that a mesh axis runs over, the one named last changes fastest.
Arguments:
- image: bfloat16 [256, 512, 640], P('sec', 'row'), may hold values from -8 to 8, as said below
- grid_shift: int32 [256, 4, 5, 2], P('sec', 'row'), may hold values from -32 to 32
- partner_step: int32 [256, 2], P('sec'), may hold values from 1 to 2
- tissue: int32 [256, 4, 5], P('sec', 'row'), may hold values 0 or 1
Outputs:
- correlation: float32 [256, 2, 4, 5, 16384], P('sec', None, 'row')
The draws below stay inside these ranges and needn't reach their ends.
Inputs may be any that keep to these rules, and one draw needn't show every extreme that they name: `image`: each section is a drifting, possibly rescaled copy of one common pattern plus independent speckle.
All inputs are finite; a program needn't handle non-finite values. No bound on the sum of `tissue` on one device may be relied on, other than what follows from the above.
Results may differ from the reference program's by a relative error of at most 0.012.
Values may be sent and summed in bfloat16 or wider, within the bound.
A program may use at most 128 MiB of HBM per device.

```python
import math
import jax
import jax.numpy as jnp
from jax import lax

PC = 5
PATCH = 256
REACH = 32
SHIFTS = 128
SECTIONS = 256
PROWS = 4
ROWS = 512
COLS = 640


def draw_image(key, part):
    key = jax.random.fold_in(key, 11)
    pattern_key, speckle_key = jax.random.split(key, 2)
    pattern = jax.random.normal(pattern_key, (ROWS, COLS), jnp.float32)
    speckle = 0.5 * jax.random.normal(speckle_key, (SECTIONS, ROWS, COLS), jnp.float32)
    section_ids = jnp.arange(SECTIONS, dtype=jnp.int32)[:, None, None]
    row_ids = jnp.arange(ROWS, dtype=jnp.int32)[None, :, None]
    col_ids = jnp.arange(COLS, dtype=jnp.int32)[None, None, :]
    moved = pattern[(row_ids + 3 * section_ids) % ROWS, (col_ids + 5 * section_ids) % COLS]
    return jnp.clip(moved + speckle, -8.0, 8.0).astype(jnp.bfloat16)


def with_ends(drawn, stream_key, smallest, top_value):
    longest = drawn.shape.index(max(drawn.shape))
    spots = []
    for shift in (0, 1):
        where = [jax.random.randint(jax.random.fold_in(stream_key, axis), (), 0, length) for axis, length in enumerate(drawn.shape)]
        where[longest] = (where[longest] + shift) % drawn.shape[longest]
        spots.append(tuple(where))
    return drawn.at[spots[0]].set(smallest).at[spots[1]].set(top_value)


def setup_inputs(seed: int = 0) -> dict:
    key_list = jax.random.split(jax.random.key(seed), 5)
    image = draw_image(jax.random.fold_in(key_list[4], 71), 0)
    grid_shift = with_ends(jax.random.randint(key_list[1], (SECTIONS, PROWS, PC, 2), 0 - REACH, REACH + 1), jax.random.fold_in(key_list[1], 1), 0 - REACH, REACH).astype(jnp.int32)
    partner_step = with_ends(jax.random.randint(key_list[2], (SECTIONS, 2), 1, 3), jax.random.fold_in(key_list[2], 1), 1, 2).astype(jnp.int32)
    tissue = with_ends((jax.random.randint(key_list[3], (SECTIONS, PROWS, PC), 0, 4) < 3).astype(jnp.int32), jax.random.fold_in(key_list[3], 1), 0, 1)
    return {"image": image, "grid_shift": grid_shift, "partner_step": partner_step, "tissue": tissue}


def forward_tables():
    indices = jnp.arange(PATCH, dtype=jnp.int32)
    product = indices[:, None] * indices[None, :] % PATCH
    phases = product.astype(jnp.float32) * (2.0 * math.pi / PATCH)
    return (jnp.cos(phases).astype(jnp.bfloat16), jnp.sin(phases).astype(jnp.bfloat16))

def inverse_tables():
    indices = jnp.arange(PATCH, dtype=jnp.int32)
    displace = jnp.arange(SHIFTS, dtype=jnp.int32) - SHIFTS // 2
    product = displace[:, None] * indices[None, :] % PATCH
    phases = product.astype(jnp.float32) * (2.0 * math.pi / PATCH)
    return (jnp.cos(phases).astype(jnp.bfloat16), jnp.sin(phases).astype(jnp.bfloat16))

def normalize(patches):
    values = patches.astype(jnp.float32)
    centre = lax.optimization_barrier(jnp.mean(values, axis=(1, 2), keepdims=True))
    deviate = values - centre
    spread = lax.optimization_barrier(jnp.mean(deviate * deviate, axis=(1, 2), keepdims=True))
    return (deviate * lax.rsqrt(spread + 1e-05)).astype(jnp.bfloat16)

def transform(patches, cosine, sine):
    highest = lax.Precision.HIGHEST
    values = patches.astype(jnp.float32)
    cos_wide = cosine.astype(jnp.float32)
    sin_wide = sine.astype(jnp.float32)
    right_re = jnp.einsum('bij,jk->bik', values, cos_wide, precision=highest).astype(jnp.bfloat16)
    right_im = (-jnp.einsum('bij,jk->bik', values, sin_wide, precision=highest)).astype(jnp.bfloat16)
    right_re, right_im = lax.optimization_barrier((right_re, right_im))
    wide_re = right_re.astype(jnp.float32)
    wide_im = right_im.astype(jnp.float32)
    spec_re = jnp.einsum('ij,bjk->bik', cos_wide, wide_re, precision=highest) + jnp.einsum('ij,bjk->bik', sin_wide, wide_im, precision=highest)
    spec_im = jnp.einsum('ij,bjk->bik', cos_wide, wide_im, precision=highest) - jnp.einsum('ij,bjk->bik', sin_wide, wide_re, precision=highest)
    return (spec_re.astype(jnp.bfloat16), spec_im.astype(jnp.bfloat16))

def correlate(own_re, own_im, part_re, part_im, back_re, back_im):
    highest = lax.Precision.HIGHEST
    real_a = own_re.astype(jnp.float32)
    imag_a = own_im.astype(jnp.float32)
    real_b = part_re.astype(jnp.float32)
    imag_b = part_im.astype(jnp.float32)
    cross_re = (real_a * real_b + imag_a * imag_b).astype(jnp.bfloat16)
    cross_im = (real_a * imag_b - imag_a * real_b).astype(jnp.bfloat16)
    cross_re, cross_im = lax.optimization_barrier((cross_re, cross_im))
    wide_cre = cross_re.astype(jnp.float32)
    wide_cim = cross_im.astype(jnp.float32)
    table_re = back_re.astype(jnp.float32)
    table_im = back_im.astype(jnp.float32)
    half_re = jnp.einsum('uk,bkl->bul', table_re, wide_cre, precision=highest) - jnp.einsum('uk,bkl->bul', table_im, wide_cim, precision=highest)
    half_im = jnp.einsum('uk,bkl->bul', table_re, wide_cim, precision=highest) + jnp.einsum('uk,bkl->bul', table_im, wide_cre, precision=highest)
    half_re = half_re.astype(jnp.bfloat16)
    half_im = half_im.astype(jnp.bfloat16)
    half_re, half_im = lax.optimization_barrier((half_re, half_im))
    maps = jnp.einsum('bul,vl->buv', half_re.astype(jnp.float32), table_re, precision=highest) - jnp.einsum('bul,vl->buv', half_im.astype(jnp.float32), table_im, precision=highest)
    maps = maps / float(PATCH * PATCH)
    return maps.reshape(maps.shape[0], SHIFTS * SHIFTS)

def cut_plain(plane):
    margin = PATCH // 4 + REACH
    half = PATCH // 2
    wide = jnp.pad(plane, ((0, 0), (margin, margin)))
    strip = wide[:, REACH:REACH + half * (PC + 1)].reshape(PATCH, PC + 1, half)
    joined = jnp.concatenate([strip[:, :-1], strip[:, 1:]], axis=2)
    return jnp.transpose(joined, (1, 0, 2))

def reference(image, grid_shift, partner_step, tissue):
    margin = PATCH // 4 + REACH
    half = PATCH // 2
    cosine, sine = forward_tables()
    back_re, back_im = inverse_tables()
    padded = jnp.pad(image, ((0, 2), (margin, margin), (0, 0)))

    def plain_one(plane):
        pieces = [cut_plain(plane[half * prow + REACH:half * prow + REACH + PATCH]) for prow in range(PROWS)]
        return transform(normalize(jnp.concatenate(pieces, 0)), cosine, sine)
    plain_re, plain_im = lax.map(plain_one, padded)
    padcols = jnp.pad(padded, ((0, 0), (0, 0), (margin, margin)))
    prow_ids = jnp.repeat(jnp.arange(PROWS, dtype=jnp.int32), PC)
    pcol_ids = jnp.tile(jnp.arange(PC, dtype=jnp.int32), PROWS)

    def section_maps(section):
        plane = lax.dynamic_index_in_dim(padcols, section, 0, keepdims=False)
        shifts = lax.dynamic_index_in_dim(grid_shift, section, 0, keepdims=False).reshape(PROWS * PC, 2)
        starts_row = half * prow_ids + REACH + shifts[:, 0]
        starts_col = half * pcol_ids + REACH + shifts[:, 1]

        def cut_one(first_row, first_col):
            return lax.dynamic_slice(plane, (first_row.astype(jnp.int32), first_col.astype(jnp.int32)), (PATCH, PATCH))
        own_re, own_im = transform(normalize(jax.vmap(cut_one)(starts_row, starts_col)), cosine, sine)
        steps = lax.dynamic_index_in_dim(partner_step, section, 0, keepdims=False)
        near_re = lax.dynamic_index_in_dim(plain_re, section + 1, 0, keepdims=False)
        near_im = lax.dynamic_index_in_dim(plain_im, section + 1, 0, keepdims=False)
        far_re = lax.dynamic_index_in_dim(plain_re, section + 2, 0, keepdims=False)
        far_im = lax.dynamic_index_in_dim(plain_im, section + 2, 0, keepdims=False)
        weight = lax.dynamic_index_in_dim(tissue, section, 0, keepdims=False).astype(jnp.float32)
        slots = []
        for slot in range(2):
            chosen = steps[slot] == 1
            part_re = jnp.where(chosen, near_re, far_re)
            part_im = jnp.where(chosen, near_im, far_im)
            maps = correlate(own_re, own_im, part_re, part_im, back_re, back_im).reshape(PROWS, PC, SHIFTS * SHIFTS)
            slots.append(maps * weight[:, :, None])
        return jnp.stack(slots, 0)
    return lax.map(section_maps, jnp.arange(SECTIONS, dtype=jnp.int32))
```

```python
import functools

import jax
import jax.numpy as jnp
import ml_dtypes
import numpy as np
from jax import lax
from jax.experimental import pallas as pl
from jax.experimental.pallas import tpu as pltpu
from jax.sharding import PartitionSpec as P

PC = 5
PATCH = 256
HALF = 128
REACH = 32
HALO = 96
SHIFTS = 128
WIDE = 4 * HALF


def angle(product):
    return 2.0 * np.pi * (product % PATCH) / PATCH


def row_table():
    k = np.arange(HALF)[:, None]
    r = np.arange(PATCH)[None, :]
    sine = np.sin(angle(k * r))
    sine[0] = 1.0 - 2.0 * (np.arange(PATCH) % 2)
    return np.concatenate([np.cos(angle(k * r)), sine], 0).astype(ml_dtypes.bfloat16)


def col_tables():
    c = np.arange(HALF)[:, None]
    out = []
    for odd in (0, 1):
        ell = 2 * np.arange(HALF)[None, :] + odd
        cos, sin = np.cos(angle(ell * c)), np.sin(angle(ell * c))
        out.append(np.block([[cos, -sin], [-sin, -cos]]))
    return np.stack(out).astype(ml_dtypes.bfloat16)


def back_col_tables():
    v = np.arange(SHIFTS)[None, :] - SHIFTS // 2
    out = []
    for odd in (0, 1):
        ell = 2 * np.arange(HALF)[:, None] + odd
        cos, sin = np.cos(angle(ell * v)), np.sin(angle(ell * v))
        out.append(np.block([[cos, sin], [-sin, cos]]))
    return np.stack(out).astype(ml_dtypes.bfloat16)


def back_row_tables():
    rows = SHIFTS + 2 * REACH
    u = np.arange(rows + 16)[:, None] - (SHIFTS // 2 + REACH)
    k = np.arange(HALF)[None, :]
    weight = np.where(k == 0, 1.0, 2.0)
    sine = -weight * np.sin(angle(u * k))
    sine[:, 0] = 1.0 - 2.0 * (u[:, 0] % 2)
    full = np.concatenate([weight * np.cos(angle(u * k)), sine], 1)
    return np.stack([full[q : q + rows] for q in range(16)]).astype(ml_dtypes.bfloat16)


def phase_table():
    s = np.arange(2 * REACH + 1)[:, None] - REACH
    even = 2 * np.arange(HALF)[None, :]
    parts = [f(angle(ell * s)) for f in (np.cos, np.sin) for ell in (even, even + 1)]
    return np.concatenate(parts, 1).astype(np.float32)[:, None, :]


def dot(a, b):
    return jnp.dot(a, b, preferred_element_type=jnp.float32)


def folded(own, above, below, tile, start):
    lanes = slice(tile * HALF, (tile + 1) * HALF)
    low = above[0:64, lanes]
    high = below[32:96, lanes]
    rows = lax.broadcasted_iota(jnp.int32, (64, HALF), 0) + 32
    mixed = jnp.where(rows >= start, low.astype(jnp.float32), high.astype(jnp.float32)).astype(jnp.bfloat16)
    return jnp.concatenate([below[0:32, lanes], mixed, above[64:96, lanes], own[:, lanes]], 0)


def window(own, above, below, c, row_start, col_start):
    right = folded(own, above, below, c, row_start)
    zero = jnp.zeros((PATCH, HALF), jnp.bfloat16)
    far = folded(own, above, below, c - 1, row_start) if c > 0 else zero
    near = folded(own, above, below, c + 1, row_start) if c < PC - 1 else zero
    lanes = lax.broadcasted_iota(jnp.int32, (PATCH, HALF), 1)
    left = jnp.where(lanes >= col_start, far.astype(jnp.float32), near.astype(jnp.float32)).astype(jnp.bfloat16)
    return jnp.concatenate([left, right], 1)


def forward(own, above, below, starts, phases, tab_row, tab_col, nyq, spec, spec_nyq, rstd):
    first = lax.broadcasted_iota(jnp.int32, (8, HALF), 0) == 0

    def top(block):
        return block[0:8], block[8:]

    for c in range(PC):
        x = window(own, above, below, c, *starts[c])
        part = dot(tab_row[...], x)
        lo, hi = part[:, :HALF], part[:, HALF:]
        even, odd = lo + hi, lo - hi
        ce, se, co, so = even[:HALF], even[HALF:], odd[:HALF], odd[HALF:]
        head, tail = top(ce)
        centre = jnp.mean(head[0:1], axis=1, keepdims=True)
        head = jnp.where(first, head - centre, head)
        ce = jnp.concatenate([head, tail], 0)
        square = jnp.zeros((8, HALF), jnp.float32)
        edge = jnp.zeros((8, HALF), jnp.float32)
        for block in (ce, se, co, so):
            sq = block * block
            square = square + jnp.sum(sq.reshape(HALF // 8, 8, HALF), axis=0)
            edge = edge + sq[0:8]
        total = 2.0 * square - jnp.where(first, edge, 0.0)
        var = jnp.sum(jnp.sum(total, axis=0, keepdims=True), axis=1, keepdims=True) * (
            HALF / float(PATCH**4)
        )
        rstd[c] = jnp.broadcast_to(lax.rsqrt(var + 1e-05), (8, HALF))
        he, te = top(se)
        ho, to = top(so)
        nyq[c : c + 1, :HALF] = he[0:1]
        nyq[c : c + 1, HALF:] = ho[0:1]
        se = jnp.concatenate([jnp.where(first, 0.0, he), te], 0)
        so = jnp.concatenate([jnp.where(first, 0.0, ho), to], 0)
        fe = dot(jnp.concatenate([ce, se], 1).astype(jnp.bfloat16), tab_col[0])
        fo = dot(jnp.concatenate([co, so], 1).astype(jnp.bfloat16), tab_col[1])
        f = [fe[:, :HALF], fe[:, HALF:], fo[:, :HALF], fo[:, HALF:]]
        if phases is not None:
            f = turned(f, phases[c])
        spec[c] = jnp.concatenate(f, 1).astype(jnp.bfloat16)
    zero = jnp.zeros((16, HALF), jnp.bfloat16)
    ne = jnp.concatenate([nyq[:, :HALF].astype(jnp.bfloat16), zero], 1)
    no = jnp.concatenate([nyq[:, HALF:].astype(jnp.bfloat16), zero], 1)
    fe, fo = dot(ne, tab_col[0]), dot(no, tab_col[1])
    f = [fe[:, :HALF], fe[:, HALF:], fo[:, :HALF], fo[:, HALF:]]
    if phases is not None:
        rows = [jnp.concatenate([p[c] for c in range(PC)] + [jnp.zeros((16 - PC, HALF), jnp.float32)], 0) for p in zip(*[split4(q) for q in phases])]
        f = turned(f, rows)
    spec_nyq[...] = jnp.concatenate(f, 1).astype(jnp.bfloat16)


def split4(p):
    return [p[:, i * HALF : (i + 1) * HALF] for i in range(4)]


def turned(f, phase):
    ce, co, se, so = phase if isinstance(phase, list) else split4(phase)
    return [
        f[0] * ce - f[1] * se,
        f[0] * se + f[1] * ce,
        f[2] * co - f[3] * so,
        f[2] * so + f[3] * co,
    ]


def crossed(a, b):
    out = []
    for base in (0, 2 * HALF):
        re, im = slice(base, base + HALF), slice(base + HALF, base + 2 * HALF)
        are, aim = a[:, re].astype(jnp.float32), a[:, im].astype(jnp.float32)
        bre, bim = b[:, re].astype(jnp.float32), b[:, im].astype(jnp.float32)
        g = jnp.concatenate([are * bre + aim * bim, are * bim - aim * bre], 1)
        out.append(g.astype(jnp.bfloat16))
    return out


def kernel(
    shift_ref, step_ref, tissue_ref, img, above, below, nxt, nxt_above, nxt_below,
    tab_row, tab_col, tab_bcol, tab_brow, tab_phase, out,
    nyq, own_spec, own_nyq, own_rstd, spec, spec_nyq, rstd,
):
    secs = img.shape[0]
    nyq[...] = jnp.zeros_like(nyq)

    def plain(rows, up, down, slot):
        forward(rows, up, down, [(64, 64)] * PC, None, tab_row, tab_col, nyq, spec.at[slot], spec_nyq.at[slot], rstd.at[slot])

    def pairs(s):
        for c in range(PC):
            stage = []
            scales = []
            for slot in range(2):
                part = s + step_ref[s, slot] - 1
                ge, go = crossed(own_spec[c], spec[part, c])
                xe, xo = crossed(own_nyq[...], spec_nyq[part])
                ge = jnp.concatenate([ge, xe], 0)
                go = jnp.concatenate([go, xo], 0)
                g = dot(ge, tab_bcol[0]) + dot(go, tab_bcol[1])
                stage.append(g)
                scales.append(own_rstd[c] * rstd[part, c] * (tissue_ref[s, 0, c].astype(jnp.float32) / float(PATCH * PATCH)))
            first = lax.broadcasted_iota(jnp.int32, (8, HALF), 0) == 0
            cols = []
            for g in stage:
                edge = jnp.broadcast_to(g[HALF + c : HALF + c + 1, :HALF], (8, HALF))
                im = g[:HALF, HALF:]
                head = jnp.where(first, edge, im[0:8])
                cols.append(jnp.concatenate([g[:HALF, :HALF], head, im[8:]], 0))
            right = jnp.concatenate(cols, 1).astype(jnp.bfloat16)
            at = REACH - shift_ref[s, 0, c, 0]
            fine = lax.rem(at, 16)
            start = pl.multiple_of(at - fine, 16)
            left = tab_brow[fine, pl.ds(start, SHIFTS), :]
            maps = dot(left, right)
            for slot in range(2):
                piece = maps[:, slot * HALF : (slot + 1) * HALF].reshape(SHIFTS // 8, 8, HALF)
                out[s, slot, c] = (piece * scales[slot][None]).reshape(SHIFTS, SHIFTS)

    def own(s):
        starts = [(shift_ref[s, 0, c, 0] + 64, shift_ref[s, 0, c, 1] + 64) for c in range(PC)]
        phases = [tab_phase[shift_ref[s, 0, c, 1] + REACH] for c in range(PC)]
        forward(img.at[s], above.at[s], below.at[s], starts, phases, tab_row, tab_col, nyq, own_spec, own_nyq, own_rstd)

    for j in range(2):
        plain(nxt.at[j], nxt_above.at[j], nxt_below.at[j], secs - 1 + j)

    def local(i, carry):
        plain(img.at[i + 1], above.at[i + 1], below.at[i + 1], i)
        return carry

    lax.fori_loop(0, secs - 1, local, 0)

    def each(s, carry):
        own(s)
        pairs(s)
        return carry

    lax.fori_loop(0, secs, each, 0)


def from_row(block, by):
    count = lax.axis_size("row")
    return lax.ppermute(block, "row", [(i - by, i) for i in range(count) if 0 <= i - by < count])


def from_next(block, by):
    secs, rows = lax.axis_size("sec"), lax.axis_size("row")
    pairs = [
        ((s + 1) * rows + r - by, s * rows + r)
        for s in range(secs - 1)
        for r in range(rows)
        if 0 <= r - by < rows
    ]
    return lax.ppermute(block, ("sec", "row"), pairs)


def compute(image, above, below, nxt, nxt_above, nxt_below, grid_shift, partner_step, tissue):
    secs = image.shape[0]
    tables = [row_table(), col_tables(), back_col_tables(), back_row_tables(), phase_table()]
    smem = pl.BlockSpec(memory_space=pltpu.SMEM)
    vmem = pl.BlockSpec(memory_space=pltpu.VMEM)
    return pl.pallas_call(
        kernel,
        out_shape=jax.ShapeDtypeStruct((secs, 2, PC, SHIFTS, SHIFTS), jnp.float32),
        in_specs=[smem] * 3 + [vmem] * 11,
        out_specs=vmem,
        scratch_shapes=[
            pltpu.VMEM((16, PATCH), jnp.float32),
            pltpu.VMEM((PC, HALF, WIDE), jnp.bfloat16),
            pltpu.VMEM((16, WIDE), jnp.bfloat16),
            pltpu.VMEM((PC, 8, HALF), jnp.float32),
            pltpu.VMEM((secs + 1, PC, HALF, WIDE), jnp.bfloat16),
            pltpu.VMEM((secs + 1, 16, WIDE), jnp.bfloat16),
            pltpu.VMEM((secs + 1, PC, 8, HALF), jnp.float32),
        ],
        compiler_params=pltpu.CompilerParams(vmem_limit_bytes=56 * 1024 * 1024),
        cost_estimate=pl.CostEstimate(flops=6_000_000_000, bytes_accessed=8_000_000, transcendentals=0),
    )(
        grid_shift, partner_step, tissue, image, above, below, nxt, nxt_above, nxt_below,
        *[jnp.asarray(t) for t in tables],
    )


def on_device(image, grid_shift, partner_step, tissue):
    above = from_row(image[:, HALF - HALO :], 1)
    below = from_row(image[:, :HALO], -1)
    nxt = from_next(image[:2], 0)
    nxt_above = from_next(image[:2, HALF - HALO :], 1)
    nxt_below = from_next(image[:2, :HALO], -1)
    maps = compute(image, above, below, nxt, nxt_above, nxt_below, grid_shift, partner_step, tissue)
    return maps.reshape(image.shape[0], 2, 1, PC, SHIFTS * SHIFTS)


def solution(mesh):
    return jax.shard_map(
        on_device,
        mesh=mesh,
        in_specs=(
            P("sec", "row", None),
            P("sec", "row", None, None),
            P("sec", None),
            P("sec", "row", None),
        ),
        out_specs=P("sec", None, "row", None, None),
        check_vma=False,
    )
```

```python
import functools

import jax
import jax.numpy as jnp
import ml_dtypes
import numpy as np
from jax import lax
from jax.experimental import pallas as pl
from jax.experimental.pallas import tpu as pltpu
from jax.sharding import PartitionSpec as P

PC = 5
PATCH = 256
HALF = 128
REACH = 32
HALO = 96
SHIFTS = 128
WIDE = 4 * HALF


def angle(product):
    return 2.0 * np.pi * (product % PATCH) / PATCH


def row_table():
    k = np.arange(HALF)[:, None]
    r = np.arange(PATCH)[None, :]
    sine = np.sin(angle(k * r))
    sine[0] = 1.0 - 2.0 * (np.arange(PATCH) % 2)
    return np.concatenate([np.cos(angle(k * r)), sine], 0).astype(ml_dtypes.bfloat16)


def col_tables():
    c = np.arange(HALF)[:, None]
    out = []
    for odd in (0, 1):
        ell = 2 * np.arange(HALF)[None, :] + odd
        cos, sin = np.cos(angle(ell * c)), np.sin(angle(ell * c))
        out.append(np.block([[cos, -sin], [-sin, -cos]]))
    return np.stack(out).astype(ml_dtypes.bfloat16)


def back_col_tables():
    v = np.arange(SHIFTS)[None, :] - SHIFTS // 2
    out = []
    for odd in (0, 1):
        ell = 2 * np.arange(HALF)[:, None] + odd
        cos, sin = np.cos(angle(ell * v)), np.sin(angle(ell * v))
        out.append(np.block([[cos, sin], [-sin, cos]]))
    return np.stack(out).astype(ml_dtypes.bfloat16)


def back_row_table():
    u = np.arange(SHIFTS)[:, None] - SHIFTS // 2
    k = np.arange(HALF)[None, :]
    weight = np.where(k == 0, 1.0, 2.0)
    sine = -weight * np.sin(angle(u * k))
    sine[:, 0] = 1.0 - 2.0 * (u[:, 0] % 2)
    return np.concatenate([weight * np.cos(angle(u * k)), sine], 1).astype(np.float32)


def phase_table(frequencies):
    s = np.arange(2 * REACH + 1)[:, None] - REACH
    parts = np.concatenate([f(angle(ell[None, :] * s)) for f, ell in frequencies], 1)
    high = parts.astype(ml_dtypes.bfloat16)
    low = (parts - high.astype(np.float64)).astype(ml_dtypes.bfloat16)
    out = np.zeros((PATCH, parts.shape[1]), ml_dtypes.bfloat16)
    out[: len(s)], out[HALF : HALF + len(s)] = high, low
    return out


def col_phases():
    even = 2 * np.arange(HALF)
    return phase_table([(f, ell) for f in (np.cos, np.sin) for ell in (even, even + 1)])


def row_phases():
    k = np.arange(HALF)
    return phase_table([(np.cos, k), (np.cos, np.where(k == 0, HALF, k)), (np.sin, k)])


def dot(a, b):
    return jnp.dot(a, b, preferred_element_type=jnp.float32)


def folded(own, above, below, tile, start):
    lanes = slice(tile * HALF, (tile + 1) * HALF)
    if start is None:
        return jnp.concatenate([below[0:64, lanes], above[32:96, lanes], own[:, lanes]], 0)
    low = above[0:64, lanes]
    high = below[32:96, lanes]
    rows = lax.broadcasted_iota(jnp.int32, (64, HALF), 0) + 32
    mixed = jnp.where(rows >= start, low.astype(jnp.float32), high.astype(jnp.float32)).astype(jnp.bfloat16)
    return jnp.concatenate([below[0:32, lanes], mixed, above[64:96, lanes], own[:, lanes]], 0)


def window(own, above, below, c, row_start, col_start):
    right = folded(own, above, below, c, row_start)
    zero = jnp.zeros((PATCH, HALF), jnp.bfloat16)
    far = folded(own, above, below, c - 1, row_start) if c > 0 else zero
    near = folded(own, above, below, c + 1, row_start) if c < PC - 1 else zero
    lanes = lax.broadcasted_iota(jnp.int32, (PATCH, HALF), 1)
    left = jnp.where(lanes >= col_start, far.astype(jnp.float32), near.astype(jnp.float32)).astype(jnp.bfloat16)
    return jnp.concatenate([left, right], 1)


def forward(own, above, below, starts, phases, tab_row, tab_col, nyq, spec, spec_nyq, rstd):
    first = lax.broadcasted_iota(jnp.int32, (8, HALF), 0) == 0

    def top(block):
        return block[0:8], block[8:]

    for c in range(PC):
        x = window(own, above, below, c, *starts[c])
        part = dot(tab_row[...], x)
        lo, hi = part[:, :HALF], part[:, HALF:]
        even, odd = lo + hi, lo - hi
        ce, se, co, so = even[:HALF], even[HALF:], odd[:HALF], odd[HALF:]
        head, tail = top(ce)
        centre = jnp.mean(head[0:1], axis=1, keepdims=True)
        head = jnp.where(first, head - centre, head)
        ce = jnp.concatenate([head, tail], 0)
        square = jnp.zeros((8, HALF), jnp.float32)
        edge = jnp.zeros((8, HALF), jnp.float32)
        for block in (ce, se, co, so):
            sq = block * block
            square = square + jnp.sum(sq.reshape(HALF // 8, 8, HALF), axis=0)
            edge = edge + sq[0:8]
        total = 2.0 * square - jnp.where(first, edge, 0.0)
        var = jnp.sum(jnp.sum(total, axis=0, keepdims=True), axis=1, keepdims=True) * (
            HALF / float(PATCH**4)
        )
        rstd[c] = jnp.broadcast_to(lax.rsqrt(var + 1e-05), (8, HALF))
        he, te = top(se)
        ho, to = top(so)
        nyq[c : c + 1, :HALF] = he[0:1]
        nyq[c : c + 1, HALF:] = ho[0:1]
        se = jnp.concatenate([jnp.where(first, 0.0, he), te], 0)
        so = jnp.concatenate([jnp.where(first, 0.0, ho), to], 0)
        fe = dot(jnp.concatenate([ce, se], 1).astype(jnp.bfloat16), tab_col[0])
        fo = dot(jnp.concatenate([co, so], 1).astype(jnp.bfloat16), tab_col[1])
        f = [fe[:, :HALF], fe[:, HALF:], fo[:, :HALF], fo[:, HALF:]]
        if phases is not None:
            f = turned(f, phases[c])
        spec[c] = jnp.concatenate(f, 1).astype(jnp.bfloat16)
    zero = jnp.zeros((16, HALF), jnp.bfloat16)
    ne = jnp.concatenate([nyq[:, :HALF].astype(jnp.bfloat16), zero], 1)
    no = jnp.concatenate([nyq[:, HALF:].astype(jnp.bfloat16), zero], 1)
    fe, fo = dot(ne, tab_col[0]), dot(no, tab_col[1])
    f = [fe[:, :HALF], fe[:, HALF:], fo[:, :HALF], fo[:, HALF:]]
    if phases is not None:
        rows = [jnp.concatenate([p[c] for c in range(PC)] + [jnp.zeros((16 - PC, HALF), jnp.float32)], 0) for p in zip(*[split4(q) for q in phases])]
        f = turned(f, rows)
    spec_nyq[...] = jnp.concatenate(f, 1).astype(jnp.bfloat16)


def split4(p):
    return [p[:, i * HALF : (i + 1) * HALF] for i in range(4)]


def turned(f, phase):
    ce, co, se, so = phase if isinstance(phase, list) else split4(phase)
    return [
        f[0] * ce - f[1] * se,
        f[0] * se + f[1] * ce,
        f[2] * co - f[3] * so,
        f[2] * so + f[3] * co,
    ]


def crossed(a, b):
    out = []
    for base in (0, 2 * HALF):
        re, im = slice(base, base + HALF), slice(base + HALF, base + 2 * HALF)
        are, aim = a[:, re].astype(jnp.float32), a[:, im].astype(jnp.float32)
        bre, bim = b[:, re].astype(jnp.float32), b[:, im].astype(jnp.float32)
        g = jnp.concatenate([are * bre + aim * bim, are * bim - aim * bre], 1)
        out.append(g.astype(jnp.bfloat16))
    return out


def remote(src, dst, send, recv, where):
    return pltpu.make_async_remote_copy(
        src_ref=src, dst_ref=dst, send_sem=send, recv_sem=recv, device_id=where, device_id_type=pl.DeviceIdType.MESH
    )


def kernel(
    secs_axis, rows_axis,
    shift_ref, step_ref, tissue_ref, img, *refs,
):
    tables, refs = refs[:6], refs[6:]
    out, refs = refs[0], refs[1:]
    tabs, refs = refs[:6], refs[6:]
    (strip, above, below, pcol, prow, nyq, own_spec, own_nyq, own_rstd, spec, spec_nyq, rstd, stage,
     tab_sem, img_sem, out_sem, up_send, up_recv, down_send, down_recv, sec_send, sec_recv) = refs
    tab_row, tab_col, tab_bcol, tab_brow, tab_pcol, tab_prow = tabs
    secs = own_spec.shape[0]
    sec, row = lax.axis_index("sec"), lax.axis_index("row")
    has_up, has_down = row > 0, row < rows_axis - 1
    has_prev, has_next = sec > 0, sec < secs_axis - 1
    up, down, prev, following = (sec, row - 1), (sec, row + 1), (sec - 1, row), (sec + 1, row)
    sides = ((has_up, up), (has_down, down), (has_prev, prev), (has_next, following))

    barrier = pltpu.get_barrier_semaphore()
    for there, where in sides:
        @pl.when(there)
        def _():
            pl.semaphore_signal(barrier, inc=1, device_id=where, device_id_type=pl.DeviceIdType.MESH)

    img_copy = pltpu.make_async_copy(img, strip.at[0:secs], img_sem)
    img_copy.start()
    loads = [pltpu.make_async_copy(t, v, tab_sem.at[i]) for i, (t, v) in enumerate(zip(tables, tabs))]
    for load in loads:
        load.start()

    pl.semaphore_wait(barrier, sum(there.astype(jnp.int32) for there, _ in sides))

    def to_prev(j):
        return remote(img.at[j], strip.at[secs + j], sec_send.at[j], sec_recv.at[j], prev)

    def to_down(t):
        return remote(img.at[t, HALF - HALO : HALF], above.at[t], down_send.at[t], down_recv.at[t], down)

    def to_up(t):
        return remote(img.at[t, 0:HALO], below.at[t], up_send.at[t], up_recv.at[t], up)

    def relay_down(j):
        t = secs + j
        return remote(strip.at[t, HALF // 2 : HALF], above.at[t, HALO - HALF // 2 : HALO], down_send.at[t], down_recv.at[t], down)

    def relay_up(j):
        t = secs + j
        return remote(strip.at[t, 0 : HALF // 2], below.at[t, 0 : HALF // 2], up_send.at[t], up_recv.at[t], up)

    @pl.when(has_prev)
    def _():
        for j in range(2):
            to_prev(j).start()

    @pl.when(has_down)
    def _():
        for t in range(secs):
            to_down(t).start()

    @pl.when(has_up)
    def _():
        for t in range(secs):
            to_up(t).start()

    @pl.when(jnp.logical_not(has_up))
    def _():
        above[...] = jnp.zeros_like(above)

    @pl.when(jnp.logical_not(has_down))
    def _():
        below[...] = jnp.zeros_like(below)

    @pl.when(jnp.logical_not(has_next))
    def _():
        strip[secs:] = jnp.zeros((2, HALF, strip.shape[2]), jnp.bfloat16)
        above[secs:] = jnp.zeros((2, HALO, strip.shape[2]), jnp.bfloat16)
        below[secs:] = jnp.zeros((2, HALO, strip.shape[2]), jnp.bfloat16)

    nyq[...] = jnp.zeros_like(nyq)
    img_copy.wait()
    for load in loads:
        load.wait()

    rows = lax.broadcasted_iota(jnp.int32, (8 * secs, PATCH), 0)
    lanes = lax.broadcasted_iota(jnp.int32, (8 * secs, PATCH), 1)
    for axis, table, phase in ((0, tab_prow, prow), (1, tab_pcol, pcol)):
        wanted = jnp.zeros_like(lanes)
        for s in range(secs):
            for c in range(PC):
                wanted = jnp.where(rows == 8 * s + c, shift_ref[s, 0, axis, c] + REACH, wanted)
        chosen = jnp.logical_or(lanes == wanted, lanes == wanted + HALF)
        picked = dot(chosen.astype(jnp.float32).astype(jnp.bfloat16), table[...])
        phase[...] = picked.reshape(secs, 8, picked.shape[1])

    def plain(t):
        forward(
            strip.at[t], above.at[t], below.at[t], [(None, 64)] * PC, None, tab_row, tab_col, nyq,
            spec.at[t - 1], spec_nyq.at[t - 1], rstd.at[t - 1],
        )

    def own(s):
        starts = [(shift_ref[s, 0, 0, c] + 64, shift_ref[s, 0, 1, c] + 64) for c in range(PC)]
        phases = [pcol[s, c : c + 1] for c in range(PC)]
        forward(
            strip.at[s], above.at[s], below.at[s], starts, phases, tab_row, tab_col, nyq,
            own_spec.at[s], own_nyq.at[s], own_rstd.at[s],
        )

    first = lax.broadcasted_iota(jnp.int32, (8, HALF), 0) == 0

    def pairs(s):
        for c in range(PC):
            cols = []
            for part in (s, s + 1):
                ge, go = crossed(own_spec[s, c], spec[part, c])
                xe, xo = crossed(own_nyq[s], spec_nyq[part])
                ge = jnp.concatenate([ge, xe], 0)
                go = jnp.concatenate([go, xo], 0)
                g = dot(ge, tab_bcol[0]) + dot(go, tab_bcol[1])
                edge = jnp.broadcast_to(g[HALF + c : HALF + c + 1, :HALF], (8, HALF))
                im = g[:HALF, HALF:]
                head = jnp.where(first, edge, im[0:8])
                cols.append(jnp.concatenate([g[:HALF, :HALF], head, im[8:]], 0))
            right = jnp.concatenate(cols, 1).astype(jnp.bfloat16)
            turn = prow[s, c : c + 1]
            cos, cos_edge, sin = turn[:, :HALF], turn[:, HALF : 2 * HALF], turn[:, 2 * HALF :]
            bc, bs = tab_brow[:, :HALF], tab_brow[:, HALF:]
            left = jnp.concatenate([bc * cos - bs * sin, bs * cos_edge + bc * sin], 1).astype(jnp.bfloat16)
            maps = dot(left, right)
            weight = tissue_ref[s, 0, c].astype(jnp.float32) / float(PATCH * PATCH)
            base = own_rstd[s, c] * weight
            near = maps[:, :HALF].reshape(SHIFTS // 8, 8, HALF)
            far = maps[:, HALF:].reshape(SHIFTS // 8, 8, HALF)
            for slot in range(2):
                step = step_ref[slot, s].astype(jnp.float32)
                by_near = base * rstd[s, c] * (2.0 - step)
                by_far = base * rstd[s + 1, c] * (step - 1.0)
                stage[s, slot, c] = (near * by_near[None] + far * by_far[None]).reshape(SHIFTS, SHIFTS)

    def save(s):
        return pltpu.make_async_copy(stage.at[s], out.at[s], out_sem.at[s])

    def each(t, carry):
        for j in range(2):
            @pl.when(jnp.logical_and(has_next, t == 2 + j))
            def _():
                to_prev(j).wait_recv()

                @pl.when(has_down)
                def _():
                    relay_down(j).start()

                @pl.when(has_up)
                def _():
                    relay_up(j).start()

        @pl.when(t < secs)
        def _():
            @pl.when(has_up)
            def _():
                to_down(t).wait_recv()

            @pl.when(has_down)
            def _():
                to_up(t).wait_recv()

            own(t)

        for j in range(2):
            @pl.when(jnp.logical_and(has_next, t == secs + j))
            def _():
                @pl.when(has_up)
                def _():
                    relay_down(j).wait_recv()

                @pl.when(has_down)
                def _():
                    relay_up(j).wait_recv()

        @pl.when(t >= 1)
        def _():
            plain(t)

        @pl.when(t >= 2)
        def _():
            pairs(t - 2)
            save(t - 2).start()

        return carry

    lax.fori_loop(0, secs + 2, each, 0)

    @pl.when(has_prev)
    def _():
        for j in range(2):
            to_prev(j).wait_send()

    @pl.when(has_down)
    def _():
        for t in range(secs):
            to_down(t).wait_send()

    @pl.when(has_up)
    def _():
        for t in range(secs):
            to_up(t).wait_send()

    @pl.when(jnp.logical_and(has_next, has_down))
    def _():
        for j in range(2):
            relay_down(j).wait_send()

    @pl.when(jnp.logical_and(has_next, has_up))
    def _():
        for j in range(2):
            relay_up(j).wait_send()

    for s in range(secs):
        save(s).wait()


def on_device(secs_axis, rows_axis, image, grid_shift, partner_step, tissue):
    secs, height, width = image.shape
    tables = [jnp.asarray(t) for t in (row_table(), col_tables(), back_col_tables(), back_row_table(), col_phases(), row_phases())]
    smem = pl.BlockSpec(memory_space=pltpu.SMEM)
    hbm = pl.BlockSpec(memory_space=pl.ANY)
    dma = pltpu.SemaphoreType.DMA
    maps = pl.pallas_call(
        functools.partial(kernel, secs_axis, rows_axis),
        out_shape=jax.ShapeDtypeStruct((secs, 2, PC, SHIFTS, SHIFTS), jnp.float32),
        in_specs=[smem] * 3 + [hbm] * 7,
        out_specs=hbm,
        scratch_shapes=[pltpu.VMEM(t.shape, t.dtype) for t in tables]
        + [
            pltpu.VMEM((secs + 2, height, width), jnp.bfloat16),
            pltpu.VMEM((secs + 2, HALO, width), jnp.bfloat16),
            pltpu.VMEM((secs + 2, HALO, width), jnp.bfloat16),
            pltpu.VMEM((secs, 8, 4 * HALF), jnp.float32),
            pltpu.VMEM((secs, 8, 3 * HALF), jnp.float32),
            pltpu.VMEM((16, PATCH), jnp.float32),
            pltpu.VMEM((secs, PC, HALF, WIDE), jnp.bfloat16),
            pltpu.VMEM((secs, 16, WIDE), jnp.bfloat16),
            pltpu.VMEM((secs, PC, 8, HALF), jnp.float32),
            pltpu.VMEM((secs + 1, PC, HALF, WIDE), jnp.bfloat16),
            pltpu.VMEM((secs + 1, 16, WIDE), jnp.bfloat16),
            pltpu.VMEM((secs + 1, PC, 8, HALF), jnp.float32),
            pltpu.VMEM((secs, 2, PC, SHIFTS, SHIFTS), jnp.float32),
            dma((6,)),
            dma,
            dma((secs,)),
            dma((secs + 2,)),
            dma((secs + 2,)),
            dma((secs + 2,)),
            dma((secs + 2,)),
            dma((2,)),
            dma((2,)),
        ],
        compiler_params=pltpu.CompilerParams(
            vmem_limit_bytes=60 * 1024 * 1024, collective_id=0, has_side_effects=True
        ),
        cost_estimate=pl.CostEstimate(flops=6_000_000_000, bytes_accessed=8_000_000, transcendentals=0),
    )(jnp.swapaxes(grid_shift, 2, 3), jnp.swapaxes(partner_step, 0, 1), tissue, image, *tables)
    return maps.reshape(secs, 2, 1, PC, SHIFTS * SHIFTS)


def solution(mesh):
    return jax.shard_map(
        functools.partial(on_device, mesh.shape["sec"], mesh.shape["row"]),
        mesh=mesh,
        in_specs=(
            P("sec", "row", None),
            P("sec", "row", None, None),
            P("sec", None),
            P("sec", "row", None),
        ),
        out_specs=P("sec", None, "row", None, None),
        check_vma=False,
    )
```

```python
import functools

import jax
import jax.numpy as jnp
import ml_dtypes
import numpy as np
from jax import lax
from jax.experimental import pallas as pl
from jax.experimental.pallas import tpu as pltpu
from jax.sharding import PartitionSpec as P

PC = 5
PATCH = 256
HALF = 128
REACH = 32
GROUP = 4
HALO = 96
SHIFTS = 128
WIDE = 4 * HALF


def angle(product):
    return 2.0 * np.pi * (product % PATCH) / PATCH


def row_table():
    k = np.arange(HALF)[:, None]
    r = np.arange(PATCH)[None, :]
    sine = np.sin(angle(k * r))
    sine[0] = 1.0 - 2.0 * (np.arange(PATCH) % 2)
    return np.concatenate([np.cos(angle(k * r)), sine], 0).astype(ml_dtypes.bfloat16)


def col_tables():
    c = np.arange(HALF)[:, None]
    out = []
    for odd in (0, 1):
        ell = 2 * np.arange(HALF)[None, :] + odd
        cos, sin = np.cos(angle(ell * c)), np.sin(angle(ell * c))
        out.append(np.block([[cos, -sin], [-sin, -cos]]))
    return np.stack(out).astype(ml_dtypes.bfloat16)


def back_col_tables():
    v = np.arange(SHIFTS)[None, :] - SHIFTS // 2
    out = []
    for odd in (0, 1):
        ell = 2 * np.arange(HALF)[:, None] + odd
        cos, sin = np.cos(angle(ell * v)), np.sin(angle(ell * v))
        out.append(np.block([[cos, sin], [-sin, cos]]))
    return np.stack(out).astype(ml_dtypes.bfloat16)


def back_row_table():
    u = np.arange(SHIFTS)[:, None] - SHIFTS // 2
    k = np.arange(HALF)[None, :]
    weight = np.where(k == 0, 1.0, 2.0)
    sine = -weight * np.sin(angle(u * k))
    sine[:, 0] = 1.0 - 2.0 * (u[:, 0] % 2)
    return np.concatenate([weight * np.cos(angle(u * k)), sine], 1).astype(np.float32)


def phase_table(frequencies):
    s = np.arange(2 * REACH + 1)[:, None] - REACH
    parts = np.concatenate([f(angle(ell[None, :] * s)) for f, ell in frequencies], 1)
    high = parts.astype(ml_dtypes.bfloat16)
    low = (parts - high.astype(np.float64)).astype(ml_dtypes.bfloat16)
    out = np.zeros((PATCH, parts.shape[1]), ml_dtypes.bfloat16)
    out[: len(s)], out[HALF : HALF + len(s)] = high, low
    return out


def col_phases():
    even = 2 * np.arange(HALF)
    return phase_table([(f, ell) for f in (np.cos, np.sin) for ell in (even, even + 1)])


def row_phases():
    k = np.arange(HALF)
    return phase_table([(np.cos, k), (np.cos, np.where(k == 0, HALF, k)), (np.sin, k)])


def dot(a, b):
    return jnp.dot(a, b, preferred_element_type=jnp.float32)


def folded(own, above, below, tile, start):
    lanes = slice(tile * HALF, (tile + 1) * HALF)
    if start is None:
        return jnp.concatenate([below[0:64, lanes], above[32:96, lanes], own[:, lanes]], 0)
    low = above[0:64, lanes]
    high = below[32:96, lanes]
    rows = lax.broadcasted_iota(jnp.int32, (64, HALF), 0) + 32
    mixed = jnp.where(rows >= start, low.astype(jnp.float32), high.astype(jnp.float32)).astype(jnp.bfloat16)
    return jnp.concatenate([below[0:32, lanes], mixed, above[64:96, lanes], own[:, lanes]], 0)


def window(own, above, below, c, row_start, col_start):
    right = folded(own, above, below, c, row_start)
    zero = jnp.zeros((PATCH, HALF), jnp.bfloat16)
    far = folded(own, above, below, c - 1, row_start) if c > 0 else zero
    near = folded(own, above, below, c + 1, row_start) if c < PC - 1 else zero
    lanes = lax.broadcasted_iota(jnp.int32, (PATCH, HALF), 1)
    left = jnp.where(lanes >= col_start, far.astype(jnp.float32), near.astype(jnp.float32)).astype(jnp.bfloat16)
    return jnp.concatenate([left, right], 1)


def forward(own, above, below, starts, phases, tab_row, tab_col, nyq, spec, spec_nyq, rstd):
    first = lax.broadcasted_iota(jnp.int32, (8, HALF), 0) == 0

    def top(block):
        return block[0:8], block[8:]

    for c in range(PC):
        x = window(own, above, below, c, *starts[c])
        part = dot(tab_row[...], x)
        lo, hi = part[:, :HALF], part[:, HALF:]
        even, odd = lo + hi, lo - hi
        ce, se, co, so = even[:HALF], even[HALF:], odd[:HALF], odd[HALF:]
        head, tail = top(ce)
        centre = jnp.mean(head[0:1], axis=1, keepdims=True)
        head = jnp.where(first, head - centre, head)
        ce = jnp.concatenate([head, tail], 0)
        square = jnp.zeros((8, HALF), jnp.float32)
        edge = jnp.zeros((8, HALF), jnp.float32)
        for block in (ce, se, co, so):
            sq = block * block
            square = square + jnp.sum(sq.reshape(HALF // 8, 8, HALF), axis=0)
            edge = edge + sq[0:8]
        total = 2.0 * square - jnp.where(first, edge, 0.0)
        var = jnp.sum(jnp.sum(total, axis=0, keepdims=True), axis=1, keepdims=True) * (
            HALF / float(PATCH**4)
        )
        rstd[c] = jnp.broadcast_to(lax.rsqrt(var + 1e-05), (8, HALF))
        he, te = top(se)
        ho, to = top(so)
        nyq[c : c + 1, :HALF] = he[0:1]
        nyq[c : c + 1, HALF:] = ho[0:1]
        se = jnp.concatenate([jnp.where(first, 0.0, he), te], 0)
        so = jnp.concatenate([jnp.where(first, 0.0, ho), to], 0)
        fe = dot(jnp.concatenate([ce, se], 1).astype(jnp.bfloat16), tab_col[0])
        fo = dot(jnp.concatenate([co, so], 1).astype(jnp.bfloat16), tab_col[1])
        f = [fe[:, :HALF], fe[:, HALF:], fo[:, :HALF], fo[:, HALF:]]
        if phases is not None:
            f = turned(f, phases[c])
        spec[c] = jnp.concatenate(f, 1).astype(jnp.bfloat16)
    zero = jnp.zeros((16, HALF), jnp.bfloat16)
    ne = jnp.concatenate([nyq[:, :HALF].astype(jnp.bfloat16), zero], 1)
    no = jnp.concatenate([nyq[:, HALF:].astype(jnp.bfloat16), zero], 1)
    fe, fo = dot(ne, tab_col[0]), dot(no, tab_col[1])
    f = [fe[:, :HALF], fe[:, HALF:], fo[:, :HALF], fo[:, HALF:]]
    if phases is not None:
        rows = [jnp.concatenate([p[c] for c in range(PC)] + [jnp.zeros((16 - PC, HALF), jnp.float32)], 0) for p in zip(*[split4(q) for q in phases])]
        f = turned(f, rows)
    spec_nyq[...] = jnp.concatenate(f, 1).astype(jnp.bfloat16)


def split4(p):
    return [p[:, i * HALF : (i + 1) * HALF] for i in range(4)]


def turned(f, phase):
    ce, co, se, so = phase if isinstance(phase, list) else split4(phase)
    return [
        f[0] * ce - f[1] * se,
        f[0] * se + f[1] * ce,
        f[2] * co - f[3] * so,
        f[2] * so + f[3] * co,
    ]


def crossed(a, b):
    out = []
    for base in (0, 2 * HALF):
        re, im = slice(base, base + HALF), slice(base + HALF, base + 2 * HALF)
        are, aim = a[:, re].astype(jnp.float32), a[:, im].astype(jnp.float32)
        bre, bim = b[:, re].astype(jnp.float32), b[:, im].astype(jnp.float32)
        g = jnp.concatenate([are * bre + aim * bim, are * bim - aim * bre], 1)
        out.append(g.astype(jnp.bfloat16))
    return out


def remote(src, dst, send, recv, where):
    return pltpu.make_async_remote_copy(
        src_ref=src, dst_ref=dst, send_sem=send, recv_sem=recv, device_id=where, device_id_type=pl.DeviceIdType.MESH
    )


def kernel(
    secs_axis, rows_axis,
    shift_hbm, step_hbm, tissue_hbm, img, *refs,
):
    tables, refs = refs[:6], refs[6:]
    out, refs = refs[0], refs[1:]
    tabs, refs = refs[:6], refs[6:]
    (strip, above, below, pcol, prow, nyq, own_spec, own_nyq, own_rstd, spec, spec_nyq, rstd, stage,
     tab_sem, img_sem, out_sem, up_send, up_recv, down_send, down_recv, sec_send, sec_recv,
     transit, via_send, via_recv, shift_ref, step_ref, tissue_ref, int_sem) = refs
    tab_row, tab_col, tab_bcol, tab_brow, tab_pcol, tab_prow = tabs
    secs = own_spec.shape[0]
    sec, row = lax.axis_index("sec"), lax.axis_index("row")
    has_up, has_down = row > 0, row < rows_axis - 1
    has_prev, has_next = sec > 0, sec < secs_axis - 1
    up, down, prev, following = (sec, row - 1), (sec, row + 1), (sec - 1, row), (sec + 1, row)
    place = lax.rem(sec, GROUP)
    far_send = jnp.logical_and(place == 0, has_prev)
    carries = jnp.logical_and(place == GROUP - 1, sec >= GROUP)
    far_take = jnp.logical_and(place == GROUP - 1, has_next)
    via, origin, goal, carrier = [(sec + d, row) for d in (GROUP - 1, 1 - GROUP, -GROUP, GROUP)]
    sides = (
        (has_up, up), (has_down, down), (has_prev, prev), (has_next, following),
        (far_send, via), (carries, origin), (carries, goal), (far_take, carrier),
    )

    barrier = pltpu.get_barrier_semaphore()
    for there, where in sides:
        @pl.when(there)
        def _():
            pl.semaphore_signal(barrier, inc=1, device_id=where, device_id_type=pl.DeviceIdType.MESH)

    img_copy = pltpu.make_async_copy(img, strip.at[0:secs], img_sem)
    img_copy.start()
    loads = [pltpu.make_async_copy(t, v, tab_sem.at[i]) for i, (t, v) in enumerate(zip(tables, tabs))]
    ints = ((shift_hbm, shift_ref), (step_hbm, step_ref), (tissue_hbm, tissue_ref))
    loads += [pltpu.make_async_copy(h, v, int_sem.at[i]) for i, (h, v) in enumerate(ints)]
    for load in loads:
        load.start()

    pl.semaphore_wait(barrier, sum(there.astype(jnp.int32) for there, _ in sides))

    def to_prev(j):
        return remote(img.at[j], strip.at[secs + j], sec_send.at[j], sec_recv.at[j], prev)

    def to_down(t):
        return remote(img.at[t, HALF - HALO : HALF], above.at[t], down_send.at[t], down_recv.at[t], down)

    def to_up(t):
        return remote(img.at[t, 0:HALO], below.at[t], up_send.at[t], up_recv.at[t], up)

    def relay_down(j):
        t = secs + j
        return remote(strip.at[t, HALF // 2 : HALF], above.at[t, HALO - HALF // 2 : HALO], down_send.at[t], down_recv.at[t], down)

    def relay_up(j):
        t = secs + j
        return remote(strip.at[t, 0 : HALF // 2], below.at[t, 0 : HALF // 2], up_send.at[t], up_recv.at[t], up)

    def to_via():
        return remote(img.at[1], transit, sec_send.at[1], via_recv, via)

    def onward():
        return remote(transit, strip.at[secs + 1], via_send, sec_recv.at[1], goal)

    def start_halo(t):
        @pl.when(has_down)
        def _():
            to_down(t).start()

        @pl.when(has_up)
        def _():
            to_up(t).start()

    start_halo(0)

    @pl.when(far_send)
    def _():
        to_via().start()

    @pl.when(has_prev)
    def _():
        to_prev(0).start()

    start_halo(1)

    @pl.when(jnp.logical_and(has_prev, place > 0))
    def _():
        to_prev(1).start()

    @pl.when(jnp.logical_not(has_up))
    def _():
        above[...] = jnp.zeros_like(above)

    @pl.when(jnp.logical_not(has_down))
    def _():
        below[...] = jnp.zeros_like(below)

    @pl.when(jnp.logical_not(has_next))
    def _():
        strip[secs:] = jnp.zeros((2, HALF, strip.shape[2]), jnp.bfloat16)
        above[secs:] = jnp.zeros((2, HALO, strip.shape[2]), jnp.bfloat16)
        below[secs:] = jnp.zeros((2, HALO, strip.shape[2]), jnp.bfloat16)

    nyq[...] = jnp.zeros_like(nyq)
    for load in loads:
        load.wait()

    rows = lax.broadcasted_iota(jnp.int32, (8 * secs, PATCH), 0)
    lanes = lax.broadcasted_iota(jnp.int32, (8 * secs, PATCH), 1)
    for axis, table, phase in ((0, tab_prow, prow), (1, tab_pcol, pcol)):
        wanted = jnp.zeros_like(lanes)
        for s in range(secs):
            for c in range(PC):
                wanted = jnp.where(rows == 8 * s + c, shift_ref[s, 0, axis, c] + REACH, wanted)
        chosen = jnp.logical_or(lanes == wanted, lanes == wanted + HALF)
        picked = dot(chosen.astype(jnp.float32).astype(jnp.bfloat16), table[...])
        phase[...] = picked.reshape(secs, 8, picked.shape[1])

    def plain(t):
        forward(
            strip.at[t], above.at[t], below.at[t], [(None, 64)] * PC, None, tab_row, tab_col, nyq,
            spec.at[t - 1], spec_nyq.at[t - 1], rstd.at[t - 1],
        )

    def own(s):
        starts = [(shift_ref[s, 0, 0, c] + 64, shift_ref[s, 0, 1, c] + 64) for c in range(PC)]
        phases = [pcol[s, c : c + 1] for c in range(PC)]
        forward(
            strip.at[s], above.at[s], below.at[s], starts, phases, tab_row, tab_col, nyq,
            own_spec.at[s], own_nyq.at[s], own_rstd.at[s],
        )

    first = lax.broadcasted_iota(jnp.int32, (8, HALF), 0) == 0

    def pairs(s):
        for c in range(PC):
            cols = []
            for part in (s, s + 1):
                ge, go = crossed(own_spec[s, c], spec[part, c])
                xe, xo = crossed(own_nyq[s], spec_nyq[part])
                ge = jnp.concatenate([ge, xe], 0)
                go = jnp.concatenate([go, xo], 0)
                g = dot(ge, tab_bcol[0]) + dot(go, tab_bcol[1])
                edge = jnp.broadcast_to(g[HALF + c : HALF + c + 1, :HALF], (8, HALF))
                im = g[:HALF, HALF:]
                head = jnp.where(first, edge, im[0:8])
                cols.append(jnp.concatenate([g[:HALF, :HALF], head, im[8:]], 0))
            right = jnp.concatenate(cols, 1).astype(jnp.bfloat16)
            turn = prow[s, c : c + 1]
            cos, cos_edge, sin = turn[:, :HALF], turn[:, HALF : 2 * HALF], turn[:, 2 * HALF :]
            bc, bs = tab_brow[:, :HALF], tab_brow[:, HALF:]
            left = jnp.concatenate([bc * cos - bs * sin, bs * cos_edge + bc * sin], 1).astype(jnp.bfloat16)
            maps = dot(left, right)
            weight = tissue_ref[s, 0, c].astype(jnp.float32) / float(PATCH * PATCH)
            base = own_rstd[s, c] * weight
            near = maps[:, :HALF].reshape(SHIFTS // 8, 8, HALF)
            far = maps[:, HALF:].reshape(SHIFTS // 8, 8, HALF)
            for slot in range(2):
                step = step_ref[slot, s].astype(jnp.float32)
                by_near = base * rstd[s, c] * (2.0 - step)
                by_far = base * rstd[s + 1, c] * (step - 1.0)
                stage[s, slot, c] = (near * by_near[None] + far * by_far[None]).reshape(SHIFTS, SHIFTS)

    def save(s):
        return pltpu.make_async_copy(stage.at[s], out.at[s], out_sem.at[s])

    def each(t, carry):
        @pl.when(t + 2 < secs)
        def _():
            start_halo(t + 2)

        @pl.when(jnp.logical_and(carries, t == 1))
        def _():
            to_via().wait_recv()
            onward().start()

        for j in range(2):
            @pl.when(jnp.logical_and(has_next, t == 2 + j))
            def _():
                to_prev(j).wait_recv()

                @pl.when(has_down)
                def _():
                    relay_down(j).start()

                @pl.when(has_up)
                def _():
                    relay_up(j).start()

        @pl.when(t < secs)
        def _():
            @pl.when(has_up)
            def _():
                to_down(t).wait_recv()

            @pl.when(has_down)
            def _():
                to_up(t).wait_recv()

            own(t)

        for j in range(2):
            @pl.when(jnp.logical_and(has_next, t == secs + j))
            def _():
                @pl.when(has_up)
                def _():
                    relay_down(j).wait_recv()

                @pl.when(has_down)
                def _():
                    relay_up(j).wait_recv()

        @pl.when(t >= 1)
        def _():
            plain(t)

        @pl.when(t >= 2)
        def _():
            pairs(t - 2)
            save(t - 2).start()

        return carry

    img_copy.wait()
    lax.fori_loop(0, secs + 2, each, 0)

    @pl.when(has_prev)
    def _():
        for j in range(2):
            to_prev(j).wait_send()

    @pl.when(carries)
    def _():
        onward().wait_send()

    @pl.when(has_down)
    def _():
        for t in range(secs):
            to_down(t).wait_send()

    @pl.when(has_up)
    def _():
        for t in range(secs):
            to_up(t).wait_send()

    @pl.when(jnp.logical_and(has_next, has_down))
    def _():
        for j in range(2):
            relay_down(j).wait_send()

    @pl.when(jnp.logical_and(has_next, has_up))
    def _():
        for j in range(2):
            relay_up(j).wait_send()

    for s in range(secs):
        save(s).wait()


def on_device(secs_axis, rows_axis, image, grid_shift, partner_step, tissue):
    secs, height, width = image.shape
    tables = [jnp.asarray(t) for t in (row_table(), col_tables(), back_col_tables(), back_row_table(), col_phases(), row_phases())]
    ints = [jnp.swapaxes(grid_shift, 2, 3), jnp.swapaxes(partner_step, 0, 1), tissue]
    dma = pltpu.SemaphoreType.DMA
    maps = pl.pallas_call(
        functools.partial(kernel, secs_axis, rows_axis),
        out_shape=jax.ShapeDtypeStruct((secs, 2, PC, SHIFTS, SHIFTS), jnp.float32),
        in_specs=[pl.BlockSpec(memory_space=pltpu.HBM)] * 10,
        out_specs=pl.BlockSpec(memory_space=pl.ANY),
        scratch_shapes=[pltpu.VMEM(t.shape, t.dtype) for t in tables]
        + [
            pltpu.VMEM((secs + 2, height, width), jnp.bfloat16),
            pltpu.VMEM((secs + 2, HALO, width), jnp.bfloat16),
            pltpu.VMEM((secs + 2, HALO, width), jnp.bfloat16),
            pltpu.VMEM((secs, 8, 4 * HALF), jnp.float32),
            pltpu.VMEM((secs, 8, 3 * HALF), jnp.float32),
            pltpu.VMEM((16, PATCH), jnp.float32),
            pltpu.VMEM((secs, PC, HALF, WIDE), jnp.bfloat16),
            pltpu.VMEM((secs, 16, WIDE), jnp.bfloat16),
            pltpu.VMEM((secs, PC, 8, HALF), jnp.float32),
            pltpu.VMEM((secs + 1, PC, HALF, WIDE), jnp.bfloat16),
            pltpu.VMEM((secs + 1, 16, WIDE), jnp.bfloat16),
            pltpu.VMEM((secs + 1, PC, 8, HALF), jnp.float32),
            pltpu.VMEM((secs, 2, PC, SHIFTS, SHIFTS), jnp.float32),
            dma((6,)),
            dma,
            dma((secs,)),
            dma((secs + 2,)),
            dma((secs + 2,)),
            dma((secs + 2,)),
            dma((secs + 2,)),
            dma((2,)),
            dma((2,)),
            pltpu.VMEM((height, width), jnp.bfloat16),
            dma,
            dma,
        ]
        + [pltpu.SMEM(x.shape, x.dtype) for x in ints]
        + [
            dma((3,)),
        ],
        compiler_params=pltpu.CompilerParams(
            vmem_limit_bytes=40 * 1024 * 1024, collective_id=0, has_side_effects=True
        ),
        cost_estimate=pl.CostEstimate(flops=6_000_000_000, bytes_accessed=8_000_000, transcendentals=0),
    )(
        *[pltpu.with_memory_space_constraint(x, pltpu.HBM) for x in (*ints, image, *tables)]
    )
    return maps.reshape(secs, 2, 1, PC, SHIFTS * SHIFTS)


def solution(mesh):
    return jax.shard_map(
        functools.partial(on_device, mesh.shape["sec"], mesh.shape["row"]),
        mesh=mesh,
        in_specs=(
            P("sec", "row", None),
            P("sec", "row", None, None),
            P("sec", None),
            P("sec", "row", None),
        ),
        out_specs=P("sec", None, "row", None, None),
        check_vma=False,
    )
```

```python
import functools

import jax
import jax.numpy as jnp
import ml_dtypes
import numpy as np
from jax import lax
from jax.experimental import pallas as pl
from jax.experimental.pallas import tpu as pltpu
from jax.sharding import PartitionSpec as P

PC = 5
PATCH = 256
HALF = 128
REACH = 32
GROUP = 4
HALO = 96
SHIFTS = 128
WIDE = 4 * HALF
STACK = PC * HALF + 16


def angle(product):
    return 2.0 * np.pi * (product % PATCH) / PATCH


def row_table():
    k = np.arange(HALF)[:, None]
    r = np.arange(PATCH)[None, :]
    sine = np.sin(angle(k * r))
    sine[0] = 1.0 - 2.0 * (np.arange(PATCH) % 2)
    return np.concatenate([np.cos(angle(k * r)), sine], 0).astype(ml_dtypes.bfloat16)


def col_tables():
    c = np.arange(HALF)[:, None]
    out = []
    for odd in (0, 1):
        ell = 2 * np.arange(HALF)[None, :] + odd
        cos, sin = np.cos(angle(ell * c)), np.sin(angle(ell * c))
        out.append(np.block([[cos, -sin], [-sin, -cos]]))
    return np.stack(out).astype(ml_dtypes.bfloat16)


def back_col_tables():
    v = np.arange(SHIFTS)[None, :] - SHIFTS // 2
    out = []
    for odd in (0, 1):
        ell = 2 * np.arange(HALF)[:, None] + odd
        cos, sin = np.cos(angle(ell * v)), np.sin(angle(ell * v))
        out.append(np.block([[cos, sin], [-sin, cos]]))
    return np.stack(out).astype(ml_dtypes.bfloat16)


def back_row_table():
    u = np.arange(SHIFTS)[:, None] - SHIFTS // 2
    k = np.arange(HALF)[None, :]
    weight = np.where(k == 0, 1.0, 2.0)
    sine = -weight * np.sin(angle(u * k))
    sine[:, 0] = 1.0 - 2.0 * (u[:, 0] % 2)
    return np.concatenate([weight * np.cos(angle(u * k)), sine], 1).astype(np.float32)


def phase_table(frequencies):
    s = np.arange(2 * REACH + 1)[:, None] - REACH
    parts = np.concatenate([f(angle(ell[None, :] * s)) for f, ell in frequencies], 1)
    high = parts.astype(ml_dtypes.bfloat16)
    low = (parts - high.astype(np.float64)).astype(ml_dtypes.bfloat16)
    out = np.zeros((PATCH, parts.shape[1]), ml_dtypes.bfloat16)
    out[: len(s)], out[HALF : HALF + len(s)] = high, low
    return out


def col_phases():
    even = 2 * np.arange(HALF)
    return phase_table([(f, ell) for f in (np.cos, np.sin) for ell in (even, even + 1)])


def row_phases():
    k = np.arange(HALF)
    return phase_table([(np.cos, k), (np.cos, np.where(k == 0, HALF, k)), (np.sin, k)])


def dot(a, b):
    return jnp.dot(a, b, preferred_element_type=jnp.float32)


def folded(own, above, below, tile, start):
    lanes = slice(tile * HALF, (tile + 1) * HALF)
    if start is None:
        return jnp.concatenate([below[0:64, lanes], above[32:96, lanes], own[:, lanes]], 0)
    low = above[0:64, lanes]
    high = below[32:96, lanes]
    rows = lax.broadcasted_iota(jnp.int32, (64, HALF), 0) + 32
    mixed = jnp.where(rows >= start, low.astype(jnp.float32), high.astype(jnp.float32)).astype(jnp.bfloat16)
    return jnp.concatenate([below[0:32, lanes], mixed, above[64:96, lanes], own[:, lanes]], 0)


def window(own, above, below, c, row_start, col_start):
    right = folded(own, above, below, c, row_start)
    zero = jnp.zeros((PATCH, HALF), jnp.bfloat16)
    far = folded(own, above, below, c - 1, row_start) if c > 0 else zero
    near = folded(own, above, below, c + 1, row_start) if c < PC - 1 else zero
    lanes = lax.broadcasted_iota(jnp.int32, (PATCH, HALF), 1)
    left = jnp.where(lanes >= col_start, far.astype(jnp.float32), near.astype(jnp.float32)).astype(jnp.bfloat16)
    return jnp.concatenate([left, right], 1)


def forward(jobs, tab_row, tab_col, lhs, nyq):
    first = lax.broadcasted_iota(jnp.int32, (8, HALF), 0) == 0

    def top(block):
        return block[0:8], block[8:]

    for i, (own, above, below, starts, phases, spec, rstd) in enumerate(jobs):
        base = i * STACK
        for c in range(PC):
            x = window(own, above, below, c, *starts[c])
            part = dot(tab_row[...], x)
            lo, hi = part[:, :HALF], part[:, HALF:]
            even, odd = lo + hi, lo - hi
            ce, se, co, so = even[:HALF], even[HALF:], odd[:HALF], odd[HALF:]
            head, tail = top(ce)
            centre = jnp.mean(head[0:1], axis=1, keepdims=True)
            head = jnp.where(first, head - centre, head)
            ce = jnp.concatenate([head, tail], 0)
            square = jnp.zeros((8, HALF), jnp.float32)
            edge = jnp.zeros((8, HALF), jnp.float32)
            for block in (ce, se, co, so):
                sq = block * block
                square = square + jnp.sum(sq.reshape(HALF // 8, 8, HALF), axis=0)
                edge = edge + sq[0:8]
            total = 2.0 * square - jnp.where(first, edge, 0.0)
            var = jnp.sum(jnp.sum(total, axis=0, keepdims=True), axis=1, keepdims=True) * (
                HALF / float(PATCH**4)
            )
            rstd[c] = jnp.broadcast_to(lax.rsqrt(var + 1e-05), (8, HALF))
            he, te = top(se)
            ho, to = top(so)
            nyq[i, c : c + 1, :HALF] = he[0:1]
            nyq[i, c : c + 1, HALF:] = ho[0:1]
            se = jnp.concatenate([jnp.where(first, 0.0, he), te], 0)
            so = jnp.concatenate([jnp.where(first, 0.0, ho), to], 0)
            rows = slice(base + c * HALF, base + (c + 1) * HALF)
            lhs[0, rows] = jnp.concatenate([ce, se], 1).astype(jnp.bfloat16)
            lhs[1, rows] = jnp.concatenate([co, so], 1).astype(jnp.bfloat16)
        rows = slice(base + PC * HALF, base + STACK)
        zero = jnp.zeros((16, HALF), jnp.bfloat16)
        lhs[0, rows] = jnp.concatenate([nyq[i, :, :HALF].astype(jnp.bfloat16), zero], 1)
        lhs[1, rows] = jnp.concatenate([nyq[i, :, HALF:].astype(jnp.bfloat16), zero], 1)
    for q in range(2):
        f = dot(lhs[q, : len(jobs) * STACK], tab_col[q])
        for i, (_, _, _, _, phases, spec, _) in enumerate(jobs):
            block = f[i * STACK : (i + 1) * STACK]
            if phases is None:
                spec[:, q * PATCH : (q + 1) * PATCH] = block.astype(jnp.bfloat16)
                continue
            cos = [p[:, q * HALF : (q + 1) * HALF] for p in phases]
            sin = [p[:, (q + 2) * HALF : (q + 3) * HALF] for p in phases]
            spare = jnp.zeros((16 - PC, HALF), jnp.float32)
            cos.append(jnp.concatenate(cos + [spare], 0))
            sin.append(jnp.concatenate(sin + [spare], 0))
            for c in range(PC + 1):
                rows = slice(c * HALF, min((c + 1) * HALF, STACK))
                re, im = block[rows, :HALF], block[rows, HALF:]
                turned = jnp.concatenate([re * cos[c] - im * sin[c], re * sin[c] + im * cos[c]], 1)
                spec[rows, q * PATCH : (q + 1) * PATCH] = turned.astype(jnp.bfloat16)


def crossed(a, b):
    out = []
    for base in (0, 2 * HALF):
        re, im = slice(base, base + HALF), slice(base + HALF, base + 2 * HALF)
        are, aim = a[:, re], a[:, im]
        bre, bim = b[:, re], b[:, im]
        g = jnp.concatenate([are * bre + aim * bim, are * bim - aim * bre], 1)
        out.append(g)
    return out


def remote(src, dst, send, recv, where):
    return pltpu.make_async_remote_copy(
        src_ref=src, dst_ref=dst, send_sem=send, recv_sem=recv, device_id=where, device_id_type=pl.DeviceIdType.MESH
    )


def kernel(
    secs_axis, rows_axis,
    shift_hbm, step_hbm, tissue_hbm, img, *refs,
):
    tables, refs = refs[:6], refs[6:]
    out, refs = refs[0], refs[1:]
    tabs, refs = refs[:6], refs[6:]
    (strip, above, below, pcol, prow, lhs, nyq, right, own_spec, own_rstd, spec, rstd, stage,
     tab_sem, img_sem, out_sem, up_send, up_recv, down_send, down_recv, sec_send, sec_recv,
     part_send, part_recv, transit, via_send, via_recv, shift_ref, step_ref, tissue_ref, int_sem) = refs
    tab_row, tab_col, tab_bcol, tab_brow, tab_pcol, tab_prow = tabs
    secs = own_spec.shape[0]
    sec, row = lax.axis_index("sec"), lax.axis_index("row")
    has_up, has_down = row > 0, row < rows_axis - 1
    has_prev, has_next = sec > 0, sec < secs_axis - 1
    up, down, prev, following = (sec, row - 1), (sec, row + 1), (sec - 1, row), (sec + 1, row)
    place = lax.rem(sec, GROUP)
    far_send = jnp.logical_and(place == 0, has_prev)
    far_take = jnp.logical_and(place == GROUP - 1, has_next)
    carries = [jnp.logical_and(place == p, sec > p) for p in range(GROUP)]
    sides = [(has_up, up), (has_down, down), (has_prev, prev), (has_next, following)]
    for p in range(1, GROUP):
        if p > 1:
            sides += [(far_send, (sec + p, row)), (carries[p], (sec - p, row))]
        sides += [(far_take, (sec + p + 1, row)), (carries[p], (sec - p - 1, row))]

    barrier = pltpu.get_barrier_semaphore()
    for there, where in sides:
        @pl.when(there)
        def _():
            pl.semaphore_signal(barrier, inc=1, device_id=where, device_id_type=pl.DeviceIdType.MESH)

    img_copy = pltpu.make_async_copy(img, strip.at[0:secs], img_sem)
    img_copy.start()
    loads = [pltpu.make_async_copy(t, v, tab_sem.at[i]) for i, (t, v) in enumerate(zip(tables, tabs))]
    ints = ((shift_hbm, shift_ref), (step_hbm, step_ref), (tissue_hbm, tissue_ref))
    loads += [pltpu.make_async_copy(h, v, int_sem.at[i]) for i, (h, v) in enumerate(ints)]
    for load in loads:
        load.start()

    pl.semaphore_wait(barrier, sum(there.astype(jnp.int32) for there, _ in sides))

    def to_prev(j):
        return remote(img.at[j], strip.at[secs + j], sec_send.at[j], sec_recv.at[j], prev)

    def to_down(t):
        return remote(img.at[t, HALF - HALO : HALF], above.at[t], down_send.at[t], down_recv.at[t], down)

    def to_up(t):
        return remote(img.at[t, 0:HALO], below.at[t], up_send.at[t], up_recv.at[t], up)

    def relay_down(j):
        t = secs + j
        return remote(strip.at[t, HALF // 2 : HALF], above.at[t, HALO - HALF // 2 : HALO], down_send.at[t], down_recv.at[t], down)

    def relay_up(j):
        t = secs + j
        return remote(strip.at[t, 0 : HALF // 2], below.at[t, 0 : HALF // 2], up_send.at[t], up_recv.at[t], up)

    def part(p):
        return p // 2, slice(p % 2 * (HALF // 2), (p % 2 + 1) * (HALF // 2))

    def to_far():
        return remote(img.at[0, : HALF // 2], strip.at[secs, : HALF // 2], part_send.at[0], part_recv.at[0], prev)

    def to_carrier(p):
        j, rows = part(p)
        return remote(img.at[j, rows], transit, part_send.at[p], via_recv, (sec + p, row))

    def onward(p):
        j, rows = part(p)
        return remote(transit, strip.at[secs + j, rows], via_send, part_recv.at[p], (sec - p - 1, row))

    def arrival(p):
        j, rows = part(p)
        return remote(transit, strip.at[secs + j, rows], via_send, part_recv.at[p], (sec + p + 1, row))

    def start_halo(t):
        @pl.when(has_down)
        def _():
            to_down(t).start()

        @pl.when(has_up)
        def _():
            to_up(t).start()

    start_halo(0)

    near_send = jnp.logical_and(has_prev, place > 0)
    near_take = jnp.logical_and(has_next, place < GROUP - 1)

    @pl.when(far_send)
    def _():
        for p in range(1, GROUP):
            to_carrier(p).start()
        to_far().start()

    @pl.when(near_send)
    def _():
        to_prev(0).start()

    start_halo(1)

    @pl.when(near_send)
    def _():
        to_prev(1).start()

    @pl.when(jnp.logical_not(has_up))
    def _():
        above[...] = jnp.zeros_like(above)

    @pl.when(jnp.logical_not(has_down))
    def _():
        below[...] = jnp.zeros_like(below)

    @pl.when(jnp.logical_not(has_next))
    def _():
        strip[secs:] = jnp.zeros((2, HALF, strip.shape[2]), jnp.bfloat16)
        above[secs:] = jnp.zeros((2, HALO, strip.shape[2]), jnp.bfloat16)
        below[secs:] = jnp.zeros((2, HALO, strip.shape[2]), jnp.bfloat16)

    nyq[...] = jnp.zeros_like(nyq)
    for load in loads:
        load.wait()

    rows = lax.broadcasted_iota(jnp.int32, (8 * secs, PATCH), 0)
    lanes = lax.broadcasted_iota(jnp.int32, (8 * secs, PATCH), 1)
    for axis, table, phase in ((0, tab_prow, prow), (1, tab_pcol, pcol)):
        wanted = jnp.zeros_like(lanes)
        for s in range(secs):
            for c in range(PC):
                wanted = jnp.where(rows == 8 * s + c, shift_ref[s, 0, axis, c] + REACH, wanted)
        chosen = jnp.logical_or(lanes == wanted, lanes == wanted + HALF)
        picked = dot(chosen.astype(jnp.float32).astype(jnp.bfloat16), table[...])
        phase[...] = picked.reshape(secs, 8, picked.shape[1])

    def plain(t):
        return (strip.at[t], above.at[t], below.at[t], [(None, 64)] * PC, None, spec.at[t - 1], rstd.at[t - 1])

    def own(s):
        starts = [(shift_ref[s, 0, 0, c] + 64, shift_ref[s, 0, 1, c] + 64) for c in range(PC)]
        phases = [pcol[s, c : c + 1] for c in range(PC)]
        return (strip.at[s], above.at[s], below.at[s], starts, phases, own_spec.at[s], own_rstd.at[s])

    def spectra(*jobs):
        forward(jobs, tab_row, tab_col, lhs, nyq)

    first = lax.broadcasted_iota(jnp.int32, (8, HALF), 0) == 0

    def pairs(s):
        for part in range(2):
            ge, go = crossed(own_spec[s], spec[s + part])
            g = dot(ge, tab_bcol[0]) + dot(go, tab_bcol[1])
            lanes = slice(part * HALF, (part + 1) * HALF)
            for c in range(PC):
                block = g[c * HALF : (c + 1) * HALF]
                edge = jnp.broadcast_to(g[PC * HALF + c : PC * HALF + c + 1, :HALF], (8, HALF))
                im = block[:, HALF:]
                im = jnp.concatenate([jnp.where(first, edge, im[0:8]), im[8:]], 0)
                right[c, :HALF, lanes] = block[:, :HALF].astype(jnp.bfloat16)
                right[c, HALF:, lanes] = im.astype(jnp.bfloat16)
        for c in range(PC):
            turn = prow[s, c : c + 1]
            cos, cos_edge, sin = turn[:, :HALF], turn[:, HALF : 2 * HALF], turn[:, 2 * HALF :]
            bc, bs = tab_brow[:, :HALF], tab_brow[:, HALF:]
            left = jnp.concatenate([bc * cos - bs * sin, bs * cos_edge + bc * sin], 1).astype(jnp.bfloat16)
            maps = dot(left, right[c])
            weight = tissue_ref[s, 0, c].astype(jnp.float32) / float(PATCH * PATCH)
            base = own_rstd[s, c] * weight
            near = maps[:, :HALF].reshape(SHIFTS // 8, 8, HALF)
            far = maps[:, HALF:].reshape(SHIFTS // 8, 8, HALF)
            for slot in range(2):
                step = step_ref[slot, s].astype(jnp.float32)
                by_near = base * rstd[s, c] * (2.0 - step)
                by_far = base * rstd[s + 1, c] * (step - 1.0)
                stage[s, slot, c] = (near * by_near[None] + far * by_far[None]).reshape(SHIFTS, SHIFTS)

    def save(s):
        return pltpu.make_async_copy(stage.at[s], out.at[s], out_sem.at[s])

    def each(t, carry):
        @pl.when(t + 2 < secs)
        def _():
            start_halo(t + 2)

        for p in range(1, GROUP):
            @pl.when(jnp.logical_and(carries[p], t == 1))
            def _():
                to_carrier(p).wait_recv()
                onward(p).start()

        for j in range(2):
            @pl.when(jnp.logical_and(near_take, t == 3 + j))
            def _():
                to_prev(j).wait_recv()

            @pl.when(jnp.logical_and(far_take, t == 3 + j))
            def _():
                arrival(2 * j).wait_recv()
                arrival(2 * j + 1).wait_recv()

            @pl.when(jnp.logical_and(has_next, t == 3 + j))
            def _():
                @pl.when(has_down)
                def _():
                    relay_down(j).start()

                @pl.when(has_up)
                def _():
                    relay_up(j).start()

        @pl.when(t < secs)
        def _():
            @pl.when(has_up)
            def _():
                to_down(t).wait_recv()

            @pl.when(has_down)
            def _():
                to_up(t).wait_recv()

        for j in range(2):
            @pl.when(jnp.logical_and(has_next, t == secs + j))
            def _():
                @pl.when(has_up)
                def _():
                    relay_down(j).wait_recv()

                @pl.when(has_down)
                def _():
                    relay_up(j).wait_recv()

        @pl.when(t == 0)
        def _():
            spectra(own(t))

        @pl.when(jnp.logical_and(t >= 1, t < secs))
        def _():
            spectra(own(t), plain(t))

        @pl.when(t >= secs)
        def _():
            spectra(plain(t))

        @pl.when(t >= 2)
        def _():
            pairs(t - 2)
            save(t - 2).start()

        return carry

    img_copy.wait()
    lax.fori_loop(0, secs + 2, each, 0)

    @pl.when(near_send)
    def _():
        for j in range(2):
            to_prev(j).wait_send()

    @pl.when(far_send)
    def _():
        to_far().wait_send()
        for p in range(1, GROUP):
            to_carrier(p).wait_send()

    for p in range(1, GROUP):
        @pl.when(carries[p])
        def _():
            onward(p).wait_send()

    @pl.when(has_down)
    def _():
        for t in range(secs):
            to_down(t).wait_send()

    @pl.when(has_up)
    def _():
        for t in range(secs):
            to_up(t).wait_send()

    @pl.when(jnp.logical_and(has_next, has_down))
    def _():
        for j in range(2):
            relay_down(j).wait_send()

    @pl.when(jnp.logical_and(has_next, has_up))
    def _():
        for j in range(2):
            relay_up(j).wait_send()

    for s in range(secs):
        save(s).wait()


def on_device(secs_axis, rows_axis, image, grid_shift, partner_step, tissue):
    secs, height, width = image.shape
    tables = [jnp.asarray(t) for t in (row_table(), col_tables(), back_col_tables(), back_row_table(), col_phases(), row_phases())]
    ints = [jnp.swapaxes(grid_shift, 2, 3), jnp.swapaxes(partner_step, 0, 1), tissue]
    dma = pltpu.SemaphoreType.DMA
    maps = pl.pallas_call(
        functools.partial(kernel, secs_axis, rows_axis),
        out_shape=jax.ShapeDtypeStruct((secs, 2, PC, SHIFTS, SHIFTS), jnp.float32),
        in_specs=[pl.BlockSpec(memory_space=pltpu.HBM)] * 10,
        out_specs=pl.BlockSpec(memory_space=pl.ANY),
        scratch_shapes=[pltpu.VMEM(t.shape, t.dtype) for t in tables]
        + [
            pltpu.VMEM((secs + 2, height, width), jnp.bfloat16),
            pltpu.VMEM((secs + 2, HALO, width), jnp.bfloat16),
            pltpu.VMEM((secs + 2, HALO, width), jnp.bfloat16),
            pltpu.VMEM((secs, 8, 4 * HALF), jnp.float32),
            pltpu.VMEM((secs, 8, 3 * HALF), jnp.float32),
            pltpu.VMEM((2, 2 * STACK, PATCH), jnp.bfloat16),
            pltpu.VMEM((2, 16, PATCH), jnp.float32),
            pltpu.VMEM((PC, PATCH, PATCH), jnp.bfloat16),
            pltpu.VMEM((secs, STACK, WIDE), jnp.bfloat16),
            pltpu.VMEM((secs, PC, 8, HALF), jnp.float32),
            pltpu.VMEM((secs + 1, STACK, WIDE), jnp.bfloat16),
            pltpu.VMEM((secs + 1, PC, 8, HALF), jnp.float32),
            pltpu.VMEM((secs, 2, PC, SHIFTS, SHIFTS), jnp.float32),
            dma((6,)),
            dma,
            dma((secs,)),
            dma((secs + 2,)),
            dma((secs + 2,)),
            dma((secs + 2,)),
            dma((secs + 2,)),
            dma((2,)),
            dma((2,)),
            dma((GROUP,)),
            dma((GROUP,)),
            pltpu.VMEM((HALF // 2, width), jnp.bfloat16),
            dma,
            dma,
        ]
        + [pltpu.SMEM(x.shape, x.dtype) for x in ints]
        + [
            dma((3,)),
        ],
        compiler_params=pltpu.CompilerParams(
            vmem_limit_bytes=40 * 1024 * 1024, collective_id=0, has_side_effects=True
        ),
        cost_estimate=pl.CostEstimate(flops=6_000_000_000, bytes_accessed=8_000_000, transcendentals=0),
    )(
        *[pltpu.with_memory_space_constraint(x, pltpu.HBM) for x in (*ints, image, *tables)]
    )
    return maps.reshape(secs, 2, 1, PC, SHIFTS * SHIFTS)


def solution(mesh):
    return jax.shard_map(
        functools.partial(on_device, mesh.shape["sec"], mesh.shape["row"]),
        mesh=mesh,
        in_specs=(
            P("sec", "row", None),
            P("sec", "row", None, None),
            P("sec", None),
            P("sec", "row", None),
        ),
        out_specs=P("sec", None, "row", None, None),
        check_vma=False,
    )
```

```python
import functools

import jax
import jax.numpy as jnp
import ml_dtypes
import numpy as np
from jax import lax
from jax.experimental import pallas as pl
from jax.experimental.pallas import tpu as pltpu
from jax.sharding import PartitionSpec as P

PC = 5
PATCH = 256
HALF = 128
REACH = 32
GROUP = 4
HALO = 96
SHIFTS = 128
WIDE = 4 * HALF
STACK = PC * HALF + 16


def angle(product):
    return 2.0 * np.pi * (product % PATCH) / PATCH


def row_table():
    k = np.arange(HALF)[:, None]
    r = np.arange(PATCH)[None, :]
    sine = np.sin(angle(k * r))
    sine[0] = 1.0 - 2.0 * (np.arange(PATCH) % 2)
    return np.concatenate([np.cos(angle(k * r)), sine], 0).astype(ml_dtypes.bfloat16)


def col_tables():
    c = np.arange(HALF)[:, None]
    out = []
    for odd in (0, 1):
        ell = 2 * np.arange(HALF)[None, :] + odd
        cos, sin = np.cos(angle(ell * c)), np.sin(angle(ell * c))
        out.append(np.block([[cos, -sin], [-sin, -cos]]))
    return np.stack(out).astype(ml_dtypes.bfloat16)


def back_col_tables():
    v = np.arange(SHIFTS)[None, :] - SHIFTS // 2
    out = []
    for odd in (0, 1):
        ell = 2 * np.arange(HALF)[:, None] + odd
        cos, sin = np.cos(angle(ell * v)), np.sin(angle(ell * v))
        out.append(np.block([[cos, sin], [-sin, cos]]))
    return np.stack(out).astype(ml_dtypes.bfloat16)


def back_row_table():
    u = np.arange(SHIFTS)[:, None] - SHIFTS // 2
    k = np.arange(HALF)[None, :]
    weight = np.where(k == 0, 1.0, 2.0)
    sine = -weight * np.sin(angle(u * k))
    sine[:, 0] = 1.0 - 2.0 * (u[:, 0] % 2)
    return np.concatenate([weight * np.cos(angle(u * k)), sine], 1).astype(np.float32)


def phase_table(frequencies):
    s = np.arange(2 * REACH + 1)[:, None] - REACH
    parts = np.concatenate([f(angle(ell[None, :] * s)) for f, ell in frequencies], 1)
    high = parts.astype(ml_dtypes.bfloat16)
    low = (parts - high.astype(np.float64)).astype(ml_dtypes.bfloat16)
    out = np.zeros((PATCH, parts.shape[1]), ml_dtypes.bfloat16)
    out[: len(s)], out[HALF : HALF + len(s)] = high, low
    return out


def col_phases():
    even = 2 * np.arange(HALF)
    return phase_table([(f, ell) for f in (np.cos, np.sin) for ell in (even, even + 1)])


def row_phases():
    k = np.arange(HALF)
    return phase_table([(np.cos, k), (np.cos, np.where(k == 0, HALF, k)), (np.sin, k)])


def dot(a, b):
    return jnp.dot(a, b, preferred_element_type=jnp.float32)


def folded(own, above, below, tile, start):
    lanes = slice(tile * HALF, (tile + 1) * HALF)
    if start is None:
        return jnp.concatenate([below[0:64, lanes], above[32:96, lanes], own[:, lanes]], 0)
    low = above[0:64, lanes]
    high = below[32:96, lanes]
    rows = lax.broadcasted_iota(jnp.int32, (64, HALF), 0) + 32
    mixed = jnp.where(rows >= start, low.astype(jnp.float32), high.astype(jnp.float32)).astype(jnp.bfloat16)
    return jnp.concatenate([below[0:32, lanes], mixed, above[64:96, lanes], own[:, lanes]], 0)


def window(own, above, below, c, row_start, col_start):
    right = folded(own, above, below, c, row_start)
    zero = jnp.zeros((PATCH, HALF), jnp.bfloat16)
    far = folded(own, above, below, c - 1, row_start) if c > 0 else zero
    near = folded(own, above, below, c + 1, row_start) if c < PC - 1 else zero
    lanes = lax.broadcasted_iota(jnp.int32, (PATCH, HALF), 1)
    left = jnp.where(lanes >= col_start, far.astype(jnp.float32), near.astype(jnp.float32)).astype(jnp.bfloat16)
    return jnp.concatenate([left, right], 1)


def forward(jobs, tab_row, tab_col, lhs, nyq):
    first = lax.broadcasted_iota(jnp.int32, (8, HALF), 0) == 0

    def top(block):
        return block[0:8], block[8:]

    for i, (own, above, below, starts, phases, spec, rstd) in enumerate(jobs):
        base = i * STACK
        for c in range(PC):
            x = window(own, above, below, c, *starts[c])
            part = dot(tab_row[...], x)
            lo, hi = part[:, :HALF], part[:, HALF:]
            even, odd = lo + hi, lo - hi
            ce, se, co, so = even[:HALF], even[HALF:], odd[:HALF], odd[HALF:]
            head, tail = top(ce)
            centre = jnp.mean(head[0:1], axis=1, keepdims=True)
            head = jnp.where(first, head - centre, head)
            ce = jnp.concatenate([head, tail], 0)
            square = jnp.zeros((8, HALF), jnp.float32)
            edge = jnp.zeros((8, HALF), jnp.float32)
            for block in (ce, se, co, so):
                sq = block * block
                square = square + jnp.sum(sq.reshape(HALF // 8, 8, HALF), axis=0)
                edge = edge + sq[0:8]
            total = 2.0 * square - jnp.where(first, edge, 0.0)
            var = jnp.sum(jnp.sum(total, axis=0, keepdims=True), axis=1, keepdims=True) * (
                HALF / float(PATCH**4)
            )
            rstd[c] = jnp.broadcast_to(lax.rsqrt(var + 1e-05), (8, HALF))
            he, te = top(se)
            ho, to = top(so)
            nyq[i, c : c + 1, :HALF] = he[0:1]
            nyq[i, c : c + 1, HALF:] = ho[0:1]
            se = jnp.concatenate([jnp.where(first, 0.0, he), te], 0)
            so = jnp.concatenate([jnp.where(first, 0.0, ho), to], 0)
            rows = slice(base + c * HALF, base + (c + 1) * HALF)
            lhs[0, rows] = jnp.concatenate([ce, se], 1).astype(jnp.bfloat16)
            lhs[1, rows] = jnp.concatenate([co, so], 1).astype(jnp.bfloat16)
        rows = slice(base + PC * HALF, base + STACK)
        zero = jnp.zeros((16, HALF), jnp.bfloat16)
        lhs[0, rows] = jnp.concatenate([nyq[i, :, :HALF].astype(jnp.bfloat16), zero], 1)
        lhs[1, rows] = jnp.concatenate([nyq[i, :, HALF:].astype(jnp.bfloat16), zero], 1)
    for q in range(2):
        f = dot(lhs[q, : len(jobs) * STACK], tab_col[q])
        for i, (_, _, _, _, phases, spec, _) in enumerate(jobs):
            block = f[i * STACK : (i + 1) * STACK]
            if phases is None:
                spec[:, q * PATCH : (q + 1) * PATCH] = block.astype(jnp.bfloat16)
                continue
            cos = [p[:, q * HALF : (q + 1) * HALF] for p in phases]
            sin = [p[:, (q + 2) * HALF : (q + 3) * HALF] for p in phases]
            spare = jnp.zeros((16 - PC, HALF), jnp.float32)
            cos.append(jnp.concatenate(cos + [spare], 0))
            sin.append(jnp.concatenate(sin + [spare], 0))
            for c in range(PC + 1):
                rows = slice(c * HALF, min((c + 1) * HALF, STACK))
                re, im = block[rows, :HALF], block[rows, HALF:]
                turned = jnp.concatenate([re * cos[c] - im * sin[c], re * sin[c] + im * cos[c]], 1)
                spec[rows, q * PATCH : (q + 1) * PATCH] = turned.astype(jnp.bfloat16)


def crossed(a, b):
    out = []
    for base in (0, 2 * HALF):
        re, im = slice(base, base + HALF), slice(base + HALF, base + 2 * HALF)
        are, aim = a[:, re], a[:, im]
        bre, bim = b[:, re], b[:, im]
        g = jnp.concatenate([are * bre + aim * bim, are * bim - aim * bre], 1)
        out.append(g)
    return out


def remote(src, dst, send, recv, where):
    return pltpu.make_async_remote_copy(
        src_ref=src, dst_ref=dst, send_sem=send, recv_sem=recv, device_id=where, device_id_type=pl.DeviceIdType.MESH
    )


def kernel(
    secs_axis, rows_axis,
    shift_hbm, step_hbm, tissue_hbm, img, *refs,
):
    tables, refs = refs[:6], refs[6:]
    out, refs = refs[0], refs[1:]
    tabs, refs = refs[:6], refs[6:]
    (strip, above, below, pcol, prow, lhs, nyq, right, own_spec, own_rstd, spec, rstd, stage,
     tab_sem, img_sem, out_sem, up_send, up_recv, down_send, down_recv, sec_send, sec_recv,
     part_send, part_recv, transit, via_send, via_recv, shift_ref, step_ref, tissue_ref, int_sem) = refs
    tab_row, tab_col, tab_bcol, tab_brow, tab_pcol, tab_prow = tabs
    secs = own_spec.shape[0]
    sec, row = lax.axis_index("sec"), lax.axis_index("row")
    has_up, has_down = row > 0, row < rows_axis - 1
    has_prev, has_next = sec > 0, sec < secs_axis - 1
    up, down, prev, following = (sec, row - 1), (sec, row + 1), (sec - 1, row), (sec + 1, row)
    place = lax.rem(sec, GROUP)
    far_send = jnp.logical_and(place == 0, has_prev)
    far_take = jnp.logical_and(place == GROUP - 1, has_next)
    carries = [jnp.logical_and(place == p, sec > p) for p in range(GROUP)]
    sides = [(has_up, up), (has_down, down), (has_prev, prev), (has_next, following)]
    for p in range(1, GROUP):
        if p > 1:
            sides += [(far_send, (sec + p, row)), (carries[p], (sec - p, row))]
        sides += [(far_take, (sec + p + 1, row)), (carries[p], (sec - p - 1, row))]

    barrier = pltpu.get_barrier_semaphore()
    for there, where in sides:
        @pl.when(there)
        def _():
            pl.semaphore_signal(barrier, inc=1, device_id=where, device_id_type=pl.DeviceIdType.MESH)

    img_copy = pltpu.make_async_copy(img, strip.at[0:secs], img_sem)
    img_copy.start()
    loads = [pltpu.make_async_copy(t, v, tab_sem.at[i]) for i, (t, v) in enumerate(zip(tables, tabs))]
    ints = ((shift_hbm, shift_ref), (step_hbm, step_ref), (tissue_hbm, tissue_ref))
    loads += [pltpu.make_async_copy(h, v, int_sem.at[i]) for i, (h, v) in enumerate(ints)]
    for load in loads:
        load.start()

    pl.semaphore_wait(barrier, sum(there.astype(jnp.int32) for there, _ in sides))

    def to_prev(j):
        return remote(img.at[j], strip.at[secs + j], sec_send.at[j], sec_recv.at[j], prev)

    def to_down(t):
        return remote(img.at[t, HALF - HALO : HALF], above.at[t], down_send.at[t], down_recv.at[t], down)

    def to_up(t):
        return remote(img.at[t, 0:HALO], below.at[t], up_send.at[t], up_recv.at[t], up)

    def relay_down(j):
        t = secs + j
        return remote(strip.at[t, HALF // 2 : HALF], above.at[t, HALO - HALF // 2 : HALO], down_send.at[t], down_recv.at[t], down)

    def relay_up(j):
        t = secs + j
        return remote(strip.at[t, 0 : HALF // 2], below.at[t, 0 : HALF // 2], up_send.at[t], up_recv.at[t], up)

    def part(p):
        return p // 2, slice(p % 2 * (HALF // 2), (p % 2 + 1) * (HALF // 2))

    def to_far():
        return remote(img.at[0, : HALF // 2], strip.at[secs, : HALF // 2], part_send.at[0], part_recv.at[0], prev)

    def to_carrier(p):
        j, rows = part(p)
        return remote(img.at[j, rows], transit, part_send.at[p], via_recv, (sec + p, row))

    def onward(p):
        j, rows = part(p)
        return remote(transit, strip.at[secs + j, rows], via_send, part_recv.at[p], (sec - p - 1, row))

    def arrival(p):
        j, rows = part(p)
        return remote(transit, strip.at[secs + j, rows], via_send, part_recv.at[p], (sec + p + 1, row))

    def start_halo(t):
        @pl.when(has_down)
        def _():
            to_down(t).start()

        @pl.when(has_up)
        def _():
            to_up(t).start()

    start_halo(0)

    near_send = jnp.logical_and(has_prev, place > 0)
    near_take = jnp.logical_and(has_next, place < GROUP - 1)

    @pl.when(far_send)
    def _():
        for p in range(1, GROUP):
            to_carrier(p).start()
        to_far().start()

    @pl.when(near_send)
    def _():
        to_prev(0).start()

    for t in range(1, secs - 1):
        start_halo(t)

    @pl.when(near_send)
    def _():
        to_prev(1).start()

    @pl.when(jnp.logical_not(jnp.logical_or(jnp.logical_or(carries[1], carries[2]), carries[3])))
    def _():
        start_halo(secs - 1)

    @pl.when(jnp.logical_not(has_up))
    def _():
        above[...] = jnp.zeros_like(above)

    @pl.when(jnp.logical_not(has_down))
    def _():
        below[...] = jnp.zeros_like(below)

    @pl.when(jnp.logical_not(has_next))
    def _():
        strip[secs:] = jnp.zeros((2, HALF, strip.shape[2]), jnp.bfloat16)
        above[secs:] = jnp.zeros((2, HALO, strip.shape[2]), jnp.bfloat16)
        below[secs:] = jnp.zeros((2, HALO, strip.shape[2]), jnp.bfloat16)

    nyq[...] = jnp.zeros_like(nyq)
    for load in loads:
        load.wait()

    rows = lax.broadcasted_iota(jnp.int32, (8 * secs, PATCH), 0)
    lanes = lax.broadcasted_iota(jnp.int32, (8 * secs, PATCH), 1)
    for axis, table, phase in ((0, tab_prow, prow), (1, tab_pcol, pcol)):
        wanted = jnp.zeros_like(lanes)
        for s in range(secs):
            for c in range(PC):
                wanted = jnp.where(rows == 8 * s + c, shift_ref[s, 0, axis, c] + REACH, wanted)
        chosen = jnp.logical_or(lanes == wanted, lanes == wanted + HALF)
        picked = dot(chosen.astype(jnp.float32).astype(jnp.bfloat16), table[...])
        phase[...] = picked.reshape(secs, 8, picked.shape[1])

    def plain(t):
        return (strip.at[t], above.at[t], below.at[t], [(None, 64)] * PC, None, spec.at[t - 1], rstd.at[t - 1])

    def own(s):
        starts = [(shift_ref[s, 0, 0, c] + 64, shift_ref[s, 0, 1, c] + 64) for c in range(PC)]
        phases = [pcol[s, c : c + 1] for c in range(PC)]
        return (strip.at[s], above.at[s], below.at[s], starts, phases, own_spec.at[s], own_rstd.at[s])

    def spectra(*jobs):
        forward(jobs, tab_row, tab_col, lhs, nyq)

    first = lax.broadcasted_iota(jnp.int32, (8, HALF), 0) == 0

    def pairs(s):
        for part in range(2):
            ge, go = crossed(own_spec[s], spec[s + part])
            g = dot(ge, tab_bcol[0]) + dot(go, tab_bcol[1])
            lanes = slice(part * HALF, (part + 1) * HALF)
            for c in range(PC):
                block = g[c * HALF : (c + 1) * HALF]
                edge = jnp.broadcast_to(g[PC * HALF + c : PC * HALF + c + 1, :HALF], (8, HALF))
                im = block[:, HALF:]
                im = jnp.concatenate([jnp.where(first, edge, im[0:8]), im[8:]], 0)
                right[c, :HALF, lanes] = block[:, :HALF].astype(jnp.bfloat16)
                right[c, HALF:, lanes] = im.astype(jnp.bfloat16)
        for c in range(PC):
            turn = prow[s, c : c + 1]
            cos, cos_edge, sin = turn[:, :HALF], turn[:, HALF : 2 * HALF], turn[:, 2 * HALF :]
            bc, bs = tab_brow[:, :HALF], tab_brow[:, HALF:]
            left = jnp.concatenate([bc * cos - bs * sin, bs * cos_edge + bc * sin], 1).astype(jnp.bfloat16)
            maps = dot(left, right[c])
            weight = tissue_ref[s, 0, c].astype(jnp.float32) / float(PATCH * PATCH)
            base = own_rstd[s, c] * weight
            near = maps[:, :HALF].reshape(SHIFTS // 8, 8, HALF)
            far = maps[:, HALF:].reshape(SHIFTS // 8, 8, HALF)
            for slot in range(2):
                step = step_ref[slot, s].astype(jnp.float32)
                by_near = base * rstd[s, c] * (2.0 - step)
                by_far = base * rstd[s + 1, c] * (step - 1.0)
                stage[s, slot, c] = (near * by_near[None] + far * by_far[None]).reshape(SHIFTS, SHIFTS)

    def save(s):
        return pltpu.make_async_copy(stage.at[s], out.at[s], out_sem.at[s])

    def take(t, cases):
        for there, j, when in cases:
            @pl.when(jnp.logical_and(there, t == when))
            def _():
                if there is near_take:
                    to_prev(j).wait_recv()
                else:
                    arrival(2 * j).wait_recv()

                @pl.when(has_up)
                def _():
                    relay_up(j).start()

                if there is not near_take:
                    arrival(2 * j + 1).wait_recv()

                @pl.when(has_down)
                def _():
                    relay_down(j).start()

    def each(t, carry):
        for p in range(1, GROUP):
            @pl.when(jnp.logical_and(carries[p], t == 0))
            def _():
                to_carrier(p).wait_recv()
                onward(p).start()
                start_halo(secs - 1)

        take(t, ((far_take, 0, 3),))

        @pl.when(t < secs)
        def _():
            @pl.when(has_up)
            def _():
                to_down(t).wait_recv()

            @pl.when(has_down)
            def _():
                to_up(t).wait_recv()

        for j in range(2):
            @pl.when(jnp.logical_and(has_next, t == secs + j))
            def _():
                @pl.when(has_up)
                def _():
                    relay_down(j).wait_recv()

                @pl.when(has_down)
                def _():
                    relay_up(j).wait_recv()

        @pl.when(t == 0)
        def _():
            spectra(own(t))

        @pl.when(jnp.logical_and(t >= 1, t < secs))
        def _():
            spectra(own(t), plain(t))

        @pl.when(t >= secs)
        def _():
            spectra(plain(t))

        take(t, ((near_take, 0, 2), (near_take, 1, 3), (far_take, 1, 3)))

        @pl.when(t >= 2)
        def _():
            pairs(t - 2)
            save(t - 2).start()

        return carry

    img_copy.wait()
    lax.fori_loop(0, secs + 2, each, 0)

    @pl.when(near_send)
    def _():
        for j in range(2):
            to_prev(j).wait_send()

    @pl.when(far_send)
    def _():
        to_far().wait_send()
        for p in range(1, GROUP):
            to_carrier(p).wait_send()

    for p in range(1, GROUP):
        @pl.when(carries[p])
        def _():
            onward(p).wait_send()

    @pl.when(has_down)
    def _():
        for t in range(secs):
            to_down(t).wait_send()

    @pl.when(has_up)
    def _():
        for t in range(secs):
            to_up(t).wait_send()

    @pl.when(jnp.logical_and(has_next, has_down))
    def _():
        for j in range(2):
            relay_down(j).wait_send()

    @pl.when(jnp.logical_and(has_next, has_up))
    def _():
        for j in range(2):
            relay_up(j).wait_send()

    for s in range(secs):
        save(s).wait()


def on_device(secs_axis, rows_axis, image, grid_shift, partner_step, tissue):
    secs, height, width = image.shape
    tables = [jnp.asarray(t) for t in (row_table(), col_tables(), back_col_tables(), back_row_table(), col_phases(), row_phases())]
    ints = [jnp.swapaxes(grid_shift, 2, 3), jnp.swapaxes(partner_step, 0, 1), tissue]
    dma = pltpu.SemaphoreType.DMA
    maps = pl.pallas_call(
        functools.partial(kernel, secs_axis, rows_axis),
        out_shape=jax.ShapeDtypeStruct((secs, 2, PC, SHIFTS, SHIFTS), jnp.float32),
        in_specs=[pl.BlockSpec(memory_space=pltpu.HBM)] * 10,
        out_specs=pl.BlockSpec(memory_space=pl.ANY),
        scratch_shapes=[pltpu.VMEM(t.shape, t.dtype) for t in tables]
        + [
            pltpu.VMEM((secs + 2, height, width), jnp.bfloat16),
            pltpu.VMEM((secs + 2, HALO, width), jnp.bfloat16),
            pltpu.VMEM((secs + 2, HALO, width), jnp.bfloat16),
            pltpu.VMEM((secs, 8, 4 * HALF), jnp.float32),
            pltpu.VMEM((secs, 8, 3 * HALF), jnp.float32),
            pltpu.VMEM((2, 2 * STACK, PATCH), jnp.bfloat16),
            pltpu.VMEM((2, 16, PATCH), jnp.float32),
            pltpu.VMEM((PC, PATCH, PATCH), jnp.bfloat16),
            pltpu.VMEM((secs, STACK, WIDE), jnp.bfloat16),
            pltpu.VMEM((secs, PC, 8, HALF), jnp.float32),
            pltpu.VMEM((secs + 1, STACK, WIDE), jnp.bfloat16),
            pltpu.VMEM((secs + 1, PC, 8, HALF), jnp.float32),
            pltpu.VMEM((secs, 2, PC, SHIFTS, SHIFTS), jnp.float32),
            dma((6,)),
            dma,
            dma((secs,)),
            dma((secs + 2,)),
            dma((secs + 2,)),
            dma((secs + 2,)),
            dma((secs + 2,)),
            dma((2,)),
            dma((2,)),
            dma((GROUP,)),
            dma((GROUP,)),
            pltpu.VMEM((HALF // 2, width), jnp.bfloat16),
            dma,
            dma,
        ]
        + [pltpu.SMEM(x.shape, x.dtype) for x in ints]
        + [
            dma((3,)),
        ],
        compiler_params=pltpu.CompilerParams(
            vmem_limit_bytes=40 * 1024 * 1024, collective_id=0, has_side_effects=True
        ),
        cost_estimate=pl.CostEstimate(flops=6_000_000_000, bytes_accessed=8_000_000, transcendentals=0),
    )(
        *[pltpu.with_memory_space_constraint(x, pltpu.HBM) for x in (*ints, image, *tables)]
    )
    return maps.reshape(secs, 2, 1, PC, SHIFTS * SHIFTS)


def solution(mesh):
    return jax.shard_map(
        functools.partial(on_device, mesh.shape["sec"], mesh.shape["row"]),
        mesh=mesh,
        in_specs=(
            P("sec", "row", None),
            P("sec", "row", None, None),
            P("sec", None),
            P("sec", "row", None),
        ),
        out_specs=P("sec", None, "row", None, None),
        check_vma=False,
    )
```

```python
import functools

import jax
import jax.numpy as jnp
import ml_dtypes
import numpy as np
from jax import lax
from jax.experimental import pallas as pl
from jax.experimental.pallas import tpu as pltpu
from jax.sharding import PartitionSpec as P

PC = 5
PATCH = 256
HALF = 128
REACH = 32
GROUP = 4
HALO = 96
SHIFTS = 128
WIDE = 4 * HALF
STACK = PC * HALF + 16


def angle(product):
    return 2.0 * np.pi * (product % PATCH) / PATCH


def row_table():
    k = np.arange(HALF)[:, None]
    r = np.arange(PATCH)[None, :]
    sine = np.sin(angle(k * r))
    sine[0] = 1.0 - 2.0 * (np.arange(PATCH) % 2)
    return np.concatenate([np.cos(angle(k * r)), sine], 0).astype(ml_dtypes.bfloat16)


def col_tables():
    c = np.arange(HALF)[:, None]
    out = []
    for odd in (0, 1):
        ell = 2 * np.arange(HALF)[None, :] + odd
        cos, sin = np.cos(angle(ell * c)), np.sin(angle(ell * c))
        out.append(np.block([[cos, -sin], [-sin, -cos]]))
    return np.stack(out).astype(ml_dtypes.bfloat16)


def back_col_tables():
    v = np.arange(SHIFTS)[None, :] - SHIFTS // 2
    out = []
    for odd in (0, 1):
        ell = 2 * np.arange(HALF)[:, None] + odd
        cos, sin = np.cos(angle(ell * v)), np.sin(angle(ell * v))
        out.append(np.block([[cos, sin], [-sin, cos]]))
    return np.stack(out).astype(ml_dtypes.bfloat16)


def back_row_table():
    u = np.arange(SHIFTS)[:, None] - SHIFTS // 2
    k = np.arange(HALF)[None, :]
    weight = np.where(k == 0, 1.0, 2.0)
    sine = -weight * np.sin(angle(u * k))
    sine[:, 0] = 1.0 - 2.0 * (u[:, 0] % 2)
    return np.concatenate([weight * np.cos(angle(u * k)), sine], 1).astype(np.float32)


def phase_table(frequencies):
    s = np.arange(2 * REACH + 1)[:, None] - REACH
    parts = np.concatenate([f(angle(ell[None, :] * s)) for f, ell in frequencies], 1)
    high = parts.astype(ml_dtypes.bfloat16)
    low = (parts - high.astype(np.float64)).astype(ml_dtypes.bfloat16)
    out = np.zeros((PATCH, parts.shape[1]), ml_dtypes.bfloat16)
    out[: len(s)], out[HALF : HALF + len(s)] = high, low
    return out


def col_phases():
    even = 2 * np.arange(HALF)
    return phase_table([(f, ell) for f in (np.cos, np.sin) for ell in (even, even + 1)])


def row_phases():
    k = np.arange(HALF)
    return phase_table([(np.cos, k), (np.cos, np.where(k == 0, HALF, k)), (np.sin, k)])


def dot(a, b):
    return jnp.dot(a, b, preferred_element_type=jnp.float32)


def folded(own, above, below, tile, start):
    lanes = slice(tile * HALF, (tile + 1) * HALF)
    if start is None:
        return jnp.concatenate([below[0:64, lanes], above[32:96, lanes], own[:, lanes]], 0)
    low = above[0:64, lanes]
    high = below[32:96, lanes]
    rows = lax.broadcasted_iota(jnp.int32, (64, HALF), 0) + 32
    mixed = jnp.where(rows >= start, low.astype(jnp.float32), high.astype(jnp.float32)).astype(jnp.bfloat16)
    return jnp.concatenate([below[0:32, lanes], mixed, above[64:96, lanes], own[:, lanes]], 0)


def window(own, above, below, c, row_start, col_start):
    right = folded(own, above, below, c, row_start)
    zero = jnp.zeros((PATCH, HALF), jnp.bfloat16)
    far = folded(own, above, below, c - 1, row_start) if c > 0 else zero
    near = folded(own, above, below, c + 1, row_start) if c < PC - 1 else zero
    lanes = lax.broadcasted_iota(jnp.int32, (PATCH, HALF), 1)
    left = jnp.where(lanes >= col_start, far.astype(jnp.float32), near.astype(jnp.float32)).astype(jnp.bfloat16)
    return jnp.concatenate([left, right], 1)


def forward(jobs, tab_row, tab_col, lhs, nyq):
    first = lax.broadcasted_iota(jnp.int32, (8, HALF), 0) == 0

    def top(block):
        return block[0:8], block[8:]

    for i, (own, above, below, starts, phases, spec, rstd) in enumerate(jobs):
        base = i * STACK
        for c in range(PC):
            x = window(own, above, below, c, *starts[c])
            part = dot(tab_row[...], x)
            lo, hi = part[:, :HALF], part[:, HALF:]
            even, odd = lo + hi, lo - hi
            ce, se, co, so = even[:HALF], even[HALF:], odd[:HALF], odd[HALF:]
            head, tail = top(ce)
            centre = jnp.mean(head[0:1], axis=1, keepdims=True)
            head = jnp.where(first, head - centre, head)
            ce = jnp.concatenate([head, tail], 0)
            square = jnp.zeros((8, HALF), jnp.float32)
            edge = jnp.zeros((8, HALF), jnp.float32)
            for block in (ce, se, co, so):
                sq = block * block
                square = square + jnp.sum(sq.reshape(HALF // 8, 8, HALF), axis=0)
                edge = edge + sq[0:8]
            total = 2.0 * square - jnp.where(first, edge, 0.0)
            var = jnp.sum(jnp.sum(total, axis=0, keepdims=True), axis=1, keepdims=True) * (
                HALF / float(PATCH**4)
            )
            rstd[c] = jnp.broadcast_to(lax.rsqrt(var + 1e-05), (8, HALF))
            he, te = top(se)
            ho, to = top(so)
            nyq[i, c : c + 1, :HALF] = he[0:1]
            nyq[i, c : c + 1, HALF:] = ho[0:1]
            se = jnp.concatenate([jnp.where(first, 0.0, he), te], 0)
            so = jnp.concatenate([jnp.where(first, 0.0, ho), to], 0)
            rows = slice(base + c * HALF, base + (c + 1) * HALF)
            lhs[0, rows] = jnp.concatenate([ce, se], 1).astype(jnp.bfloat16)
            lhs[1, rows] = jnp.concatenate([co, so], 1).astype(jnp.bfloat16)
        rows = slice(base + PC * HALF, base + STACK)
        zero = jnp.zeros((16, HALF), jnp.bfloat16)
        lhs[0, rows] = jnp.concatenate([nyq[i, :, :HALF].astype(jnp.bfloat16), zero], 1)
        lhs[1, rows] = jnp.concatenate([nyq[i, :, HALF:].astype(jnp.bfloat16), zero], 1)
    for q in range(2):
        f = dot(lhs[q, : len(jobs) * STACK], tab_col[q])
        for i, (_, _, _, _, phases, spec, _) in enumerate(jobs):
            block = f[i * STACK : (i + 1) * STACK]
            if phases is None:
                spec[:, q * PATCH : (q + 1) * PATCH] = block.astype(jnp.bfloat16)
                continue
            cos = [p[:, q * HALF : (q + 1) * HALF] for p in phases]
            sin = [p[:, (q + 2) * HALF : (q + 3) * HALF] for p in phases]
            spare = jnp.zeros((16 - PC, HALF), jnp.float32)
            cos.append(jnp.concatenate(cos + [spare], 0))
            sin.append(jnp.concatenate(sin + [spare], 0))
            for c in range(PC + 1):
                rows = slice(c * HALF, min((c + 1) * HALF, STACK))
                re, im = block[rows, :HALF], block[rows, HALF:]
                turned = jnp.concatenate([re * cos[c] - im * sin[c], re * sin[c] + im * cos[c]], 1)
                spec[rows, q * PATCH : (q + 1) * PATCH] = turned.astype(jnp.bfloat16)


def crossed(a, b):
    out = []
    for base in (0, 2 * HALF):
        re, im = slice(base, base + HALF), slice(base + HALF, base + 2 * HALF)
        are, aim = a[:, re], a[:, im]
        bre, bim = b[:, re], b[:, im]
        g = jnp.concatenate([are * bre + aim * bim, are * bim - aim * bre], 1)
        out.append(g)
    return out


def remote(src, dst, send, recv, where):
    return pltpu.make_async_remote_copy(
        src_ref=src, dst_ref=dst, send_sem=send, recv_sem=recv, device_id=where, device_id_type=pl.DeviceIdType.MESH
    )


def kernel(
    secs_axis, rows_axis,
    shift_hbm, step_hbm, tissue_hbm, img, *refs,
):
    tables, refs = refs[:6], refs[6:]
    out, refs = refs[0], refs[1:]
    tabs, refs = refs[:6], refs[6:]
    (strip, above, below, pcol, prow, lhs, nyq, right, own_spec, own_rstd, spec, rstd, stage,
     tab_sem, img_sem, out_sem, up_send, up_recv, down_send, down_recv, sec_send, sec_recv,
     part_send, part_recv, transit, via_send, via_recv, shift_ref, step_ref, tissue_ref, int_sem) = refs
    tab_row, tab_col, tab_bcol, tab_brow, tab_pcol, tab_prow = tabs
    secs = own_spec.shape[0]
    sec, row = lax.axis_index("sec"), lax.axis_index("row")
    has_up, has_down = row > 0, row < rows_axis - 1
    has_prev, has_next = sec > 0, sec < secs_axis - 1
    up, down, prev, following = (sec, row - 1), (sec, row + 1), (sec - 1, row), (sec + 1, row)
    place = lax.rem(sec, GROUP)
    far_send = jnp.logical_and(place == 0, has_prev)
    far_take = jnp.logical_and(place == GROUP - 1, has_next)
    carries = [jnp.logical_and(place == p, sec > p) for p in range(GROUP)]
    sides = [(has_up, up), (has_down, down), (has_prev, prev), (has_next, following)]
    for p in range(1, GROUP):
        if p > 1:
            sides += [(far_send, (sec + p, row)), (carries[p], (sec - p, row))]
        sides += [(far_take, (sec + p + 1, row)), (carries[p], (sec - p - 1, row))]

    barrier = pltpu.get_barrier_semaphore()
    for there, where in sides:
        @pl.when(there)
        def _():
            pl.semaphore_signal(barrier, inc=1, device_id=where, device_id_type=pl.DeviceIdType.MESH)

    img_copy = pltpu.make_async_copy(img, strip.at[0:secs], img_sem)
    img_copy.start()
    loads = [pltpu.make_async_copy(t, v, tab_sem.at[i]) for i, (t, v) in enumerate(zip(tables, tabs))]
    ints = ((shift_hbm, shift_ref), (step_hbm, step_ref), (tissue_hbm, tissue_ref))
    loads += [pltpu.make_async_copy(h, v, int_sem.at[i]) for i, (h, v) in enumerate(ints)]
    for load in loads:
        load.start()

    pl.semaphore_wait(barrier, sum(there.astype(jnp.int32) for there, _ in sides))

    def to_prev(j):
        return remote(img.at[j], strip.at[secs + j], sec_send.at[j], sec_recv.at[j], prev)

    def to_down(t):
        return remote(img.at[t, HALF - HALO : HALF], above.at[t], down_send.at[t], down_recv.at[t], down)

    def to_up(t):
        return remote(img.at[t, 0:HALO], below.at[t], up_send.at[t], up_recv.at[t], up)

    def relay_down(j):
        t = secs + j
        return remote(strip.at[t, HALF // 2 : HALF], above.at[t, HALO - HALF // 2 : HALO], down_send.at[t], down_recv.at[t], down)

    def relay_up(j):
        t = secs + j
        return remote(strip.at[t, 0 : HALF // 2], below.at[t, 0 : HALF // 2], up_send.at[t], up_recv.at[t], up)

    def part(p):
        return p // 2, slice(p % 2 * (HALF // 2), (p % 2 + 1) * (HALF // 2))

    def to_far():
        return remote(img.at[0, : HALF // 2], strip.at[secs, : HALF // 2], part_send.at[0], part_recv.at[0], prev)

    def to_carrier(p):
        j, rows = part(p)
        return remote(img.at[j, rows], transit, part_send.at[p], via_recv, (sec + p, row))

    def onward(p):
        j, rows = part(p)
        return remote(transit, strip.at[secs + j, rows], via_send, part_recv.at[p], (sec - p - 1, row))

    def arrival(p):
        j, rows = part(p)
        return remote(transit, strip.at[secs + j, rows], via_send, part_recv.at[p], (sec + p + 1, row))

    def start_halo(t):
        @pl.when(has_down)
        def _():
            to_down(t).start()

        @pl.when(has_up)
        def _():
            to_up(t).start()

    start_halo(0)

    near_send = jnp.logical_and(has_prev, place > 0)
    near_take = jnp.logical_and(has_next, place < GROUP - 1)

    @pl.when(far_send)
    def _():
        for p in range(1, GROUP):
            to_carrier(p).start()
        to_far().start()

    @pl.when(near_send)
    def _():
        to_prev(0).start()

    for t in range(1, secs - 1):
        start_halo(t)

    @pl.when(near_send)
    def _():
        to_prev(1).start()

    @pl.when(jnp.logical_not(jnp.logical_or(jnp.logical_or(carries[1], carries[2]), carries[3])))
    def _():
        start_halo(secs - 1)

    @pl.when(jnp.logical_not(has_up))
    def _():
        above[...] = jnp.zeros_like(above)

    @pl.when(jnp.logical_not(has_down))
    def _():
        below[...] = jnp.zeros_like(below)

    @pl.when(jnp.logical_not(has_next))
    def _():
        strip[secs:] = jnp.zeros((2, HALF, strip.shape[2]), jnp.bfloat16)
        above[secs:] = jnp.zeros((2, HALO, strip.shape[2]), jnp.bfloat16)
        below[secs:] = jnp.zeros((2, HALO, strip.shape[2]), jnp.bfloat16)

    nyq[...] = jnp.zeros_like(nyq)
    for load in loads:
        load.wait()

    rows = lax.broadcasted_iota(jnp.int32, (8 * secs, PATCH), 0)
    lanes = lax.broadcasted_iota(jnp.int32, (8 * secs, PATCH), 1)
    for axis, table, phase in ((0, tab_prow, prow), (1, tab_pcol, pcol)):
        wanted = jnp.zeros_like(lanes)
        for s in range(secs):
            for c in range(PC):
                wanted = jnp.where(rows == 8 * s + c, shift_ref[s, 0, axis, c] + REACH, wanted)
        chosen = jnp.logical_or(lanes == wanted, lanes == wanted + HALF)
        picked = dot(chosen.astype(jnp.float32).astype(jnp.bfloat16), table[...])
        phase[...] = picked.reshape(secs, 8, picked.shape[1])

    def plain(t):
        return (strip.at[t], above.at[t], below.at[t], [(None, 64)] * PC, None, spec.at[t - 1], rstd.at[t - 1])

    def own(s):
        starts = [(shift_ref[s, 0, 0, c] + 64, shift_ref[s, 0, 1, c] + 64) for c in range(PC)]
        phases = [pcol[s, c : c + 1] for c in range(PC)]
        return (strip.at[s], above.at[s], below.at[s], starts, phases, own_spec.at[s], own_rstd.at[s])

    def spectra(*jobs):
        forward(jobs, tab_row, tab_col, lhs, nyq)

    first = lax.broadcasted_iota(jnp.int32, (8, HALF), 0) == 0

    def pairs(s):
        for part in range(2):
            ge, go = crossed(own_spec[s], spec[s + part])
            g = dot(ge, tab_bcol[0]) + dot(go, tab_bcol[1])
            lanes = slice(part * HALF, (part + 1) * HALF)
            for c in range(PC):
                block = g[c * HALF : (c + 1) * HALF]
                edge = jnp.broadcast_to(g[PC * HALF + c : PC * HALF + c + 1, :HALF], (8, HALF))
                im = block[:, HALF:]
                im = jnp.concatenate([jnp.where(first, edge, im[0:8]), im[8:]], 0)
                right[c, :HALF, lanes] = block[:, :HALF].astype(jnp.bfloat16)
                right[c, HALF:, lanes] = im.astype(jnp.bfloat16)
        for c in range(PC):
            turn = prow[s, c : c + 1]
            cos, cos_edge, sin = turn[:, :HALF], turn[:, HALF : 2 * HALF], turn[:, 2 * HALF :]
            bc, bs = tab_brow[:, :HALF], tab_brow[:, HALF:]
            left = jnp.concatenate([bc * cos - bs * sin, bs * cos_edge + bc * sin], 1).astype(jnp.bfloat16)
            maps = dot(left, right[c])
            weight = tissue_ref[s, 0, c].astype(jnp.float32) / float(PATCH * PATCH)
            base = own_rstd[s, c] * weight
            near = maps[:, :HALF].reshape(SHIFTS // 8, 8, HALF)
            far = maps[:, HALF:].reshape(SHIFTS // 8, 8, HALF)
            for slot in range(2):
                step = step_ref[slot, s].astype(jnp.float32)
                by_near = base * rstd[s, c] * (2.0 - step)
                by_far = base * rstd[s + 1, c] * (step - 1.0)
                stage[s, slot, c] = (near * by_near[None] + far * by_far[None]).reshape(SHIFTS, SHIFTS)

    def save(s):
        return pltpu.make_async_copy(stage.at[s], out.at[s], out_sem.at[s])

    def pass_on(j):
        @pl.when(has_up)
        def _():
            relay_up(j).start()

        @pl.when(has_down)
        def _():
            relay_down(j).start()

    def wait_halo(t):
        @pl.when(has_up)
        def _():
            to_down(t).wait_recv()

        @pl.when(has_down)
        def _():
            to_up(t).wait_recv()

    def far_pass(j):
        arrival(2 * j).wait_recv()

        @pl.when(has_up)
        def _():
            relay_up(j).start()

        arrival(2 * j + 1).wait_recv()

        @pl.when(has_down)
        def _():
            relay_down(j).start()

    def near_pass(j):
        to_prev(j).wait_recv()
        pass_on(j)

    def early(t, carry):
        @pl.when(jnp.logical_and(far_take, t == 3))
        def _():
            far_pass(0)

        wait_halo(t)
        spectra(own(t), plain(t))

        @pl.when(t >= 2)
        def _():
            @pl.when(near_take)
            def _():
                near_pass(t - 2)

            @pl.when(jnp.logical_and(far_take, t == 3))
            def _():
                far_pass(1)

            pairs(t - 2)
            save(t - 2).start()

        return carry

    def late(t, carry):
        @pl.when(has_next)
        def _():
            @pl.when(has_up)
            def _():
                relay_down(t - secs).wait_recv()

            @pl.when(has_down)
            def _():
                relay_up(t - secs).wait_recv()

        spectra(plain(t))
        pairs(t - 2)
        save(t - 2).start()
        return carry

    for p in range(1, GROUP):
        @pl.when(carries[p])
        def _():
            to_carrier(p).wait_recv()
            onward(p).start()
            start_halo(secs - 1)

    img_copy.wait()
    wait_halo(0)
    spectra(own(0))
    lax.fori_loop(1, secs, early, 0)
    lax.fori_loop(secs, secs + 2, late, 0)

    @pl.when(near_send)
    def _():
        for j in range(2):
            to_prev(j).wait_send()

    @pl.when(far_send)
    def _():
        to_far().wait_send()
        for p in range(1, GROUP):
            to_carrier(p).wait_send()

    for p in range(1, GROUP):
        @pl.when(carries[p])
        def _():
            onward(p).wait_send()

    @pl.when(has_down)
    def _():
        for t in range(secs):
            to_down(t).wait_send()

    @pl.when(has_up)
    def _():
        for t in range(secs):
            to_up(t).wait_send()

    @pl.when(jnp.logical_and(has_next, has_down))
    def _():
        for j in range(2):
            relay_down(j).wait_send()

    @pl.when(jnp.logical_and(has_next, has_up))
    def _():
        for j in range(2):
            relay_up(j).wait_send()

    for s in range(secs):
        save(s).wait()


def on_device(secs_axis, rows_axis, image, grid_shift, partner_step, tissue):
    secs, height, width = image.shape
    tables = [jnp.asarray(t) for t in (row_table(), col_tables(), back_col_tables(), back_row_table(), col_phases(), row_phases())]
    ints = [jnp.swapaxes(grid_shift, 2, 3), jnp.swapaxes(partner_step, 0, 1), tissue]
    dma = pltpu.SemaphoreType.DMA
    maps = pl.pallas_call(
        functools.partial(kernel, secs_axis, rows_axis),
        out_shape=jax.ShapeDtypeStruct((secs, 2, PC, SHIFTS, SHIFTS), jnp.float32),
        in_specs=[pl.BlockSpec(memory_space=pltpu.HBM)] * 10,
        out_specs=pl.BlockSpec(memory_space=pl.ANY),
        scratch_shapes=[pltpu.VMEM(t.shape, t.dtype) for t in tables]
        + [
            pltpu.VMEM((secs + 2, height, width), jnp.bfloat16),
            pltpu.VMEM((secs + 2, HALO, width), jnp.bfloat16),
            pltpu.VMEM((secs + 2, HALO, width), jnp.bfloat16),
            pltpu.VMEM((secs, 8, 4 * HALF), jnp.float32),
            pltpu.VMEM((secs, 8, 3 * HALF), jnp.float32),
            pltpu.VMEM((2, 2 * STACK, PATCH), jnp.bfloat16),
            pltpu.VMEM((2, 16, PATCH), jnp.float32),
            pltpu.VMEM((PC, PATCH, PATCH), jnp.bfloat16),
            pltpu.VMEM((secs, STACK, WIDE), jnp.bfloat16),
            pltpu.VMEM((secs, PC, 8, HALF), jnp.float32),
            pltpu.VMEM((secs + 1, STACK, WIDE), jnp.bfloat16),
            pltpu.VMEM((secs + 1, PC, 8, HALF), jnp.float32),
            pltpu.VMEM((secs, 2, PC, SHIFTS, SHIFTS), jnp.float32),
            dma((6,)),
            dma,
            dma((secs,)),
            dma((secs + 2,)),
            dma((secs + 2,)),
            dma((secs + 2,)),
            dma((secs + 2,)),
            dma((2,)),
            dma((2,)),
            dma((GROUP,)),
            dma((GROUP,)),
            pltpu.VMEM((HALF // 2, width), jnp.bfloat16),
            dma,
            dma,
        ]
        + [pltpu.SMEM(x.shape, x.dtype) for x in ints]
        + [
            dma((3,)),
        ],
        compiler_params=pltpu.CompilerParams(
            vmem_limit_bytes=40 * 1024 * 1024, collective_id=0, has_side_effects=True
        ),
        cost_estimate=pl.CostEstimate(flops=6_000_000_000, bytes_accessed=8_000_000, transcendentals=0),
    )(
        *[pltpu.with_memory_space_constraint(x, pltpu.HBM) for x in (*ints, image, *tables)]
    )
    return maps.reshape(secs, 2, 1, PC, SHIFTS * SHIFTS)


def solution(mesh):
    return jax.shard_map(
        functools.partial(on_device, mesh.shape["sec"], mesh.shape["row"]),
        mesh=mesh,
        in_specs=(
            P("sec", "row", None),
            P("sec", "row", None, None),
            P("sec", None),
            P("sec", "row", None),
        ),
        out_specs=P("sec", None, "row", None, None),
        check_vma=False,
    )
```

```python
import functools

import jax
import jax.numpy as jnp
import ml_dtypes
import numpy as np
from jax import lax
from jax.experimental import pallas as pl
from jax.experimental.pallas import tpu as pltpu
from jax.sharding import PartitionSpec as P

PC = 5
PATCH = 256
HALF = 128
REACH = 32
GROUP = 4
HALO = 96
SHIFTS = 128
WIDE = 4 * HALF
STACK = PC * HALF + 16


def angle(product):
    return 2.0 * np.pi * (product % PATCH) / PATCH


def row_table():
    k = np.arange(HALF)[:, None]
    r = np.arange(PATCH)[None, :]
    sine = np.sin(angle(k * r))
    sine[0] = 1.0 - 2.0 * (np.arange(PATCH) % 2)
    return np.concatenate([np.cos(angle(k * r)), sine], 0).astype(ml_dtypes.bfloat16)


def col_tables():
    c = np.arange(HALF)[:, None]
    out = []
    for odd in (0, 1):
        ell = 2 * np.arange(HALF)[None, :] + odd
        cos, sin = np.cos(angle(ell * c)), np.sin(angle(ell * c))
        out.append(np.block([[cos, -sin], [-sin, -cos]]))
    return np.stack(out).astype(ml_dtypes.bfloat16)


def back_col_tables():
    v = np.arange(SHIFTS)[None, :] - SHIFTS // 2
    out = []
    for odd in (0, 1):
        ell = 2 * np.arange(HALF)[:, None] + odd
        cos, sin = np.cos(angle(ell * v)), np.sin(angle(ell * v))
        out.append(np.block([[cos, sin], [-sin, cos]]))
    return np.stack(out).astype(ml_dtypes.bfloat16)


def back_row_table():
    u = np.arange(SHIFTS)[:, None] - SHIFTS // 2
    k = np.arange(HALF)[None, :]
    weight = np.where(k == 0, 1.0, 2.0)
    sine = -weight * np.sin(angle(u * k))
    sine[:, 0] = 1.0 - 2.0 * (u[:, 0] % 2)
    return np.concatenate([weight * np.cos(angle(u * k)), sine], 1).astype(np.float32)


def phase_table(frequencies):
    s = np.arange(2 * REACH + 1)[:, None] - REACH
    parts = np.concatenate([f(angle(ell[None, :] * s)) for f, ell in frequencies], 1)
    high = parts.astype(ml_dtypes.bfloat16)
    low = (parts - high.astype(np.float64)).astype(ml_dtypes.bfloat16)
    out = np.zeros((PATCH, parts.shape[1]), ml_dtypes.bfloat16)
    out[: len(s)], out[HALF : HALF + len(s)] = high, low
    return out


def col_phases():
    even = 2 * np.arange(HALF)
    return phase_table([(f, ell) for f in (np.cos, np.sin) for ell in (even, even + 1)])


def row_phases():
    k = np.arange(HALF)
    return phase_table([(np.cos, k), (np.cos, np.where(k == 0, HALF, k)), (np.sin, k)])


def dot(a, b):
    return jnp.dot(a, b, preferred_element_type=jnp.float32)


def folded(own, above, below, tile, start):
    lanes = slice(tile * HALF, (tile + 1) * HALF)
    if start is None:
        return jnp.concatenate([below[0:64, lanes], above[32:96, lanes], own[:, lanes]], 0)
    low = above[0:64, lanes]
    high = below[32:96, lanes]
    rows = lax.broadcasted_iota(jnp.int32, (64, HALF), 0) + 32
    mixed = jnp.where(rows >= start, low.astype(jnp.float32), high.astype(jnp.float32)).astype(jnp.bfloat16)
    return jnp.concatenate([below[0:32, lanes], mixed, above[64:96, lanes], own[:, lanes]], 0)


def window(own, above, below, c, row_start, col_start):
    right = folded(own, above, below, c, row_start)
    zero = jnp.zeros((PATCH, HALF), jnp.bfloat16)
    far = folded(own, above, below, c - 1, row_start) if c > 0 else zero
    near = folded(own, above, below, c + 1, row_start) if c < PC - 1 else zero
    lanes = lax.broadcasted_iota(jnp.int32, (PATCH, HALF), 1)
    left = jnp.where(lanes >= col_start, far.astype(jnp.float32), near.astype(jnp.float32)).astype(jnp.bfloat16)
    return jnp.concatenate([left, right], 1)


def forward(jobs, tab_row, tab_col, lhs, nyq):
    first = lax.broadcasted_iota(jnp.int32, (8, HALF), 0) == 0

    def top(block):
        return block[0:8], block[8:]

    for i, (own, above, below, starts, phases, spec, rstd) in enumerate(jobs):
        base = i * STACK
        for c in range(PC):
            x = window(own, above, below, c, *starts[c])
            part = dot(tab_row[...], x)
            lo, hi = part[:, :HALF], part[:, HALF:]
            even, odd = lo + hi, lo - hi
            ce, se, co, so = even[:HALF], even[HALF:], odd[:HALF], odd[HALF:]
            head, tail = top(ce)
            centre = jnp.mean(head[0:1], axis=1, keepdims=True)
            head = jnp.where(first, head - centre, head)
            ce = jnp.concatenate([head, tail], 0)
            square = jnp.zeros((8, HALF), jnp.float32)
            edge = jnp.zeros((8, HALF), jnp.float32)
            for block in (ce, se, co, so):
                sq = block * block
                square = square + jnp.sum(sq.reshape(HALF // 8, 8, HALF), axis=0)
                edge = edge + sq[0:8]
            total = 2.0 * square - jnp.where(first, edge, 0.0)
            var = jnp.sum(jnp.sum(total, axis=0, keepdims=True), axis=1, keepdims=True) * (
                HALF / float(PATCH**4)
            )
            rstd[c] = jnp.broadcast_to(lax.rsqrt(var + 1e-05), (8, HALF))
            he, te = top(se)
            ho, to = top(so)
            nyq[i, c : c + 1, :HALF] = he[0:1]
            nyq[i, c : c + 1, HALF:] = ho[0:1]
            se = jnp.concatenate([jnp.where(first, 0.0, he), te], 0)
            so = jnp.concatenate([jnp.where(first, 0.0, ho), to], 0)
            rows = slice(base + c * HALF, base + (c + 1) * HALF)
            lhs[0, rows] = jnp.concatenate([ce, se], 1).astype(jnp.bfloat16)
            lhs[1, rows] = jnp.concatenate([co, so], 1).astype(jnp.bfloat16)
        rows = slice(base + PC * HALF, base + STACK)
        zero = jnp.zeros((16, HALF), jnp.bfloat16)
        lhs[0, rows] = jnp.concatenate([nyq[i, :, :HALF].astype(jnp.bfloat16), zero], 1)
        lhs[1, rows] = jnp.concatenate([nyq[i, :, HALF:].astype(jnp.bfloat16), zero], 1)
    for q in range(2):
        f = dot(lhs[q, : len(jobs) * STACK], tab_col[q])
        for i, (_, _, _, _, phases, spec, _) in enumerate(jobs):
            block = f[i * STACK : (i + 1) * STACK]
            if phases is None:
                spec[:, q * PATCH : (q + 1) * PATCH] = block.astype(jnp.bfloat16)
                continue
            cos = [p[:, q * HALF : (q + 1) * HALF] for p in phases]
            sin = [p[:, (q + 2) * HALF : (q + 3) * HALF] for p in phases]
            spare = jnp.zeros((16 - PC, HALF), jnp.float32)
            cos.append(jnp.concatenate(cos + [spare], 0))
            sin.append(jnp.concatenate(sin + [spare], 0))
            for c in range(PC + 1):
                rows = slice(c * HALF, min((c + 1) * HALF, STACK))
                re, im = block[rows, :HALF], block[rows, HALF:]
                turned = jnp.concatenate([re * cos[c] - im * sin[c], re * sin[c] + im * cos[c]], 1)
                spec[rows, q * PATCH : (q + 1) * PATCH] = turned.astype(jnp.bfloat16)


def crossed(a, b):
    out = []
    for base in (0, 2 * HALF):
        re, im = slice(base, base + HALF), slice(base + HALF, base + 2 * HALF)
        are, aim = a[:, re], a[:, im]
        bre, bim = b[:, re], b[:, im]
        g = jnp.concatenate([are * bre + aim * bim, are * bim - aim * bre], 1)
        out.append(g)
    return out


def remote(src, dst, send, recv, where):
    return pltpu.make_async_remote_copy(
        src_ref=src, dst_ref=dst, send_sem=send, recv_sem=recv, device_id=where, device_id_type=pl.DeviceIdType.MESH
    )


def kernel(
    secs_axis, rows_axis,
    shift_hbm, step_hbm, tissue_hbm, img, *refs,
):
    tables, refs = refs[:6], refs[6:]
    out, refs = refs[0], refs[1:]
    tabs, refs = refs[:6], refs[6:]
    (strip, above, below, pcol, prow, lhs, nyq, right, own_spec, own_rstd, spec, rstd, stage,
     tab_sem, img_sem, out_sem, up_send, up_recv, down_send, down_recv, sec_send, sec_recv,
     part_send, part_recv, transit, via_send, via_recv, ready, shift_ref, step_ref, tissue_ref, int_sem) = refs
    tab_row, tab_col, tab_bcol, tab_brow, tab_pcol, tab_prow = tabs
    secs = own_spec.shape[0]
    sec, row = lax.axis_index("sec"), lax.axis_index("row")
    has_up, has_down = row > 0, row < rows_axis - 1
    has_prev, has_next = sec > 0, sec < secs_axis - 1
    up, down, prev, following = (sec, row - 1), (sec, row + 1), (sec - 1, row), (sec + 1, row)
    place = lax.rem(sec, GROUP)
    far_send = jnp.logical_and(place == 0, has_prev)
    far_take = jnp.logical_and(place == GROUP - 1, has_next)
    carries = [jnp.logical_and(place == p, sec > p) for p in range(GROUP)]
    near_send = jnp.logical_and(has_prev, place > 0)
    near_take = jnp.logical_and(has_next, place < GROUP - 1)
    sides = [(has_up, up), (has_down, down), (near_send, prev), (near_take, following)]
    for p in range(2, GROUP):
        sides += [(far_send, (sec + p, row)), (carries[p], (sec - p, row))]
    greeted = [(far_send, prev)] + [(carries[p], (sec - p - 1, row)) for p in range(1, GROUP)]
    expected = sum(there.astype(jnp.int32) for there, _ in sides) + GROUP * far_take.astype(jnp.int32)

    barrier = pltpu.get_barrier_semaphore()
    for there, where in sides + greeted:
        @pl.when(there)
        def _():
            pl.semaphore_signal(barrier, inc=1, device_id=where, device_id_type=pl.DeviceIdType.MESH)

    img_copy = pltpu.make_async_copy(img, strip.at[0:secs], img_sem)
    img_copy.start()
    loads = [pltpu.make_async_copy(t, v, tab_sem.at[i]) for i, (t, v) in enumerate(zip(tables, tabs))]
    ints = ((shift_hbm, shift_ref), (step_hbm, step_ref), (tissue_hbm, tissue_ref))
    loads += [pltpu.make_async_copy(h, v, int_sem.at[i]) for i, (h, v) in enumerate(ints)]
    for load in loads:
        load.start()

    pl.semaphore_wait(barrier, expected)

    @pl.when(far_take)
    def _():
        for p in range(GROUP):
            pl.semaphore_signal(ready, inc=1, device_id=(sec + p + 1, row), device_id_type=pl.DeviceIdType.MESH)

    def to_prev(j):
        return remote(img.at[j], strip.at[secs + j], sec_send.at[j], sec_recv.at[j], prev)

    def to_down(t):
        return remote(img.at[t, HALF - HALO : HALF], above.at[t], down_send.at[t], down_recv.at[t], down)

    def to_up(t):
        return remote(img.at[t, 0:HALO], below.at[t], up_send.at[t], up_recv.at[t], up)

    def relay_down(j):
        t = secs + j
        return remote(strip.at[t, HALF // 2 : HALF], above.at[t, HALO - HALF // 2 : HALO], down_send.at[t], down_recv.at[t], down)

    def relay_up(j):
        t = secs + j
        return remote(strip.at[t, 0 : HALF // 2], below.at[t, 0 : HALF // 2], up_send.at[t], up_recv.at[t], up)

    def part(p):
        return p // 2, slice(p % 2 * (HALF // 2), (p % 2 + 1) * (HALF // 2))

    def to_far():
        return remote(img.at[0, : HALF // 2], strip.at[secs, : HALF // 2], part_send.at[0], part_recv.at[0], prev)

    def to_carrier(p):
        j, rows = part(p)
        return remote(img.at[j, rows], transit, part_send.at[p], via_recv, (sec + p, row))

    def onward(p):
        j, rows = part(p)
        return remote(transit, strip.at[secs + j, rows], via_send, part_recv.at[p], (sec - p - 1, row))

    def arrival(p):
        j, rows = part(p)
        return remote(transit, strip.at[secs + j, rows], via_send, part_recv.at[p], (sec + p + 1, row))

    def start_halo(t):
        @pl.when(has_down)
        def _():
            to_down(t).start()

        @pl.when(has_up)
        def _():
            to_up(t).start()

    start_halo(0)

    @pl.when(far_send)
    def _():
        for p in range(1, GROUP):
            to_carrier(p).start()

    @pl.when(near_send)
    def _():
        to_prev(0).start()

    for t in range(1, secs - 1):
        start_halo(t)

    @pl.when(near_send)
    def _():
        to_prev(1).start()

    @pl.when(jnp.logical_not(jnp.logical_or(jnp.logical_or(carries[1], carries[2]), carries[3])))
    def _():
        start_halo(secs - 1)

    @pl.when(far_send)
    def _():
        pl.semaphore_wait(ready, 1)
        to_far().start()

    @pl.when(jnp.logical_not(has_up))
    def _():
        above[...] = jnp.zeros_like(above)

    @pl.when(jnp.logical_not(has_down))
    def _():
        below[...] = jnp.zeros_like(below)

    @pl.when(jnp.logical_not(has_next))
    def _():
        strip[secs:] = jnp.zeros((2, HALF, strip.shape[2]), jnp.bfloat16)
        above[secs:] = jnp.zeros((2, HALO, strip.shape[2]), jnp.bfloat16)
        below[secs:] = jnp.zeros((2, HALO, strip.shape[2]), jnp.bfloat16)

    nyq[...] = jnp.zeros_like(nyq)
    for load in loads:
        load.wait()

    rows = lax.broadcasted_iota(jnp.int32, (8 * secs, PATCH), 0)
    lanes = lax.broadcasted_iota(jnp.int32, (8 * secs, PATCH), 1)
    for axis, table, phase in ((0, tab_prow, prow), (1, tab_pcol, pcol)):
        wanted = jnp.zeros_like(lanes)
        for s in range(secs):
            for c in range(PC):
                wanted = jnp.where(rows == 8 * s + c, shift_ref[s, 0, axis, c] + REACH, wanted)
        chosen = jnp.logical_or(lanes == wanted, lanes == wanted + HALF)
        picked = dot(chosen.astype(jnp.float32).astype(jnp.bfloat16), table[...])
        phase[...] = picked.reshape(secs, 8, picked.shape[1])

    def plain(t):
        return (strip.at[t], above.at[t], below.at[t], [(None, 64)] * PC, None, spec.at[t - 1], rstd.at[t - 1])

    def own(s):
        starts = [(shift_ref[s, 0, 0, c] + 64, shift_ref[s, 0, 1, c] + 64) for c in range(PC)]
        phases = [pcol[s, c : c + 1] for c in range(PC)]
        return (strip.at[s], above.at[s], below.at[s], starts, phases, own_spec.at[s], own_rstd.at[s])

    def spectra(*jobs):
        forward(jobs, tab_row, tab_col, lhs, nyq)

    first = lax.broadcasted_iota(jnp.int32, (8, HALF), 0) == 0

    def pairs(s):
        for part in range(2):
            ge, go = crossed(own_spec[s], spec[s + part])
            g = dot(ge, tab_bcol[0]) + dot(go, tab_bcol[1])
            lanes = slice(part * HALF, (part + 1) * HALF)
            for c in range(PC):
                block = g[c * HALF : (c + 1) * HALF]
                edge = jnp.broadcast_to(g[PC * HALF + c : PC * HALF + c + 1, :HALF], (8, HALF))
                im = block[:, HALF:]
                im = jnp.concatenate([jnp.where(first, edge, im[0:8]), im[8:]], 0)
                right[c, :HALF, lanes] = block[:, :HALF].astype(jnp.bfloat16)
                right[c, HALF:, lanes] = im.astype(jnp.bfloat16)
        for c in range(PC):
            turn = prow[s, c : c + 1]
            cos, cos_edge, sin = turn[:, :HALF], turn[:, HALF : 2 * HALF], turn[:, 2 * HALF :]
            bc, bs = tab_brow[:, :HALF], tab_brow[:, HALF:]
            left = jnp.concatenate([bc * cos - bs * sin, bs * cos_edge + bc * sin], 1).astype(jnp.bfloat16)
            maps = dot(left, right[c])
            weight = tissue_ref[s, 0, c].astype(jnp.float32) / float(PATCH * PATCH)
            base = own_rstd[s, c] * weight
            near = maps[:, :HALF].reshape(SHIFTS // 8, 8, HALF)
            far = maps[:, HALF:].reshape(SHIFTS // 8, 8, HALF)
            for slot in range(2):
                step = step_ref[slot, s].astype(jnp.float32)
                by_near = base * rstd[s, c] * (2.0 - step)
                by_far = base * rstd[s + 1, c] * (step - 1.0)
                stage[s, slot, c] = (near * by_near[None] + far * by_far[None]).reshape(SHIFTS, SHIFTS)

    def save(s):
        return pltpu.make_async_copy(stage.at[s], out.at[s], out_sem.at[s])

    def pass_on(j):
        @pl.when(has_up)
        def _():
            relay_up(j).start()

        @pl.when(has_down)
        def _():
            relay_down(j).start()

    def wait_halo(t):
        @pl.when(has_up)
        def _():
            to_down(t).wait_recv()

        @pl.when(has_down)
        def _():
            to_up(t).wait_recv()

    def far_pass(j):
        arrival(2 * j).wait_recv()

        @pl.when(has_up)
        def _():
            relay_up(j).start()

        arrival(2 * j + 1).wait_recv()

        @pl.when(has_down)
        def _():
            relay_down(j).start()

    def near_pass(j):
        to_prev(j).wait_recv()
        pass_on(j)

    def early(t, carry):
        wait_halo(t)
        spectra(own(t), plain(t))

        @pl.when(t >= 2)
        def _():
            @pl.when(near_take)
            def _():
                near_pass(t - 2)

            @pl.when(jnp.logical_and(far_take, t == 3))
            def _():
                far_pass(0)

            pairs(t - 2)
            save(t - 2).start()

        return carry

    def late(t, carry):
        @pl.when(has_next)
        def _():
            @pl.when(has_up)
            def _():
                relay_down(t - secs).wait_recv()

            @pl.when(has_down)
            def _():
                relay_up(t - secs).wait_recv()

        spectra(plain(t))
        pairs(t - 2)
        save(t - 2).start()
        return carry

    for p in range(1, GROUP):
        @pl.when(carries[p])
        def _():
            pl.semaphore_wait(ready, 1)
            to_carrier(p).wait_recv()
            onward(p).start()
            start_halo(secs - 1)

    img_copy.wait()
    wait_halo(0)
    spectra(own(0))
    lax.fori_loop(1, secs, early, 0)

    @pl.when(far_take)
    def _():
        far_pass(1)

    lax.fori_loop(secs, secs + 2, late, 0)

    @pl.when(near_send)
    def _():
        for j in range(2):
            to_prev(j).wait_send()

    @pl.when(far_send)
    def _():
        to_far().wait_send()
        for p in range(1, GROUP):
            to_carrier(p).wait_send()

    for p in range(1, GROUP):
        @pl.when(carries[p])
        def _():
            onward(p).wait_send()

    @pl.when(has_down)
    def _():
        for t in range(secs):
            to_down(t).wait_send()

    @pl.when(has_up)
    def _():
        for t in range(secs):
            to_up(t).wait_send()

    @pl.when(jnp.logical_and(has_next, has_down))
    def _():
        for j in range(2):
            relay_down(j).wait_send()

    @pl.when(jnp.logical_and(has_next, has_up))
    def _():
        for j in range(2):
            relay_up(j).wait_send()

    for s in range(secs):
        save(s).wait()


def on_device(secs_axis, rows_axis, image, grid_shift, partner_step, tissue):
    secs, height, width = image.shape
    tables = [jnp.asarray(t) for t in (row_table(), col_tables(), back_col_tables(), back_row_table(), col_phases(), row_phases())]
    ints = [jnp.swapaxes(grid_shift, 2, 3), jnp.swapaxes(partner_step, 0, 1), tissue]
    dma = pltpu.SemaphoreType.DMA
    maps = pl.pallas_call(
        functools.partial(kernel, secs_axis, rows_axis),
        out_shape=jax.ShapeDtypeStruct((secs, 2, PC, SHIFTS, SHIFTS), jnp.float32),
        in_specs=[pl.BlockSpec(memory_space=pltpu.HBM)] * 10,
        out_specs=pl.BlockSpec(memory_space=pl.ANY),
        scratch_shapes=[pltpu.VMEM(t.shape, t.dtype) for t in tables]
        + [
            pltpu.VMEM((secs + 2, height, width), jnp.bfloat16),
            pltpu.VMEM((secs + 2, HALO, width), jnp.bfloat16),
            pltpu.VMEM((secs + 2, HALO, width), jnp.bfloat16),
            pltpu.VMEM((secs, 8, 4 * HALF), jnp.float32),
            pltpu.VMEM((secs, 8, 3 * HALF), jnp.float32),
            pltpu.VMEM((2, 2 * STACK, PATCH), jnp.bfloat16),
            pltpu.VMEM((2, 16, PATCH), jnp.float32),
            pltpu.VMEM((PC, PATCH, PATCH), jnp.bfloat16),
            pltpu.VMEM((secs, STACK, WIDE), jnp.bfloat16),
            pltpu.VMEM((secs, PC, 8, HALF), jnp.float32),
            pltpu.VMEM((secs + 1, STACK, WIDE), jnp.bfloat16),
            pltpu.VMEM((secs + 1, PC, 8, HALF), jnp.float32),
            pltpu.VMEM((secs, 2, PC, SHIFTS, SHIFTS), jnp.float32),
            dma((6,)),
            dma,
            dma((secs,)),
            dma((secs + 2,)),
            dma((secs + 2,)),
            dma((secs + 2,)),
            dma((secs + 2,)),
            dma((2,)),
            dma((2,)),
            dma((GROUP,)),
            dma((GROUP,)),
            pltpu.VMEM((HALF // 2, width), jnp.bfloat16),
            dma,
            dma,
            pltpu.SemaphoreType.REGULAR,
        ]
        + [pltpu.SMEM(x.shape, x.dtype) for x in ints]
        + [
            dma((3,)),
        ],
        compiler_params=pltpu.CompilerParams(
            vmem_limit_bytes=40 * 1024 * 1024, collective_id=0, has_side_effects=True
        ),
        cost_estimate=pl.CostEstimate(flops=6_000_000_000, bytes_accessed=8_000_000, transcendentals=0),
    )(
        *[pltpu.with_memory_space_constraint(x, pltpu.HBM) for x in (*ints, image, *tables)]
    )
    return maps.reshape(secs, 2, 1, PC, SHIFTS * SHIFTS)


def solution(mesh):
    return jax.shard_map(
        functools.partial(on_device, mesh.shape["sec"], mesh.shape["row"]),
        mesh=mesh,
        in_specs=(
            P("sec", "row", None),
            P("sec", "row", None, None),
            P("sec", None),
            P("sec", "row", None),
        ),
        out_specs=P("sec", None, "row", None, None),
        check_vma=False,
    )
```

```python
import functools

import jax
import jax.numpy as jnp
import ml_dtypes
import numpy as np
from jax import lax
from jax.experimental import pallas as pl
from jax.experimental.pallas import tpu as pltpu
from jax.sharding import PartitionSpec as P

PC = 5
PATCH = 256
HALF = 128
REACH = 32
GROUP = 4
HALO = 96
SHIFTS = 128
WIDE = 4 * HALF
STACK = PC * HALF + 16


def angle(product):
    return 2.0 * np.pi * (product % PATCH) / PATCH


def row_table():
    k = np.arange(HALF)[:, None]
    r = np.arange(PATCH)[None, :]
    sine = np.sin(angle(k * r))
    sine[0] = 1.0 - 2.0 * (np.arange(PATCH) % 2)
    return np.concatenate([np.cos(angle(k * r)), sine], 0).astype(ml_dtypes.bfloat16)


def col_tables():
    c = np.arange(HALF)[:, None]
    out = []
    for odd in (0, 1):
        ell = 2 * np.arange(HALF)[None, :] + odd
        cos, sin = np.cos(angle(ell * c)), np.sin(angle(ell * c))
        out.append(np.block([[cos, -sin], [-sin, -cos]]))
    return np.stack(out).astype(ml_dtypes.bfloat16)


def back_col_tables():
    v = np.arange(SHIFTS)[None, :] - SHIFTS // 2
    out = []
    for odd in (0, 1):
        ell = 2 * np.arange(HALF)[:, None] + odd
        cos, sin = np.cos(angle(ell * v)), np.sin(angle(ell * v))
        out.append(np.block([[cos, sin], [-sin, cos]]))
    return np.stack(out).astype(ml_dtypes.bfloat16)


def back_row_table():
    u = np.arange(SHIFTS)[:, None] - SHIFTS // 2
    k = np.arange(HALF)[None, :]
    weight = np.where(k == 0, 1.0, 2.0)
    sine = -weight * np.sin(angle(u * k))
    sine[:, 0] = 1.0 - 2.0 * (u[:, 0] % 2)
    return np.concatenate([weight * np.cos(angle(u * k)), sine], 1).astype(np.float32)


def phase_table(frequencies):
    s = np.arange(2 * REACH + 1)[:, None] - REACH
    parts = np.concatenate([f(angle(ell[None, :] * s)) for f, ell in frequencies], 1)
    high = parts.astype(ml_dtypes.bfloat16)
    low = (parts - high.astype(np.float64)).astype(ml_dtypes.bfloat16)
    out = np.zeros((PATCH, parts.shape[1]), ml_dtypes.bfloat16)
    out[: len(s)], out[HALF : HALF + len(s)] = high, low
    return out


def col_phases():
    even = 2 * np.arange(HALF)
    return phase_table([(f, ell) for f in (np.cos, np.sin) for ell in (even, even + 1)])


def row_phases():
    k = np.arange(HALF)
    return phase_table([(np.cos, k), (np.cos, np.where(k == 0, HALF, k)), (np.sin, k)])


def dot(a, b):
    return jnp.dot(a, b, preferred_element_type=jnp.float32)


def folded(own, above, below, tile, start):
    lanes = slice(tile * HALF, (tile + 1) * HALF)
    if start is None:
        return jnp.concatenate([below[0:64, lanes], above[32:96, lanes], own[:, lanes]], 0)
    low = above[0:64, lanes]
    high = below[32:96, lanes]
    rows = lax.broadcasted_iota(jnp.int32, (64, HALF), 0) + 32
    mixed = jnp.where(rows >= start, low.astype(jnp.float32), high.astype(jnp.float32)).astype(jnp.bfloat16)
    return jnp.concatenate([below[0:32, lanes], mixed, above[64:96, lanes], own[:, lanes]], 0)


def window(own, above, below, c, row_start, col_start):
    right = folded(own, above, below, c, row_start)
    zero = jnp.zeros((PATCH, HALF), jnp.bfloat16)
    far = folded(own, above, below, c - 1, row_start) if c > 0 else zero
    near = folded(own, above, below, c + 1, row_start) if c < PC - 1 else zero
    lanes = lax.broadcasted_iota(jnp.int32, (PATCH, HALF), 1)
    left = jnp.where(lanes >= col_start, far.astype(jnp.float32), near.astype(jnp.float32)).astype(jnp.bfloat16)
    return jnp.concatenate([left, right], 1)


def forward(jobs, tab_row, tab_col, lhs, nyq):
    first = lax.broadcasted_iota(jnp.int32, (8, HALF), 0) == 0

    def top(block):
        return block[0:8], block[8:]

    for i, (own, above, below, starts, phases, spec, rstd) in enumerate(jobs):
        base = i * STACK
        for c in range(PC):
            x = window(own, above, below, c, *starts[c])
            part = dot(tab_row[...], x)
            lo, hi = part[:, :HALF], part[:, HALF:]
            even, odd = lo + hi, lo - hi
            ce, se, co, so = even[:HALF], even[HALF:], odd[:HALF], odd[HALF:]
            head, tail = top(ce)
            centre = jnp.mean(head[0:1], axis=1, keepdims=True)
            head = jnp.where(first, head - centre, head)
            ce = jnp.concatenate([head, tail], 0)
            square = jnp.zeros((8, HALF), jnp.float32)
            edge = jnp.zeros((8, HALF), jnp.float32)
            for block in (ce, se, co, so):
                sq = block * block
                square = square + jnp.sum(sq.reshape(HALF // 8, 8, HALF), axis=0)
                edge = edge + sq[0:8]
            total = 2.0 * square - jnp.where(first, edge, 0.0)
            var = jnp.sum(jnp.sum(total, axis=0, keepdims=True), axis=1, keepdims=True) * (
                HALF / float(PATCH**4)
            )
            rstd[c] = jnp.broadcast_to(lax.rsqrt(var + 1e-05), (8, HALF))
            he, te = top(se)
            ho, to = top(so)
            nyq[i, c : c + 1, :HALF] = he[0:1]
            nyq[i, c : c + 1, HALF:] = ho[0:1]
            se = jnp.concatenate([jnp.where(first, 0.0, he), te], 0)
            so = jnp.concatenate([jnp.where(first, 0.0, ho), to], 0)
            rows = slice(base + c * HALF, base + (c + 1) * HALF)
            lhs[0, rows] = jnp.concatenate([ce, se], 1).astype(jnp.bfloat16)
            lhs[1, rows] = jnp.concatenate([co, so], 1).astype(jnp.bfloat16)
        rows = slice(base + PC * HALF, base + STACK)
        zero = jnp.zeros((16, HALF), jnp.bfloat16)
        lhs[0, rows] = jnp.concatenate([nyq[i, :, :HALF].astype(jnp.bfloat16), zero], 1)
        lhs[1, rows] = jnp.concatenate([nyq[i, :, HALF:].astype(jnp.bfloat16), zero], 1)
    for q in range(2):
        f = dot(lhs[q, : len(jobs) * STACK], tab_col[q])
        for i, (_, _, _, _, phases, spec, _) in enumerate(jobs):
            block = f[i * STACK : (i + 1) * STACK]
            if phases is None:
                spec[:, q * PATCH : (q + 1) * PATCH] = block.astype(jnp.bfloat16)
                continue
            cos = [p[:, q * HALF : (q + 1) * HALF] for p in phases]
            sin = [p[:, (q + 2) * HALF : (q + 3) * HALF] for p in phases]
            spare = jnp.zeros((16 - PC, HALF), jnp.float32)
            cos.append(jnp.concatenate(cos + [spare], 0))
            sin.append(jnp.concatenate(sin + [spare], 0))
            for c in range(PC + 1):
                rows = slice(c * HALF, min((c + 1) * HALF, STACK))
                re, im = block[rows, :HALF], block[rows, HALF:]
                turned = jnp.concatenate([re * cos[c] - im * sin[c], re * sin[c] + im * cos[c]], 1)
                spec[rows, q * PATCH : (q + 1) * PATCH] = turned.astype(jnp.bfloat16)


def crossed(a, b):
    out = []
    for base in (0, 2 * HALF):
        re, im = slice(base, base + HALF), slice(base + HALF, base + 2 * HALF)
        are, aim = a[:, re], a[:, im]
        bre, bim = b[:, re], b[:, im]
        g = jnp.concatenate([are * bre + aim * bim, are * bim - aim * bre], 1)
        out.append(g)
    return out


def remote(src, dst, send, recv, where):
    return pltpu.make_async_remote_copy(
        src_ref=src, dst_ref=dst, send_sem=send, recv_sem=recv, device_id=where, device_id_type=pl.DeviceIdType.MESH
    )


def kernel(
    secs_axis, rows_axis,
    shift_hbm, step_hbm, tissue_hbm, img, *refs,
):
    tables, refs = refs[:6], refs[6:]
    out, refs = refs[0], refs[1:]
    tabs, refs = refs[:6], refs[6:]
    (strip, above, below, pcol, prow, lhs, nyq, right, own_spec, own_rstd, spec, rstd, stage,
     tab_sem, img_sem, out_sem, up_send, up_recv, down_send, down_recv, sec_send, sec_recv,
     part_send, part_recv, transit, via_send, via_recv, slant_send, ready, shift_ref, step_ref, tissue_ref, int_sem) = refs
    tab_row, tab_col, tab_bcol, tab_brow, tab_pcol, tab_prow = tabs
    secs = own_spec.shape[0]
    sec, row = lax.axis_index("sec"), lax.axis_index("row")
    has_up, has_down = row > 0, row < rows_axis - 1
    has_prev, has_next = sec > 0, sec < secs_axis - 1
    up, down, prev, following = (sec, row - 1), (sec, row + 1), (sec - 1, row), (sec + 1, row)
    place = lax.rem(sec, GROUP)
    far_send = jnp.logical_and(place == 0, has_prev)
    far_take = jnp.logical_and(place == GROUP - 1, has_next)
    carries = [jnp.logical_and(place == p, sec > p) for p in range(GROUP)]
    near_send = jnp.logical_and(has_prev, place > 0)
    near_take = jnp.logical_and(has_next, place < GROUP - 1)
    sides = [(has_up, up), (has_down, down), (near_send, prev), (near_take, following)]
    for p in range(2, GROUP):
        sides += [(far_send, (sec + p, row)), (carries[p], (sec - p, row))]
    greeted = [(far_send, prev)] + [(carries[p], (sec - p - 1, row)) for p in range(1, GROUP)]
    odd = lax.rem(row, 2) == 1
    edge_up = jnp.logical_and(jnp.logical_not(odd), has_up)
    edge_down = jnp.logical_and(odd, has_down)
    expected = sum(there.astype(jnp.int32) for there, _ in sides) + GROUP * far_take.astype(jnp.int32)

    barrier = pltpu.get_barrier_semaphore()
    for there, where in sides + greeted:
        @pl.when(there)
        def _():
            pl.semaphore_signal(barrier, inc=1, device_id=where, device_id_type=pl.DeviceIdType.MESH)

    img_copy = pltpu.make_async_copy(img, strip.at[0:secs], img_sem)
    img_copy.start()
    loads = [pltpu.make_async_copy(t, v, tab_sem.at[i]) for i, (t, v) in enumerate(zip(tables, tabs))]
    ints = ((shift_hbm, shift_ref), (step_hbm, step_ref), (tissue_hbm, tissue_ref))
    loads += [pltpu.make_async_copy(h, v, int_sem.at[i]) for i, (h, v) in enumerate(ints)]
    for load in loads:
        load.start()

    pl.semaphore_wait(barrier, expected)

    @pl.when(far_take)
    def _():
        for p in range(GROUP):
            pl.semaphore_signal(ready, inc=1, device_id=(sec + p + 1, row), device_id_type=pl.DeviceIdType.MESH)

    def to_prev(j):
        return remote(img.at[j], strip.at[secs + j], sec_send.at[j], sec_recv.at[j], prev)

    def to_down(t):
        return remote(img.at[t, HALF - HALO : HALF], above.at[t], down_send.at[t], down_recv.at[t], down)

    def to_up(t):
        return remote(img.at[t, 0:HALO], below.at[t], up_send.at[t], up_recv.at[t], up)

    def relay_down(j):
        t = secs + j
        return remote(strip.at[t, HALF // 2 : HALF], above.at[t, HALO - HALF // 2 : HALO], down_send.at[t], down_recv.at[t], down)

    def relay_up(j):
        t = secs + j
        return remote(strip.at[t, 0 : HALF // 2], below.at[t, 0 : HALF // 2], up_send.at[t], up_recv.at[t], up)

    def part(p):
        return p // 2, slice(p % 2 * (HALF // 2), (p % 2 + 1) * (HALF // 2))

    def to_far():
        return remote(img.at[0, : HALF // 2], strip.at[secs, : HALF // 2], part_send.at[0], part_recv.at[0], prev)

    def to_carrier(p):
        j, rows = part(p)
        return remote(img.at[j, rows], transit, part_send.at[p], via_recv, (sec + p, row))

    def onward(p):
        j, rows = part(p)
        return remote(transit, strip.at[secs + j, rows], via_send, part_recv.at[p], (sec - p - 1, row))

    def slant(p):
        t, source = secs + p // 2, img.at[0, : HALF // 2] if p == 0 else transit
        if p % 2 == 0:
            return remote(source, below.at[t, 0 : HALF // 2], slant_send, up_recv.at[t], (sec - p - 1, row - 1))
        return remote(source, above.at[t, HALO - HALF // 2 : HALO], slant_send, down_recv.at[t], (sec - p - 1, row + 1))

    def slants(p):
        return jnp.logical_and(far_send if p == 0 else carries[p], edge_down if p % 2 else edge_up)

    def arrival(p):
        j, rows = part(p)
        return remote(transit, strip.at[secs + j, rows], via_send, part_recv.at[p], (sec + p + 1, row))

    def start_halo(t):
        @pl.when(has_down)
        def _():
            to_down(t).start()

        @pl.when(has_up)
        def _():
            to_up(t).start()

    start_halo(0)

    @pl.when(far_send)
    def _():
        for p in range(1, GROUP):
            to_carrier(p).start()

    @pl.when(near_send)
    def _():
        to_prev(0).start()

    for t in range(1, secs - 1):
        start_halo(t)

    @pl.when(near_send)
    def _():
        to_prev(1).start()

    @pl.when(jnp.logical_not(jnp.logical_or(jnp.logical_or(carries[1], carries[2]), carries[3])))
    def _():
        start_halo(secs - 1)

    @pl.when(far_send)
    def _():
        pl.semaphore_wait(ready, 1)
        to_far().start()

    @pl.when(slants(0))
    def _():
        slant(0).start()

    @pl.when(jnp.logical_not(has_up))
    def _():
        above[...] = jnp.zeros_like(above)

    @pl.when(jnp.logical_not(has_down))
    def _():
        below[...] = jnp.zeros_like(below)

    @pl.when(jnp.logical_not(has_next))
    def _():
        strip[secs:] = jnp.zeros((2, HALF, strip.shape[2]), jnp.bfloat16)
        above[secs:] = jnp.zeros((2, HALO, strip.shape[2]), jnp.bfloat16)
        below[secs:] = jnp.zeros((2, HALO, strip.shape[2]), jnp.bfloat16)

    nyq[...] = jnp.zeros_like(nyq)
    for load in loads:
        load.wait()

    rows = lax.broadcasted_iota(jnp.int32, (8 * secs, PATCH), 0)
    lanes = lax.broadcasted_iota(jnp.int32, (8 * secs, PATCH), 1)
    for axis, table, phase in ((0, tab_prow, prow), (1, tab_pcol, pcol)):
        wanted = jnp.zeros_like(lanes)
        for s in range(secs):
            for c in range(PC):
                wanted = jnp.where(rows == 8 * s + c, shift_ref[s, 0, axis, c] + REACH, wanted)
        chosen = jnp.logical_or(lanes == wanted, lanes == wanted + HALF)
        picked = dot(chosen.astype(jnp.float32).astype(jnp.bfloat16), table[...])
        phase[...] = picked.reshape(secs, 8, picked.shape[1])

    def plain(t):
        return (strip.at[t], above.at[t], below.at[t], [(None, 64)] * PC, None, spec.at[t - 1], rstd.at[t - 1])

    def own(s):
        starts = [(shift_ref[s, 0, 0, c] + 64, shift_ref[s, 0, 1, c] + 64) for c in range(PC)]
        phases = [pcol[s, c : c + 1] for c in range(PC)]
        return (strip.at[s], above.at[s], below.at[s], starts, phases, own_spec.at[s], own_rstd.at[s])

    def spectra(*jobs):
        forward(jobs, tab_row, tab_col, lhs, nyq)

    first = lax.broadcasted_iota(jnp.int32, (8, HALF), 0) == 0

    def pairs(s):
        for part in range(2):
            ge, go = crossed(own_spec[s], spec[s + part])
            g = dot(ge, tab_bcol[0]) + dot(go, tab_bcol[1])
            lanes = slice(part * HALF, (part + 1) * HALF)
            for c in range(PC):
                block = g[c * HALF : (c + 1) * HALF]
                edge = jnp.broadcast_to(g[PC * HALF + c : PC * HALF + c + 1, :HALF], (8, HALF))
                im = block[:, HALF:]
                im = jnp.concatenate([jnp.where(first, edge, im[0:8]), im[8:]], 0)
                right[c, :HALF, lanes] = block[:, :HALF].astype(jnp.bfloat16)
                right[c, HALF:, lanes] = im.astype(jnp.bfloat16)
        for c in range(PC):
            turn = prow[s, c : c + 1]
            cos, cos_edge, sin = turn[:, :HALF], turn[:, HALF : 2 * HALF], turn[:, 2 * HALF :]
            bc, bs = tab_brow[:, :HALF], tab_brow[:, HALF:]
            left = jnp.concatenate([bc * cos - bs * sin, bs * cos_edge + bc * sin], 1).astype(jnp.bfloat16)
            maps = dot(left, right[c])
            weight = tissue_ref[s, 0, c].astype(jnp.float32) / float(PATCH * PATCH)
            base = own_rstd[s, c] * weight
            near = maps[:, :HALF].reshape(SHIFTS // 8, 8, HALF)
            far = maps[:, HALF:].reshape(SHIFTS // 8, 8, HALF)
            for slot in range(2):
                step = step_ref[slot, s].astype(jnp.float32)
                by_near = base * rstd[s, c] * (2.0 - step)
                by_far = base * rstd[s + 1, c] * (step - 1.0)
                stage[s, slot, c] = (near * by_near[None] + far * by_far[None]).reshape(SHIFTS, SHIFTS)

    def save(s):
        return pltpu.make_async_copy(stage.at[s], out.at[s], out_sem.at[s])

    def pass_on(j):
        @pl.when(has_up)
        def _():
            relay_up(j).start()

        @pl.when(has_down)
        def _():
            relay_down(j).start()

    def wait_halo(t):
        @pl.when(has_up)
        def _():
            to_down(t).wait_recv()

        @pl.when(has_down)
        def _():
            to_up(t).wait_recv()

    def far_pass(j):
        arrival(2 * j).wait_recv()

        @pl.when(jnp.logical_and(has_up, jnp.logical_not(edge_up)))
        def _():
            relay_up(j).start()

        arrival(2 * j + 1).wait_recv()

        @pl.when(jnp.logical_and(has_down, jnp.logical_not(edge_down)))
        def _():
            relay_down(j).start()

    def near_pass(j):
        to_prev(j).wait_recv()
        pass_on(j)

    def early(t, carry):
        wait_halo(t)
        spectra(own(t), plain(t))

        @pl.when(t >= 2)
        def _():
            @pl.when(near_take)
            def _():
                near_pass(t - 2)

            @pl.when(jnp.logical_and(far_take, t == 3))
            def _():
                far_pass(0)

            pairs(t - 2)
            save(t - 2).start()

        return carry

    def late(t, carry):
        @pl.when(has_next)
        def _():
            @pl.when(has_up)
            def _():
                relay_down(t - secs).wait_recv()

            @pl.when(has_down)
            def _():
                relay_up(t - secs).wait_recv()

        spectra(plain(t))
        pairs(t - 2)
        save(t - 2).start()
        return carry

    for p in range(1, GROUP):
        @pl.when(carries[p])
        def _():
            pl.semaphore_wait(ready, 1)
            to_carrier(p).wait_recv()
            onward(p).start()

        @pl.when(slants(p))
        def _():
            slant(p).start()

        @pl.when(carries[p])
        def _():
            start_halo(secs - 1)

    img_copy.wait()
    wait_halo(0)
    spectra(own(0))
    lax.fori_loop(1, secs, early, 0)

    @pl.when(far_take)
    def _():
        far_pass(1)

    lax.fori_loop(secs, secs + 2, late, 0)

    @pl.when(near_send)
    def _():
        for j in range(2):
            to_prev(j).wait_send()

    @pl.when(far_send)
    def _():
        to_far().wait_send()
        for p in range(1, GROUP):
            to_carrier(p).wait_send()

    for p in range(1, GROUP):
        @pl.when(carries[p])
        def _():
            onward(p).wait_send()

    @pl.when(has_down)
    def _():
        for t in range(secs):
            to_down(t).wait_send()

    @pl.when(has_up)
    def _():
        for t in range(secs):
            to_up(t).wait_send()

    for p in range(GROUP):
        @pl.when(slants(p))
        def _():
            slant(p).wait_send()

    left_down = jnp.logical_not(jnp.logical_and(far_take, edge_down))
    left_up = jnp.logical_not(jnp.logical_and(far_take, edge_up))

    @pl.when(jnp.logical_and(jnp.logical_and(has_next, has_down), left_down))
    def _():
        for j in range(2):
            relay_down(j).wait_send()

    @pl.when(jnp.logical_and(jnp.logical_and(has_next, has_up), left_up))
    def _():
        for j in range(2):
            relay_up(j).wait_send()

    for s in range(secs):
        save(s).wait()


def on_device(secs_axis, rows_axis, image, grid_shift, partner_step, tissue):
    secs, height, width = image.shape
    tables = [jnp.asarray(t) for t in (row_table(), col_tables(), back_col_tables(), back_row_table(), col_phases(), row_phases())]
    ints = [jnp.swapaxes(grid_shift, 2, 3), jnp.swapaxes(partner_step, 0, 1), tissue]
    dma = pltpu.SemaphoreType.DMA
    maps = pl.pallas_call(
        functools.partial(kernel, secs_axis, rows_axis),
        out_shape=jax.ShapeDtypeStruct((secs, 2, PC, SHIFTS, SHIFTS), jnp.float32),
        in_specs=[pl.BlockSpec(memory_space=pltpu.HBM)] * 10,
        out_specs=pl.BlockSpec(memory_space=pl.ANY),
        scratch_shapes=[pltpu.VMEM(t.shape, t.dtype) for t in tables]
        + [
            pltpu.VMEM((secs + 2, height, width), jnp.bfloat16),
            pltpu.VMEM((secs + 2, HALO, width), jnp.bfloat16),
            pltpu.VMEM((secs + 2, HALO, width), jnp.bfloat16),
            pltpu.VMEM((secs, 8, 4 * HALF), jnp.float32),
            pltpu.VMEM((secs, 8, 3 * HALF), jnp.float32),
            pltpu.VMEM((2, 2 * STACK, PATCH), jnp.bfloat16),
            pltpu.VMEM((2, 16, PATCH), jnp.float32),
            pltpu.VMEM((PC, PATCH, PATCH), jnp.bfloat16),
            pltpu.VMEM((secs, STACK, WIDE), jnp.bfloat16),
            pltpu.VMEM((secs, PC, 8, HALF), jnp.float32),
            pltpu.VMEM((secs + 1, STACK, WIDE), jnp.bfloat16),
            pltpu.VMEM((secs + 1, PC, 8, HALF), jnp.float32),
            pltpu.VMEM((secs, 2, PC, SHIFTS, SHIFTS), jnp.float32),
            dma((6,)),
            dma,
            dma((secs,)),
            dma((secs + 2,)),
            dma((secs + 2,)),
            dma((secs + 2,)),
            dma((secs + 2,)),
            dma((2,)),
            dma((2,)),
            dma((GROUP,)),
            dma((GROUP,)),
            pltpu.VMEM((HALF // 2, width), jnp.bfloat16),
            dma,
            dma,
            dma,
            pltpu.SemaphoreType.REGULAR,
        ]
        + [pltpu.SMEM(x.shape, x.dtype) for x in ints]
        + [
            dma((3,)),
        ],
        compiler_params=pltpu.CompilerParams(
            vmem_limit_bytes=40 * 1024 * 1024, collective_id=0, has_side_effects=True
        ),
        cost_estimate=pl.CostEstimate(flops=6_000_000_000, bytes_accessed=8_000_000, transcendentals=0),
    )(
        *[pltpu.with_memory_space_constraint(x, pltpu.HBM) for x in (*ints, image, *tables)]
    )
    return maps.reshape(secs, 2, 1, PC, SHIFTS * SHIFTS)


def solution(mesh):
    return jax.shard_map(
        functools.partial(on_device, mesh.shape["sec"], mesh.shape["row"]),
        mesh=mesh,
        in_specs=(
            P("sec", "row", None),
            P("sec", "row", None, None),
            P("sec", None),
            P("sec", "row", None),
        ),
        out_specs=P("sec", None, "row", None, None),
        check_vma=False,
    )
```

```python
import functools

import jax
import jax.numpy as jnp
import ml_dtypes
import numpy as np
from jax import lax
from jax.experimental import pallas as pl
from jax.experimental.pallas import tpu as pltpu
from jax.sharding import PartitionSpec as P

PC = 5
PATCH = 256
HALF = 128
REACH = 32
GROUP = 4
HALO = 96
SHIFTS = 128
WIDE = 4 * HALF
STACK = PC * HALF + 16


def angle(product):
    return 2.0 * np.pi * (product % PATCH) / PATCH


def row_table():
    k = np.arange(HALF)[:, None]
    r = np.arange(PATCH)[None, :]
    sine = np.sin(angle(k * r))
    sine[0] = 1.0 - 2.0 * (np.arange(PATCH) % 2)
    return np.concatenate([np.cos(angle(k * r)), sine], 0).astype(ml_dtypes.bfloat16)


def col_tables():
    c = np.arange(HALF)[:, None]
    out = []
    for odd in (0, 1):
        ell = 2 * np.arange(HALF)[None, :] + odd
        cos, sin = np.cos(angle(ell * c)), np.sin(angle(ell * c))
        out.append(np.block([[cos, -sin], [-sin, -cos]]))
    return np.stack(out).astype(ml_dtypes.bfloat16)


def back_col_tables():
    v = np.arange(SHIFTS)[None, :] - SHIFTS // 2
    out = []
    for odd in (0, 1):
        ell = 2 * np.arange(HALF)[:, None] + odd
        cos, sin = np.cos(angle(ell * v)), np.sin(angle(ell * v))
        out.append(np.block([[cos, sin], [-sin, cos]]))
    return np.stack(out).astype(ml_dtypes.bfloat16)


def back_row_table():
    u = np.arange(SHIFTS)[:, None] - SHIFTS // 2
    k = np.arange(HALF)[None, :]
    weight = np.where(k == 0, 1.0, 2.0)
    sine = -weight * np.sin(angle(u * k))
    sine[:, 0] = 1.0 - 2.0 * (u[:, 0] % 2)
    return np.concatenate([weight * np.cos(angle(u * k)), sine], 1).astype(np.float32)


def phase_table(frequencies):
    s = np.arange(2 * REACH + 1)[:, None] - REACH
    parts = np.concatenate([f(angle(ell[None, :] * s)) for f, ell in frequencies], 1)
    high = parts.astype(ml_dtypes.bfloat16)
    low = (parts - high.astype(np.float64)).astype(ml_dtypes.bfloat16)
    out = np.zeros((PATCH, parts.shape[1]), ml_dtypes.bfloat16)
    out[: len(s)], out[HALF : HALF + len(s)] = high, low
    return out


def col_phases():
    even = 2 * np.arange(HALF)
    return phase_table([(f, ell) for f in (np.cos, np.sin) for ell in (even, even + 1)])


def row_phases():
    k = np.arange(HALF)
    return phase_table([(np.cos, k), (np.cos, np.where(k == 0, HALF, k)), (np.sin, k)])


def dot(a, b):
    return jnp.dot(a, b, preferred_element_type=jnp.float32)


def folded(own, above, below, tile, start):
    lanes = slice(tile * HALF, (tile + 1) * HALF)
    if start is None:
        return jnp.concatenate([below[0:64, lanes], above[32:96, lanes], own[:, lanes]], 0)
    low = above[0:64, lanes]
    high = below[32:96, lanes]
    rows = lax.broadcasted_iota(jnp.int32, (64, HALF), 0) + 32
    mixed = jnp.where(rows >= start, low.astype(jnp.float32), high.astype(jnp.float32)).astype(jnp.bfloat16)
    return jnp.concatenate([below[0:32, lanes], mixed, above[64:96, lanes], own[:, lanes]], 0)


def window(own, above, below, c, row_start, col_start):
    right = folded(own, above, below, c, row_start)
    zero = jnp.zeros((PATCH, HALF), jnp.bfloat16)
    far = folded(own, above, below, c - 1, row_start) if c > 0 else zero
    near = folded(own, above, below, c + 1, row_start) if c < PC - 1 else zero
    lanes = lax.broadcasted_iota(jnp.int32, (PATCH, HALF), 1)
    left = jnp.where(lanes >= col_start, far.astype(jnp.float32), near.astype(jnp.float32)).astype(jnp.bfloat16)
    return jnp.concatenate([left, right], 1)


def forward(jobs, tab_row, tab_col, lhs, nyq):
    first = lax.broadcasted_iota(jnp.int32, (8, HALF), 0) == 0

    def top(block):
        return block[0:8], block[8:]

    for i, (own, above, below, starts, phases, spec, rstd) in enumerate(jobs):
        base = i * STACK
        for c in range(PC):
            x = window(own, above, below, c, *starts[c])
            part = dot(tab_row[...], x)
            lo, hi = part[:, :HALF], part[:, HALF:]
            even, odd = lo + hi, lo - hi
            ce, se, co, so = even[:HALF], even[HALF:], odd[:HALF], odd[HALF:]
            head, tail = top(ce)
            centre = jnp.mean(head[0:1], axis=1, keepdims=True)
            head = jnp.where(first, head - centre, head)
            ce = jnp.concatenate([head, tail], 0)
            square = jnp.zeros((8, HALF), jnp.float32)
            edge = jnp.zeros((8, HALF), jnp.float32)
            for block in (ce, se, co, so):
                sq = block * block
                square = square + jnp.sum(sq.reshape(HALF // 8, 8, HALF), axis=0)
                edge = edge + sq[0:8]
            total = 2.0 * square - jnp.where(first, edge, 0.0)
            var = jnp.sum(jnp.sum(total, axis=0, keepdims=True), axis=1, keepdims=True) * (
                HALF / float(PATCH**4)
            )
            rstd[c] = jnp.broadcast_to(lax.rsqrt(var + 1e-05), (8, HALF))
            he, te = top(se)
            ho, to = top(so)
            nyq[i, c : c + 1, :HALF] = he[0:1]
            nyq[i, c : c + 1, HALF:] = ho[0:1]
            se = jnp.concatenate([jnp.where(first, 0.0, he), te], 0)
            so = jnp.concatenate([jnp.where(first, 0.0, ho), to], 0)
            rows = slice(base + c * HALF, base + (c + 1) * HALF)
            lhs[0, rows] = jnp.concatenate([ce, se], 1).astype(jnp.bfloat16)
            lhs[1, rows] = jnp.concatenate([co, so], 1).astype(jnp.bfloat16)
        rows = slice(base + PC * HALF, base + STACK)
        zero = jnp.zeros((16, HALF), jnp.bfloat16)
        lhs[0, rows] = jnp.concatenate([nyq[i, :, :HALF].astype(jnp.bfloat16), zero], 1)
        lhs[1, rows] = jnp.concatenate([nyq[i, :, HALF:].astype(jnp.bfloat16), zero], 1)
    for q in range(2):
        f = dot(lhs[q, : len(jobs) * STACK], tab_col[q])
        for i, (_, _, _, _, phases, spec, _) in enumerate(jobs):
            block = f[i * STACK : (i + 1) * STACK]
            if phases is None:
                spec[:, q * PATCH : (q + 1) * PATCH] = block.astype(jnp.bfloat16)
                continue
            cos = [p[:, q * HALF : (q + 1) * HALF] for p in phases]
            sin = [p[:, (q + 2) * HALF : (q + 3) * HALF] for p in phases]
            spare = jnp.zeros((16 - PC, HALF), jnp.float32)
            cos.append(jnp.concatenate(cos + [spare], 0))
            sin.append(jnp.concatenate(sin + [spare], 0))
            for c in range(PC + 1):
                rows = slice(c * HALF, min((c + 1) * HALF, STACK))
                re, im = block[rows, :HALF], block[rows, HALF:]
                turned = jnp.concatenate([re * cos[c] - im * sin[c], re * sin[c] + im * cos[c]], 1)
                spec[rows, q * PATCH : (q + 1) * PATCH] = turned.astype(jnp.bfloat16)


def crossed(a, b):
    out = []
    for base in (0, 2 * HALF):
        re, im = slice(base, base + HALF), slice(base + HALF, base + 2 * HALF)
        are, aim = a[:, re], a[:, im]
        bre, bim = b[:, re], b[:, im]
        g = jnp.concatenate([are * bre + aim * bim, are * bim - aim * bre], 1)
        out.append(g)
    return out


def remote(src, dst, send, recv, where):
    return pltpu.make_async_remote_copy(
        src_ref=src, dst_ref=dst, send_sem=send, recv_sem=recv, device_id=where, device_id_type=pl.DeviceIdType.MESH
    )


def kernel(
    secs_axis, rows_axis,
    shift_hbm, step_hbm, tissue_hbm, img, *refs,
):
    tables, refs = refs[:6], refs[6:]
    out, refs = refs[0], refs[1:]
    tabs, refs = refs[:6], refs[6:]
    (strip, above, below, pcol, prow, lhs, nyq, right, own_spec, own_rstd, spec, rstd, stage,
     tab_sem, img_sem, out_sem, up_send, up_recv, down_send, down_recv, sec_send, sec_recv,
     part_send, part_recv, transit, via_send, via_recv, slant_send, ready, shift_ref, step_ref, tissue_ref, int_sem) = refs
    tab_row, tab_col, tab_bcol, tab_brow, tab_pcol, tab_prow = tabs
    secs = own_spec.shape[0]
    sec, row = lax.axis_index("sec"), lax.axis_index("row")
    has_up, has_down = row > 0, row < rows_axis - 1
    has_prev, has_next = sec > 0, sec < secs_axis - 1
    up, down, prev, following = (sec, row - 1), (sec, row + 1), (sec - 1, row), (sec + 1, row)
    place = lax.rem(sec, GROUP)
    far_send = jnp.logical_and(place == 0, has_prev)
    far_take = jnp.logical_and(place == GROUP - 1, has_next)
    carries = [jnp.logical_and(place == p, sec > p) for p in range(GROUP)]
    near_send = jnp.logical_and(has_prev, place > 0)
    near_take = jnp.logical_and(has_next, place < GROUP - 1)
    sides = [(has_up, up), (has_down, down), (near_send, prev), (near_take, following)]
    for p in range(2, GROUP):
        sides += [(far_send, (sec + p, row)), (carries[p], (sec - p, row))]
    greeted = [(far_send, prev)] + [(carries[p], (sec - p - 1, row)) for p in range(1, GROUP)]
    odd = lax.rem(row, 2) == 1
    edge_up = jnp.logical_and(jnp.logical_not(odd), has_up)
    edge_down = jnp.logical_and(odd, has_down)
    expected = sum(there.astype(jnp.int32) for there, _ in sides) + GROUP * far_take.astype(jnp.int32)

    barrier = pltpu.get_barrier_semaphore()
    for there, where in sides + greeted:
        @pl.when(there)
        def _():
            pl.semaphore_signal(barrier, inc=1, device_id=where, device_id_type=pl.DeviceIdType.MESH)

    img_copy = pltpu.make_async_copy(img, strip.at[0:secs], img_sem)
    img_copy.start()
    loads = [pltpu.make_async_copy(t, v, tab_sem.at[i]) for i, (t, v) in enumerate(zip(tables, tabs))]
    ints = ((shift_hbm, shift_ref), (step_hbm, step_ref), (tissue_hbm, tissue_ref))
    loads += [pltpu.make_async_copy(h, v, int_sem.at[i]) for i, (h, v) in enumerate(ints)]
    for load in loads:
        load.start()

    pl.semaphore_wait(barrier, expected)

    @pl.when(far_take)
    def _():
        for p in range(GROUP):
            pl.semaphore_signal(ready, inc=1, device_id=(sec + p + 1, row), device_id_type=pl.DeviceIdType.MESH)

    def to_prev(j):
        return remote(img.at[j], strip.at[secs + j], sec_send.at[j], sec_recv.at[j], prev)

    def to_down(t):
        return remote(img.at[t, HALF - HALO : HALF], above.at[t], down_send.at[t], down_recv.at[t], down)

    def to_up(t):
        return remote(img.at[t, 0:HALO], below.at[t], up_send.at[t], up_recv.at[t], up)

    def relay_down(j):
        t = secs + j
        return remote(strip.at[t, HALF // 2 : HALF], above.at[t, HALO - HALF // 2 : HALO], down_send.at[t], down_recv.at[t], down)

    def relay_up(j):
        t = secs + j
        return remote(strip.at[t, 0 : HALF // 2], below.at[t, 0 : HALF // 2], up_send.at[t], up_recv.at[t], up)

    def part(p):
        return p // 2, slice(p % 2 * (HALF // 2), (p % 2 + 1) * (HALF // 2))

    def to_far():
        return remote(img.at[0, : HALF // 2], strip.at[secs, : HALF // 2], part_send.at[0], part_recv.at[0], prev)

    def to_carrier(p):
        j, rows = part(p)
        return remote(img.at[j, rows], transit, part_send.at[p], via_recv, (sec + p, row))

    def onward(p):
        j, rows = part(p)
        return remote(transit, strip.at[secs + j, rows], via_send, part_recv.at[p], (sec - p - 1, row))

    def slant(p):
        t, source = secs + p // 2, img.at[0, : HALF // 2] if p == 0 else transit
        if p % 2 == 0:
            return remote(source, below.at[t, 0 : HALF // 2], slant_send, up_recv.at[t], (sec - p - 1, row - 1))
        return remote(source, above.at[t, HALO - HALF // 2 : HALO], slant_send, down_recv.at[t], (sec - p - 1, row + 1))

    def slants(p):
        return jnp.logical_and(far_send if p == 0 else carries[p], edge_down if p % 2 else edge_up)

    def arrival(p):
        j, rows = part(p)
        return remote(transit, strip.at[secs + j, rows], via_send, part_recv.at[p], (sec + p + 1, row))

    def start_halo(t):
        @pl.when(has_down)
        def _():
            to_down(t).start()

        @pl.when(has_up)
        def _():
            to_up(t).start()

    start_halo(0)

    @pl.when(far_send)
    def _():
        for p in range(1, GROUP):
            to_carrier(p).start()

    @pl.when(near_send)
    def _():
        to_prev(0).start()

    for t in range(1, secs - 1):
        start_halo(t)

    @pl.when(near_send)
    def _():
        to_prev(1).start()

    @pl.when(jnp.logical_not(jnp.logical_or(jnp.logical_or(carries[1], carries[2]), carries[3])))
    def _():
        start_halo(secs - 1)

    @pl.when(far_send)
    def _():
        pl.semaphore_wait(ready, 1)
        to_far().start()

    @pl.when(slants(0))
    def _():
        slant(0).start()

    @pl.when(jnp.logical_not(has_up))
    def _():
        above[...] = jnp.zeros_like(above)

    @pl.when(jnp.logical_not(has_down))
    def _():
        below[...] = jnp.zeros_like(below)

    @pl.when(jnp.logical_not(has_next))
    def _():
        strip[secs:] = jnp.zeros((2, HALF, strip.shape[2]), jnp.bfloat16)
        above[secs:] = jnp.zeros((2, HALO, strip.shape[2]), jnp.bfloat16)
        below[secs:] = jnp.zeros((2, HALO, strip.shape[2]), jnp.bfloat16)

    nyq[...] = jnp.zeros_like(nyq)
    for load in loads:
        load.wait()

    rows = lax.broadcasted_iota(jnp.int32, (8 * secs, PATCH), 0)
    lanes = lax.broadcasted_iota(jnp.int32, (8 * secs, PATCH), 1)
    for axis, table, phase in ((0, tab_prow, prow), (1, tab_pcol, pcol)):
        wanted = jnp.zeros_like(lanes)
        for s in range(secs):
            for c in range(PC):
                wanted = jnp.where(rows == 8 * s + c, shift_ref[s, 0, axis, c] + REACH, wanted)
        chosen = jnp.logical_or(lanes == wanted, lanes == wanted + HALF)
        picked = dot(chosen.astype(jnp.float32).astype(jnp.bfloat16), table[...])
        phase[...] = picked.reshape(secs, 8, picked.shape[1])

    def plain(t):
        return (strip.at[t], above.at[t], below.at[t], [(None, 64)] * PC, None, spec.at[t - 1], rstd.at[t - 1])

    def own(s):
        starts = [(shift_ref[s, 0, 0, c] + 64, shift_ref[s, 0, 1, c] + 64) for c in range(PC)]
        phases = [pcol[s, c : c + 1] for c in range(PC)]
        return (strip.at[s], above.at[s], below.at[s], starts, phases, own_spec.at[s], own_rstd.at[s])

    def spectra(*jobs):
        forward(jobs, tab_row, tab_col, lhs, nyq)

    first = lax.broadcasted_iota(jnp.int32, (8, HALF), 0) == 0

    def pairs(s):
        for part in range(2):
            ge, go = crossed(own_spec[s], spec[s + part])
            g = dot(ge, tab_bcol[0]) + dot(go, tab_bcol[1])
            lanes = slice(part * HALF, (part + 1) * HALF)
            for c in range(PC):
                block = g[c * HALF : (c + 1) * HALF]
                edge = jnp.broadcast_to(g[PC * HALF + c : PC * HALF + c + 1, :HALF], (8, HALF))
                im = block[:, HALF:]
                im = jnp.concatenate([jnp.where(first, edge, im[0:8]), im[8:]], 0)
                right[c, :HALF, lanes] = block[:, :HALF].astype(jnp.bfloat16)
                right[c, HALF:, lanes] = im.astype(jnp.bfloat16)
        for c in range(PC):
            turn = prow[s, c : c + 1]
            cos, cos_edge, sin = turn[:, :HALF], turn[:, HALF : 2 * HALF], turn[:, 2 * HALF :]
            bc, bs = tab_brow[:, :HALF], tab_brow[:, HALF:]
            left = jnp.concatenate([bc * cos - bs * sin, bs * cos_edge + bc * sin], 1).astype(jnp.bfloat16)
            maps = dot(left, right[c])
            weight = tissue_ref[s, 0, c].astype(jnp.float32) / float(PATCH * PATCH)
            base = own_rstd[s, c] * weight
            near = maps[:, :HALF].reshape(SHIFTS // 8, 8, HALF)
            far = maps[:, HALF:].reshape(SHIFTS // 8, 8, HALF)
            for slot in range(2):
                step = step_ref[slot, s].astype(jnp.float32)
                by_near = base * rstd[s, c] * (2.0 - step)
                by_far = base * rstd[s + 1, c] * (step - 1.0)
                stage[s, slot, c] = (near * by_near[None] + far * by_far[None]).reshape(SHIFTS, SHIFTS)

    def save(s):
        return pltpu.make_async_copy(stage.at[s], out.at[s], out_sem.at[s])

    def pass_on(j):
        @pl.when(has_up)
        def _():
            relay_up(j).start()

        @pl.when(has_down)
        def _():
            relay_down(j).start()

    def wait_halo(t):
        @pl.when(has_up)
        def _():
            to_down(t).wait_recv()

        @pl.when(has_down)
        def _():
            to_up(t).wait_recv()

    def far_pass(j):
        for leads, h, there, copy in ((odd, 0, has_up, relay_up), (jnp.logical_not(odd), 1, has_down, relay_down)):
            @pl.when(leads)
            def _():
                arrival(2 * j + h).wait_recv()

                @pl.when(there)
                def _():
                    copy(j).start()

                arrival(2 * j + 1 - h).wait_recv()

    def near_pass(j):
        to_prev(j).wait_recv()
        pass_on(j)

    def early(t, carry):
        wait_halo(t)
        spectra(own(t), plain(t))

        @pl.when(t >= 2)
        def _():
            @pl.when(near_take)
            def _():
                near_pass(t - 2)

            @pl.when(jnp.logical_and(far_take, t == 3))
            def _():
                far_pass(0)

            pairs(t - 2)
            save(t - 2).start()

        return carry

    def late(t, carry):
        @pl.when(has_next)
        def _():
            @pl.when(has_up)
            def _():
                relay_down(t - secs).wait_recv()

            @pl.when(has_down)
            def _():
                relay_up(t - secs).wait_recv()

        spectra(plain(t))
        pairs(t - 2)
        save(t - 2).start()
        return carry

    for p in range(1, GROUP):
        @pl.when(carries[p])
        def _():
            pl.semaphore_wait(ready, 1)
            to_carrier(p).wait_recv()
            onward(p).start()

        @pl.when(slants(p))
        def _():
            slant(p).start()

        @pl.when(carries[p])
        def _():
            start_halo(secs - 1)

    img_copy.wait()
    wait_halo(0)
    spectra(own(0))
    lax.fori_loop(1, secs, early, 0)

    @pl.when(far_take)
    def _():
        far_pass(1)

    lax.fori_loop(secs, secs + 2, late, 0)

    @pl.when(near_send)
    def _():
        for j in range(2):
            to_prev(j).wait_send()

    @pl.when(far_send)
    def _():
        to_far().wait_send()
        for p in range(1, GROUP):
            to_carrier(p).wait_send()

    for p in range(1, GROUP):
        @pl.when(carries[p])
        def _():
            onward(p).wait_send()

    @pl.when(has_down)
    def _():
        for t in range(secs):
            to_down(t).wait_send()

    @pl.when(has_up)
    def _():
        for t in range(secs):
            to_up(t).wait_send()

    for p in range(GROUP):
        @pl.when(slants(p))
        def _():
            slant(p).wait_send()

    left_down = jnp.logical_not(jnp.logical_and(far_take, edge_down))
    left_up = jnp.logical_not(jnp.logical_and(far_take, edge_up))

    @pl.when(jnp.logical_and(jnp.logical_and(has_next, has_down), left_down))
    def _():
        for j in range(2):
            relay_down(j).wait_send()

    @pl.when(jnp.logical_and(jnp.logical_and(has_next, has_up), left_up))
    def _():
        for j in range(2):
            relay_up(j).wait_send()

    for s in range(secs):
        save(s).wait()


def on_device(secs_axis, rows_axis, image, grid_shift, partner_step, tissue):
    secs, height, width = image.shape
    tables = [jnp.asarray(t) for t in (row_table(), col_tables(), back_col_tables(), back_row_table(), col_phases(), row_phases())]
    ints = [jnp.swapaxes(grid_shift, 2, 3), jnp.swapaxes(partner_step, 0, 1), tissue]
    dma = pltpu.SemaphoreType.DMA
    maps = pl.pallas_call(
        functools.partial(kernel, secs_axis, rows_axis),
        out_shape=jax.ShapeDtypeStruct((secs, 2, PC, SHIFTS, SHIFTS), jnp.float32),
        in_specs=[pl.BlockSpec(memory_space=pltpu.HBM)] * 10,
        out_specs=pl.BlockSpec(memory_space=pl.ANY),
        scratch_shapes=[pltpu.VMEM(t.shape, t.dtype) for t in tables]
        + [
            pltpu.VMEM((secs + 2, height, width), jnp.bfloat16),
            pltpu.VMEM((secs + 2, HALO, width), jnp.bfloat16),
            pltpu.VMEM((secs + 2, HALO, width), jnp.bfloat16),
            pltpu.VMEM((secs, 8, 4 * HALF), jnp.float32),
            pltpu.VMEM((secs, 8, 3 * HALF), jnp.float32),
            pltpu.VMEM((2, 2 * STACK, PATCH), jnp.bfloat16),
            pltpu.VMEM((2, 16, PATCH), jnp.float32),
            pltpu.VMEM((PC, PATCH, PATCH), jnp.bfloat16),
            pltpu.VMEM((secs, STACK, WIDE), jnp.bfloat16),
            pltpu.VMEM((secs, PC, 8, HALF), jnp.float32),
            pltpu.VMEM((secs + 1, STACK, WIDE), jnp.bfloat16),
            pltpu.VMEM((secs + 1, PC, 8, HALF), jnp.float32),
            pltpu.VMEM((secs, 2, PC, SHIFTS, SHIFTS), jnp.float32),
            dma((6,)),
            dma,
            dma((secs,)),
            dma((secs + 2,)),
            dma((secs + 2,)),
            dma((secs + 2,)),
            dma((secs + 2,)),
            dma((2,)),
            dma((2,)),
            dma((GROUP,)),
            dma((GROUP,)),
            pltpu.VMEM((HALF // 2, width), jnp.bfloat16),
            dma,
            dma,
            dma,
            pltpu.SemaphoreType.REGULAR,
        ]
        + [pltpu.SMEM(x.shape, x.dtype) for x in ints]
        + [
            dma((3,)),
        ],
        compiler_params=pltpu.CompilerParams(
            vmem_limit_bytes=40 * 1024 * 1024, collective_id=0, has_side_effects=True
        ),
        cost_estimate=pl.CostEstimate(flops=6_000_000_000, bytes_accessed=8_000_000, transcendentals=0),
    )(
        *[pltpu.with_memory_space_constraint(x, pltpu.HBM) for x in (*ints, image, *tables)]
    )
    return maps.reshape(secs, 2, 1, PC, SHIFTS * SHIFTS)


def solution(mesh):
    return jax.shard_map(
        functools.partial(on_device, mesh.shape["sec"], mesh.shape["row"]),
        mesh=mesh,
        in_specs=(
            P("sec", "row", None),
            P("sec", "row", None, None),
            P("sec", None),
            P("sec", "row", None),
        ),
        out_specs=P("sec", None, "row", None, None),
        check_vma=False,
    )
```
